256 devices in a mesh: panel: 2 (over x_hi), lat: 4 (over y), lon: 32 (over z, x_lo, core).
Axes of the slice: x: 4 (x_hi: 2, x_lo: 2; x = x_hi * 2 + x_lo), y: 4, z: 8, core: 2. Of those that a mesh axis runs over, the one named last changes fastest.
Arguments:
- fields: float32 [2, 8, 256, 49152], P('panel', None, 'lat', 'lon'), may hold values from -6 to 6
- coupling: float32 [4, 8, 8], replicated, may hold values from -4 to 4
- export_index: int32 [2, 4, 32, 512], P('panel', 'lat', 'lon'), may hold values from 0 to 767, as said below
- ghost_ns_index: int32 [2, 2, 2, 384, 4], P('panel', None, None, 'lon'), may hold values from 0 to 511
- ghost_ns_frac: float32 [2, 2, 2, 384, 2], P('panel', None, None, 'lon'), may hold values from 0.32 to 0.68
- ghost_ew_index: int32 [2, 2, 256, 2, 4], P('panel', None, 'lat'), may hold values from 0 to 511
- ghost_ew_frac: float32 [2, 2, 256, 2, 2], P('panel', None, 'lat'), may hold values from 0.32 to 0.68
Outputs:
- advanced: float32 [2, 8, 256, 49152], P('panel', None, 'lat', 'lon')
The draws below stay inside these ranges and needn't reach their ends.
Inputs may be any that keep to these rules, and one draw needn't show every extreme that they name: `export_index`: local column of the sending device's block. `ghost_ns_index`: received slot: source position times 4 plus the slot number. `ghost_ew_index`: received slot: source position times 4 plus the slot number.
All inputs are finite; a program needn't handle non-finite values.
Results may differ from the reference program's by a relative error of at most 0.0001.
Values sent between devices are 32-bit elements; how exact they have to be, the bound alone decides.
A program may use at most 64 MiB of HBM per device.

```python
import math
import jax
import jax.numpy as jnp
from jax import lax

FIELDS = 8
NR = 128
LAT_DEV = 64
LON_DEV = 12
SLOT = 4
NLAT = 256
NLON = 384
FLAT = 49152
SLOTS = 512
N_LAT = 4
N_LON = 32


def draw_export_index(key, part):
    shape = (2, N_LAT, N_LON, SLOTS)
    pick_key = jax.random.fold_in(key, 11)
    any_key = jax.random.fold_in(key, 12)
    which_key = jax.random.fold_in(key, 13)
    column_key = jax.random.fold_in(key, 14)
    pick = jax.random.randint(pick_key, shape, 0, 4)
    edge_row = jnp.where(pick < 2, pick, LAT_DEV - 4 + pick)
    any_row = jax.random.randint(any_key, shape, 0, LAT_DEV)
    use_edge = jax.random.randint(which_key, shape, 0, 4) < 3
    row_local = jnp.where(use_edge, edge_row, any_row)
    column = jax.random.randint(column_key, shape, 0, LON_DEV)
    return (row_local * LON_DEV + column).astype(jnp.int32)


def with_ends(drawn, rng, smallest, top_value):
    index_at = [jax.random.randint(jax.random.fold_in(rng, axis), (), 0, length) for axis, length in enumerate(drawn.shape)]
    longest = drawn.shape.index(max(drawn.shape))
    beside = index_at[:longest] + [(index_at[longest] + 1) % drawn.shape[longest]] + index_at[longest + 1:]
    return drawn.at[tuple(index_at)].set(smallest).at[tuple(beside)].set(top_value)


def steps_of(rng, shape, cuts, smallest, largest):
    def one(axis_at, blocks):
        heights = jax.random.uniform(jax.random.fold_in(jax.random.fold_in(rng, 6), axis_at), (blocks,), jnp.float32, smallest / len(cuts), largest / len(cuts))
        return jnp.repeat(jnp.exp(heights), shape[axis_at] // blocks).reshape((-1,) + (1,) * (len(shape) - axis_at - 1))

    gain = one(*cuts[0])
    for cut in cuts[1:]:
        gain = gain * one(*cut)
    return gain


def gaussian(stream_key, dims, deviation, bound, cuts=(), held_as=jnp.bfloat16):
    level = steps_of(stream_key, dims, cuts, -0.22, 0.18) if cuts else 1.0
    entries = jax.random.normal(stream_key, dims, jnp.float32) * deviation * level
    return jnp.minimum(jnp.maximum(entries, -bound), bound).astype(held_as)


def setup_inputs(seed: int = 0) -> dict:
    arg_keys = jax.random.split(jax.random.key(seed), 8)
    fields = gaussian(arg_keys[0], (2, FIELDS, NLAT, FLAT), 1.0, 6.0, ((0, 2), (2, 4), (3, 32)), jnp.float32)
    coupling = gaussian(arg_keys[1], (4, FIELDS, FIELDS), 1.0, 4.0, (), jnp.float32)
    export_index = draw_export_index(jax.random.fold_in(arg_keys[7], 71), 0)
    ghost_ns_index = with_ends(jax.random.randint(arg_keys[3], (2, 2, 2, NLON, 4), 0, SLOTS), jax.random.fold_in(arg_keys[3], 1), 0, SLOTS - 1).astype(jnp.int32)
    ghost_ns_frac = jnp.clip(0.32 + 0.36 * jax.random.uniform(arg_keys[4], (2, 2, 2, NLON, 2), jnp.float32) ** steps_of(arg_keys[4], (2, 2, 2, NLON, 2), ((0, 2), (3, 32)), -0.2, 0.2), 0.32, 0.68)
    ghost_ew_index = with_ends(jax.random.randint(arg_keys[5], (2, 2, NLAT, 2, 4), 0, SLOTS), jax.random.fold_in(arg_keys[5], 1), 0, SLOTS - 1).astype(jnp.int32)
    ghost_ew_frac = jnp.clip(0.32 + 0.36 * jax.random.uniform(arg_keys[6], (2, 2, NLAT, 2, 2), jnp.float32) ** steps_of(arg_keys[6], (2, 2, NLAT, 2, 2), ((0, 2), (2, 4)), -0.2, 0.2), 0.32, 0.68)
    return dict(fields=fields, coupling=coupling, export_index=export_index, ghost_ns_index=ghost_ns_index, ghost_ns_frac=ghost_ns_frac, ghost_ew_index=ghost_ew_index, ghost_ew_frac=ghost_ew_frac)


time_step = 0.15
viscosity = 0.1
inner_radius = 0.35
flux_signs = (-1.0, -1.0, -1.0, 1.0)


def differences(minus_two, minus_one, center, plus_one, plus_two):
    first_diff = (minus_two - plus_two + 8.0 * (plus_one - minus_one)) / 12.0
    second_diff = (16.0 * (plus_one + minus_one) - (plus_two + minus_two) - 30.0 * center) / 12.0
    return first_diff, second_diff


def radius_of(radial_index):
    return inner_radius + (1.0 - inner_radius) * (radial_index.astype(jnp.float32) + 0.5) / NR


def colatitude(lat_index, total_lat):
    return math.pi / 4 + (lat_index.astype(jnp.float32) + 0.5) * (math.pi / 2) / total_lat


def bilinear(values, fractions):
    along_frac = fractions[..., 0]
    across = fractions[..., 1]
    weights = jnp.stack([(1.0 - along_frac) * (1.0 - across), along_frac * (1.0 - across),
                         (1.0 - along_frac) * across, along_frac * across], axis=-1)
    return jnp.sum(values * weights[None, ..., None], axis=-2)


def donor_values(source, exports, destination, slot_index):
    source_pos = slot_index // SLOT
    within = slot_index % SLOT
    source_lat = source_pos // N_LON
    source_lon = source_pos % N_LON
    column = exports[source_lat, source_lon, destination * SLOT + within]
    row_index = source_lat * LAT_DEV + column // LON_DEV
    col_index = source_lon * LON_DEV + column % LON_DEV
    return source[:, row_index, col_index, :]


def border_cells(source, exports, ns_index, ns_frac, ew_index, ew_frac):
    lat_side = jnp.array([0, N_LAT - 1], jnp.int32)
    lon_cell = jnp.arange(LON_DEV * N_LON, dtype=jnp.int32)
    dest_ns = lat_side[:, None, None, None] * N_LON + (lon_cell // LON_DEV)[None, None, :, None]
    ns_values = bilinear(donor_values(source, exports, dest_ns, ns_index), ns_frac)
    lon_side = jnp.array([0, N_LON - 1], jnp.int32)
    lat_cell = jnp.arange(LAT_DEV * N_LAT, dtype=jnp.int32)
    dest_ew = (lat_cell // LAT_DEV)[None, :, None, None] * N_LON + lon_side[:, None, None, None]
    ew_values = bilinear(donor_values(source, exports, dest_ew, ew_index), ew_frac)
    return ns_values[:, 0], ns_values[:, 1], ew_values[:, 0], ew_values[:, 1]


def panel_rates(current, north_rows, south_rows, west_cols, east_cols, coupling):
    total_lat = current.shape[1]
    radius = radius_of(jnp.arange(NR, dtype=jnp.int32))
    colat = colatitude(jnp.arange(total_lat, dtype=jnp.int32), total_lat)
    along_lat = inner_radius / radius
    lon_scale = (inner_radius / (radius[None, :] * jnp.sin(colat)[:, None]))[:, None, :]
    lat_pad = jnp.concatenate([north_rows, current, south_rows], axis=1)
    lon_pad = jnp.concatenate([west_cols, current, east_cols], axis=2)
    rad_pad = jnp.pad(current, ((0, 0), (0, 0), (0, 0), (2, 2)))
    lat_first, lat_second = differences(lat_pad[:, :-4], lat_pad[:, 1:-3], current, lat_pad[:, 3:-1], lat_pad[:, 4:])
    lon_first, lon_second = differences(lon_pad[:, :, :-4], lon_pad[:, :, 1:-3], current, lon_pad[:, :, 3:-1], lon_pad[:, :, 4:])
    rad_first, rad_second = differences(rad_pad[..., :-4], rad_pad[..., 1:-3], current, rad_pad[..., 3:-1], rad_pad[..., 4:])
    signed = coupling * jnp.array(flux_signs, jnp.float32)[:, None, None]
    pieces = [rad_first, along_lat * lat_first, lon_scale * lon_first, current]
    coupled = jnp.zeros_like(current)
    for which_term in range(4):
        coupled = coupled + jnp.einsum("gf,fabc->gabc", signed[which_term], pieces[which_term],
                                       precision=lax.Precision.HIGHEST)
    spread = rad_second + along_lat * along_lat * lat_second + lon_scale * lon_scale * lon_second
    return coupled + viscosity * spread


def reference(fields, coupling, export_index, ghost_ns_index, ghost_ns_frac, ghost_ew_index, ghost_ew_frac):
    grid_shape = (2, FIELDS, LAT_DEV * N_LAT, LON_DEV * N_LON, NR)

    def rates(current):
        field_grid = current.reshape(grid_shape)
        results = []
        for which_panel in range(2):
            donor_panel = 1 - which_panel
            north_rows, south_rows, west_cols, east_cols = border_cells(
                field_grid[donor_panel], export_index[donor_panel], ghost_ns_index[which_panel],
                ghost_ns_frac[which_panel], ghost_ew_index[which_panel], ghost_ew_frac[which_panel])
            results.append(panel_rates(field_grid[which_panel], north_rows, south_rows, west_cols, east_cols, coupling))
        return jnp.stack(results).reshape(current.shape)

    first_rate = rates(fields)
    middle = fields + time_step * first_rate
    second_rate = rates(middle)
    return 0.5 * fields + 0.5 * (middle + time_step * second_rate)
```

```python
import functools
import math

import jax
import jax.numpy as jnp
from jax import lax
from jax.experimental import pallas as pl
from jax.experimental.pallas import tpu as pltpu
from jax.sharding import PartitionSpec as P

NR = 128
FIELDS = 8
LAT_DEV = 64
LON_DEV = 12
N_LAT = 4
N_LON = 32
N_Z = 8

time_step = 0.15
viscosity = 0.1
inner_radius = 0.35

MESH = pl.DeviceIdType.MESH
TILE = (FIELDS, NR)


def kernel(
    x_ref, coup_ref, nsi_ref, nsw_ref, exp_ref, ewi_ref, eww_ref, isin_ref,
    out_ref,
    q_init, q_mid, p_lat, p_lon, s_ref, res_ref, lhs_ref,
    send_g, recv_g0, recv_g1, send_e, recv_e1, recv_e20, recv_e21, chunk, recv_n, lat_h, lon_h,
    got_i, got_w, adj_i, adj_w, smem_i, smem_w,
    g_send, g_recv, e1_send, e1_recv, i_send, i_recv, n_send, n_recv,
    e2_send, e2_recv, lat_send, lat_recv, lon_send, lon_recv, loc_sem,
):
    recv_g = (recv_g0, recv_g1)
    recv_e2 = (recv_e20, recv_e21)
    p = lax.axis_index("panel")
    y = lax.axis_index("lat")
    b = lax.axis_index("lon")
    z = b // 4
    w = b % 4
    other = 1 - p
    wx = (w + 2) % 4
    me_k = y * 4 + w
    upper = y >= 2
    par = jnp.where(upper, 3 - y, y)
    dest_lat = jnp.where(upper, 3, 0)
    has_idx = (z % 2) == par
    is_ns = (y == 0) | (y == 3)
    is_agg = (w == 0) | (w == 3)
    ew_lon = jnp.where(w == 0, 0, N_LON - 1)
    is_ew = (b == 0) | (b == N_LON - 1)
    ew_side = jnp.where(b == 0, 0, 1)
    parity = z % 2
    star = jnp.where(y == 0, parity, 3 - parity)

    bar = pltpu.get_barrier_semaphore()

    def greet(dev):
        pl.semaphore_signal(bar, inc=1, device_id=dev, device_id_type=MESH)

    @pl.loop(0, 16)
    def _(k):
        @pl.when(k != me_k)
        def _():
            greet((p, k // 4, z * 4 + k % 4))

        @pl.when(is_agg)
        def _():
            greet((other, k // 4, z * 4 + k % 4))

    @pl.loop(0, 4)
    def _(m):
        greet((other, y, (2 * m + par) * 4 + wx))

    @pl.loop(0, N_Z)
    def _(zz):
        @pl.when(is_ns)
        def _():
            greet((other, star, zz * 4 + wx))

        @pl.when(is_ew & (zz != z))
        def _():
            greet((p, y, zz * 4 + w))

    @pl.when(y > 0)
    def _():
        greet((p, y - 1, b))

    @pl.when(y < N_LAT - 1)
    def _():
        greet((p, y + 1, b))

    @pl.when(b > 0)
    def _():
        greet((p, y, b - 1))

    @pl.when(b < N_LON - 1)
    def _():
        greet((p, y, b + 1))

    one = lambda cond: jnp.where(cond, 1, 0)
    peers = (
        15 + 8 + 4
        + 8 * one(has_idx)
        + one(is_agg & jnp.logical_not(is_ew))
        + one(y > 0) + one(y < N_LAT - 1) + one(b > 0) + one(b < N_LON - 1)
    )

    zero_rows = jnp.zeros((2, LON_DEV) + TILE, jnp.float32)
    for ref in (q_init, q_mid, p_lat):
        ref[0:2] = zero_rows
        ref[LAT_DEV + 2:LAT_DEV + 4] = zero_rows

    @pl.loop(0, LAT_DEV // 8)
    def _(ib):
        i0 = pl.multiple_of(ib * 8, 8)
        for j in range(LON_DEV):
            v = x_ref[:, pl.ds(i0, 8), j * NR:(j + 1) * NR]
            q_init[pl.ds(i0 + 2, 8), j] = jnp.swapaxes(v, 0, 1)

    pl.semaphore_wait(bar, peers)

    def rcopy(src, dst, ssem, rsem, dev):
        pltpu.make_async_remote_copy(
            src_ref=src, dst_ref=dst, send_sem=ssem, recv_sem=rsem,
            device_id=dev, device_id_type=MESH,
        ).start()

    def wait_on(ref, sem):
        pltpu.make_async_copy(ref, ref, sem).wait()

    @pl.when(has_idx)
    def _():
        side = jnp.where(upper, 1, 0)

        @pl.loop(0, N_Z)
        def _(zz):
            dev = (other, y, zz * 4 + wx)
            rcopy(nsi_ref.at[side], got_i.at[z // 2], i_send.at[0, zz], i_recv.at[0, z // 2], dev)
            rcopy(nsw_ref.at[side], got_w.at[z // 2], i_send.at[1, zz], i_recv.at[1, z // 2], dev)

    radius = inner_radius + (1.0 - inner_radius) * (
        lax.broadcasted_iota(jnp.int32, TILE, 1).astype(jnp.float32) + 0.5) / NR
    ct = inner_radius / radius
    ct2 = ct * ct * (viscosity / 12.0)

    def build_lhs():
        r64 = lax.broadcasted_iota(jnp.int32, (64, 8), 0) % 8
        c8 = lax.broadcasted_iota(jnp.int32, (64, 8), 1)
        ex = jnp.where(r64 == c8, 1.0, 0.0).astype(jnp.float32)
        r8 = lax.broadcasted_iota(jnp.int32, (8, 64), 0)
        c64 = lax.broadcasted_iota(jnp.int32, (8, 64), 1) % 8
        ext = jnp.where(r8 == c64, 1.0, 0.0).astype(jnp.float32)
        rr = lax.broadcasted_iota(jnp.int32, (64, 64), 0)
        cc = lax.broadcasted_iota(jnp.int32, (64, 64), 1)
        same = (rr // 8) == (cc // 8)
        eye = jnp.where(rr == cc, 1.0, 0.0).astype(jnp.float32)

        def kron(k):
            tall = jnp.dot(ex, coup_ref[k], precision=lax.Precision.HIGHEST,
                           preferred_element_type=jnp.float32)
            full = jnp.dot(tall, ext, precision=lax.Precision.HIGHEST,
                           preferred_element_type=jnp.float32)
            return jnp.where(same, full, 0.0)

        c0, c1, c2, c3 = kron(0), kron(1), kron(2), kron(3)
        nu = viscosity
        blocks = [
            (8.0 * c0 + 16.0 * nu * eye) / 12.0,
            (-8.0 * c0 + 16.0 * nu * eye) / 12.0,
            (-c0 - nu * eye) / 12.0,
            (c0 - nu * eye) / 12.0,
            c3 - (30.0 * nu / 12.0) * eye,
            c1 / -12.0,
            c2 / -12.0,
        ]
        for n, blk in enumerate(blocks):
            hi = blk.astype(jnp.bfloat16)
            lo = (blk - hi.astype(jnp.float32)).astype(jnp.bfloat16)
            lhs_ref[64 * n:64 * (n + 1), :] = jnp.concatenate([hi, hi, lo], axis=1)

    def split(cols):
        n = cols.shape[0] // 8
        flat = cols.reshape(n * 64, NR)
        wide = jnp.concatenate([flat[64 * t:64 * (t + 1)] for t in range(n)], axis=1)
        hi = wide.astype(jnp.bfloat16)
        lo = (wide - hi.astype(jnp.float32)).astype(jnp.bfloat16)
        return jnp.concatenate([hi, lo, hi], axis=0)

    def mixed(rows, cols):
        return jnp.dot(lhs_ref[rows], split(cols), preferred_element_type=jnp.float32)

    def unsplit(wide, n):
        return jnp.concatenate(
            [wide[:, NR * t:NR * (t + 1)] for t in range(n)], axis=0).reshape((8 * n,) + TILE)

    lane = lax.broadcasted_iota(jnp.int32, (64, NR), 1)

    def column(cur, idx):
        i = (idx * 43691) >> 19
        return cur[i + 2, idx - 12 * i]

    def donors(st, cur):
        @pl.loop(0, 16)
        def _(n):
            k = lax.rem(me_k + 1 + n, 16)
            ky = k // 4
            kw = k % 4
            kup = ky >= 2
            kpar = jnp.where(kup, 3 - ky, ky)
            first = (jnp.where(kup, 96, 0) + kpar * 4 + (kw + 2) % 4) * 4
            for m in range(4):
                for s in range(4):
                    send_g[st, k, m * 4 + s] = column(cur, exp_ref[first + m * 32 + s])

            @pl.when(k != me_k)
            def _():
                rcopy(send_g.at[st, k], recv_g[st].at[me_k], g_send.at[st, k],
                      g_recv.at[st, me_k], (p, ky, z * 4 + kw))

            @pl.when(k == me_k)
            def _():
                pltpu.make_async_copy(
                    send_g.at[st, k], recv_g[st].at[me_k], g_recv.at[st, me_k]).start()

        @pl.loop(0, 8)
        def _(t):
            ta = t // 2
            side = t % 2
            first = (ta * N_LON + side * (N_LON - 1)) * 4
            for s in range(4):
                send_e[st, t, s] = column(cur, exp_ref[first + s])
            rcopy(send_e.at[st, t], recv_e1.at[st, me_k], e1_send.at[st, t],
                  e1_recv.at[st, me_k], (other, ta, z * 4 + side * 3))

    def halos(st, cur):
        @pl.when(b < N_LON - 1)
        def _():
            rcopy(cur.at[2:LAT_DEV + 2, 10:12], lon_h.at[st, 0], lon_send.at[st, 0],
                  lon_recv.at[st, 0], (p, y, b + 1))

        @pl.when(b > 0)
        def _():
            rcopy(cur.at[2:LAT_DEV + 2, 0:2], lon_h.at[st, 1], lon_send.at[st, 1],
                  lon_recv.at[st, 1], (p, y, b - 1))

        @pl.when(y < N_LAT - 1)
        def _():
            rcopy(cur.at[LAT_DEV:LAT_DEV + 2], lat_h.at[st, 0], lat_send.at[st, 0],
                  lat_recv.at[st, 0], (p, y + 1, b))

        @pl.when(y > 0)
        def _():
            rcopy(cur.at[2:4], lat_h.at[st, 1], lat_send.at[st, 1],
                  lat_recv.at[st, 1], (p, y - 1, b))

    def products(cur):
        @pl.loop(0, LAT_DEV // 4)
        def _(c):
            i0 = c * 4
            cols = cur[pl.ds(i0 + 2, 4)].reshape((48,) + TILE)
            sums, lats, lons = [], [], []
            for t in range(3):
                wide = mixed(slice(0, 448), cols[16 * t:16 * (t + 1)])
                for h in range(2):
                    part = wide[:, NR * h:NR * (h + 1)]
                    total = part[256:320]
                    total = total + jnp.where(lane >= 1, pltpu.roll(part[0:64], 1, 1), 0.0)
                    total = total + jnp.where(lane < NR - 1, pltpu.roll(part[64:128], NR - 1, 1), 0.0)
                    total = total + jnp.where(lane >= 2, pltpu.roll(part[128:192], 2, 1), 0.0)
                    total = total + jnp.where(lane < NR - 2, pltpu.roll(part[192:256], NR - 2, 1), 0.0)
                    sums.append(total)
                    lats.append(part[320:384])
                    lons.append(part[384:448])
            shape = (4, LON_DEV) + TILE
            s_ref[pl.ds(i0, 4)] = jnp.concatenate(sums, axis=0).reshape(shape)
            p_lat[pl.ds(i0 + 2, 4)] = jnp.concatenate(lats, axis=0).reshape(shape)
            p_lon[pl.ds(i0, 4)] = jnp.concatenate(lons, axis=0).reshape(shape)

    def shifted(v, n):
        pad = jnp.zeros((abs(n),) + TILE, jnp.float32)
        if n > 0:
            return jnp.concatenate([v[n:], pad], axis=0)
        return jnp.concatenate([pad, v[:n]], axis=0)

    def stencil(st, cur):
        @pl.loop(0, LAT_DEV)
        def _(i):
            si = isin_ref[y * LAT_DEV + i]
            q0 = cur[i + 2]
            pl0 = p_lon[i]
            d1 = (p_lat[i] - p_lat[i + 4]) + 8.0 * (p_lat[i + 3] - p_lat[i + 1])
            e1 = (shifted(pl0, -2) - shifted(pl0, 2)) + 8.0 * (shifted(pl0, 1) - shifted(pl0, -1))
            d2 = 16.0 * (cur[i + 1] + cur[i + 3]) - (cur[i] + cur[i + 4])
            e2 = 16.0 * (shifted(q0, -1) + shifted(q0, 1)) - (shifted(q0, -2) + shifted(q0, 2))
            rate = s_ref[i] + ct * (d1 + si * e1) + ct2 * (
                d2 + (si * si) * e2 - (30.0 * (1.0 + si * si)) * q0)
            if st == 0:
                q_mid[i + 2] = q0 + time_step * rate
            else:
                res_ref[i] = 0.5 * q_init[i + 2] + 0.5 * (q0 + time_step * rate)

    def aggregate(st):
        @pl.loop(0, 16)
        def _(k):
            wait_on(recv_g[st].at[k], g_recv.at[st, k])

        @pl.loop(0, 4)
        def _(m):
            @pl.loop(0, 24)
            def _(cell):
                acc = jnp.zeros(TILE, jnp.float32)
                for t in range(4):
                    e = cell * 4 + t
                    idx = smem_i[m, 0, e]
                    acc = acc + smem_w[m, 0, e] * recv_g[st][idx >> 4, idx & 15]
                chunk[st, m, cell] = acc

            rcopy(chunk.at[st, m], recv_n.at[st, z], n_send.at[st, m], n_recv.at[st, z],
                  (other, dest_lat, (2 * m + par) * 4 + wx))

    def forward_ew(st):
        @pl.when(is_agg)
        def _():
            @pl.loop(0, 16)
            def _(k):
                wait_on(recv_e1.at[st, k], e1_recv.at[st, k])

            @pl.when(jnp.logical_not(is_ew))
            def _():
                rcopy(recv_e1.at[st], recv_e2[st].at[z], e2_send.at[st], e2_recv.at[st, z],
                      (p, y, ew_lon))

            @pl.when(is_ew)
            def _():
                pltpu.make_async_copy(recv_e1.at[st], recv_e2[st].at[z], e2_recv.at[st, z]).start()

    def adjust_indices():
        for m in range(4):
            wait_on(got_i.at[m], i_recv.at[0, m])
            wait_on(got_w.at[m], i_recv.at[1, m])
            s = got_i[m]
            col = (s >> 2) & (N_LON - 1)
            k = (s >> 7) * 4 + (col & 3)
            adj_i[m] = k * 16 + m * 4 + (s & 3)
            adj_w[m] = jnp.where((col >> 2) == z, got_w[m], 0.0)
        ci = pltpu.make_async_copy(adj_i, smem_i, loc_sem.at[0])
        cw = pltpu.make_async_copy(adj_w, smem_w, loc_sem.at[1])
        ci.start()
        cw.start()
        ci.wait()
        cw.wait()

    def border_ns(st):
        @pl.when(is_ns)
        def _():
            @pl.loop(0, N_Z)
            def _(zz):
                wait_on(recv_n.at[st, zz], n_recv.at[st, zz])

            side = jnp.where(upper, 1, 0)

            @pl.loop(0, 2)
            def _(g):
                acc = recv_n[st, 0, pl.ds(g * 12, 12)]
                for zz in range(1, N_Z):
                    acc = acc + recv_n[st, zz, pl.ds(g * 12, 12)]
                lat_h[st, side, g] = acc

    def border_ew(st):
        @pl.when(is_ew)
        def _():
            @pl.loop(0, N_Z)
            def _(zz):
                wait_on(recv_e2[st].at[zz], e2_recv.at[st, zz])

            @pl.loop(0, LAT_DEV)
            def _(i):
                for g in range(2):
                    acc = jnp.zeros(TILE, jnp.float32)
                    for t in range(4):
                        e = ew_side * 512 + i * 8 + g * 4 + t
                        s = ewi_ref[e]
                        col = (s >> 2) & (N_LON - 1)
                        k = (s >> 7) * 4 + (col & 3)
                        acc = acc + eww_ref[e] * recv_e2[st][col >> 2, k, s & 3]
                    lon_h[st, ew_side, i, g] = acc

    def wait_halos(st):
        @pl.when(b > 0)
        def _():
            wait_on(lon_h.at[st, 0], lon_recv.at[st, 0])

        @pl.when(b < N_LON - 1)
        def _():
            wait_on(lon_h.at[st, 1], lon_recv.at[st, 1])

        @pl.when(y > 0)
        def _():
            wait_on(lat_h.at[st, 0], lat_recv.at[st, 0])

        @pl.when(y < N_LAT - 1)
        def _():
            wait_on(lat_h.at[st, 1], lat_recv.at[st, 1])

    def correct(st):
        if st == 0:
            dst, off, scale = q_mid, 2, time_step
        else:
            dst, off, scale = res_ref, 0, 0.5 * time_step
        hal = lat_h[st].reshape((48,) + TILE)
        mix_lat = jnp.concatenate(
            [unsplit(mixed(slice(320, 384), hal[16 * t:16 * (t + 1)]), 2) for t in range(3)],
            axis=0).reshape((2, 2, LON_DEV) + TILE)
        hal = hal.reshape((2, 2, LON_DEV) + TILE)
        sc, sc2 = scale * ct, scale * ct2
        dst[off] += sc * (mix_lat[0, 0] - 8.0 * mix_lat[0, 1]) + sc2 * (16.0 * hal[0, 1] - hal[0, 0])
        dst[off + 1] += sc * mix_lat[0, 1] - sc2 * hal[0, 1]
        dst[off + 63] += sc * (8.0 * mix_lat[1, 0] - mix_lat[1, 1]) + sc2 * (16.0 * hal[1, 0] - hal[1, 1])
        dst[off + 62] += -sc * mix_lat[1, 0] - sc2 * hal[1, 0]

        @pl.loop(0, LAT_DEV // 4)
        def _(c):
            i0 = c * 4
            west = lon_h[st, 0, pl.ds(i0, 4)].reshape((8,) + TILE)
            east = lon_h[st, 1, pl.ds(i0, 4)].reshape((8,) + TILE)
            both = unsplit(mixed(slice(384, 448), jnp.concatenate([west, east], axis=0)), 2)
            for n in range(4):
                i = i0 + n
                si = isin_ref[y * LAT_DEV + i]
                a1 = sc * si
                a2 = sc2 * (si * si)
                w2, w1, pw2, pw1 = west[2 * n], west[2 * n + 1], both[2 * n], both[2 * n + 1]
                e1, e2, pe1, pe2 = east[2 * n], east[2 * n + 1], both[8 + 2 * n], both[9 + 2 * n]
                dst[off + i, 0] += a1 * (pw2 - 8.0 * pw1) + a2 * (16.0 * w1 - w2)
                dst[off + i, 1] += a1 * pw1 - a2 * w1
                dst[off + i, 11] += a1 * (8.0 * pe1 - pe2) + a2 * (16.0 * e1 - e2)
                dst[off + i, 10] += -a1 * pe1 - a2 * e1

    for st, cur in ((0, q_init), (1, q_mid)):
        donors(st, cur)
        halos(st, cur)
        if st == 0:
            build_lhs()
            adjust_indices()
        products(cur)
        forward_ew(st)
        aggregate(st)
        stencil(st, cur)
        wait_halos(st)
        border_ns(st)
        border_ew(st)
        correct(st)

    @pl.loop(0, LAT_DEV // 8)
    def _(ib):
        i0 = pl.multiple_of(ib * 8, 8)
        for j in range(LON_DEV):
            v = res_ref[pl.ds(i0, 8), j]
            out_ref[:, pl.ds(i0, 8), j * NR:(j + 1) * NR] = jnp.swapaxes(v, 0, 1)

    @pl.when(has_idx)
    def _():
        @pl.loop(0, N_Z)
        def _(zz):
            wait_on(nsi_ref.at[0], i_send.at[0, zz])
            wait_on(nsw_ref.at[0], i_send.at[1, zz])

    for st, cur in ((0, q_init), (1, q_mid)):
        @pl.loop(0, 16)
        def _(k):
            @pl.when(k != me_k)
            def _():
                wait_on(send_g.at[st, k], g_send.at[st, k])

        @pl.loop(0, 8)
        def _(t):
            wait_on(send_e.at[st, t], e1_send.at[st, t])

        @pl.loop(0, 4)
        def _(m):
            wait_on(chunk.at[st, m], n_send.at[st, m])

        @pl.when(is_agg & jnp.logical_not(is_ew))
        def _():
            wait_on(recv_e1.at[st], e2_send.at[st])

        @pl.when(b < N_LON - 1)
        def _():
            wait_on(lon_h.at[st, 0], lon_send.at[st, 0])

        @pl.when(b > 0)
        def _():
            wait_on(lon_h.at[st, 1], lon_send.at[st, 1])

        @pl.when(y < N_LAT - 1)
        def _():
            wait_on(lat_h.at[st, 0], lat_send.at[st, 0])

        @pl.when(y > 0)
        def _():
            wait_on(lat_h.at[st, 1], lat_send.at[st, 1])


def corner_weights(frac):
    a, c = frac[..., 0], frac[..., 1]
    return jnp.stack(
        [(1.0 - a) * (1.0 - c), a * (1.0 - c), (1.0 - a) * c, a * c], axis=-1)


def inverse_sines():
    total = LAT_DEV * N_LAT
    colat = math.pi / 4 + (jnp.arange(total, dtype=jnp.int32).astype(jnp.float32) + 0.5) * (
        math.pi / 2) / total
    return 1.0 / jnp.sin(colat)


def local(
    fields, coupling, export_index, ghost_ns_index, ghost_ns_frac, ghost_ew_index, ghost_ew_frac
):
    x = fields[0]

    def padded(v):
        flat = jnp.pad(v.reshape(2, 1, 96), ((0, 0), (0, 7), (0, 32)))
        return flat

    nsi = padded(ghost_ns_index[0])
    nsw = padded(corner_weights(ghost_ns_frac[0]))
    exports = export_index.reshape(-1)
    ewi = ghost_ew_index.reshape(-1)
    eww = corner_weights(ghost_ew_frac[0]).reshape(-1)
    isin = inverse_sines()

    vm = pl.BlockSpec(memory_space=pltpu.VMEM)
    sm = pl.BlockSpec(memory_space=pltpu.SMEM)
    V = lambda *shape: pltpu.VMEM(shape + TILE, jnp.float32)
    D = lambda *shape: pltpu.SemaphoreType.DMA(shape)
    out = pl.pallas_call(
        kernel,
        out_shape=jax.ShapeDtypeStruct(x.shape, jnp.float32),
        in_specs=[vm, vm, vm, vm, sm, sm, sm, sm],
        out_specs=vm,
        scratch_shapes=[
            V(LAT_DEV + 4, LON_DEV), V(LAT_DEV + 4, LON_DEV), V(LAT_DEV + 4, LON_DEV),
            V(LAT_DEV, LON_DEV), V(LAT_DEV, LON_DEV), V(LAT_DEV, LON_DEV),
            pltpu.VMEM((448, 192), jnp.bfloat16),
            V(2, 16, 16), V(16, 16), V(16, 16), V(2, 8, 4), V(2, 16, 4), V(N_Z, 16, 4), V(N_Z, 16, 4),
            V(2, 4, 24), V(2, N_Z, 24), V(2, 2, 2, LON_DEV), V(2, 2, LAT_DEV, 2),
            pltpu.VMEM((4,) + TILE, jnp.int32), V(4),
            pltpu.VMEM((4,) + TILE, jnp.int32), V(4),
            pltpu.SMEM((4,) + TILE, jnp.int32), pltpu.SMEM((4,) + TILE, jnp.float32),
            D(2, 16), D(2, 16), D(2, 8), D(2, 16), D(2, 8), D(2, 4), D(2, 4), D(2, N_Z),
            D(2), D(2, N_Z), D(2, 2), D(2, 2), D(2, 2), D(2, 2), D(2),
        ],
        compiler_params=pltpu.CompilerParams(
            collective_id=0, has_side_effects=True, vmem_limit_bytes=60 * 2**20),
        name="two_sections",
    )(x, coupling, nsi, nsw, exports, ewi, eww, isin)
    return out[None]


def solution(mesh):
    placed = (
        P("panel", None, "lat", "lon"),
        P(),
        P("panel", "lat", "lon", None),
        P("panel", None, None, "lon", None),
        P("panel", None, None, "lon", None),
        P("panel", None, "lat", None, None),
        P("panel", None, "lat", None, None),
    )
    return jax.shard_map(
        local, mesh=mesh, in_specs=placed, out_specs=P("panel", None, "lat", "lon"), check_vma=False
    )
```

```python
import math

import jax
import jax.numpy as jnp
from jax import lax
from jax.experimental import pallas as pl
from jax.experimental.pallas import tpu as pltpu
from jax.sharding import PartitionSpec as P

NR = 128
FIELDS = 8
LAT_DEV = 64
LON_DEV = 12
N_LAT = 4
N_LON = 32
N_Z = 8

time_step = 0.15
viscosity = 0.1
inner_radius = 0.35

MESH = pl.DeviceIdType.MESH
TILE = (FIELDS, NR)


def kernel(
    x_ref, coup_ref, nsi_ref, nsf_ref, exp_ref, ewi_ref, ewf_ref,
    out_ref,
    x_buf, q_init, q_mid, p_lat, p_lon, s_ref, res_ref, lhs_ref, isin_ref,
    send_g, recv_g0, recv_g1, send_e, recv_e1, recv_e20, recv_e21, chunk, recv_n, summed,
    lat_h, lon_h,
    own_i, own_w, got_i, got_w, adj_i, adj_w, smem_i, smem_w,
    adj_ei, adj_ew, smem_ei, smem_ew,
    g_send, g_recv, e1_send, e1_recv, i_send, i_recv, n_send, n_recv, f_send,
    e2_send, e2_recv, lat_send, lat_recv, lon_send, lon_recv, loc_sem,
):
    recv_g = (recv_g0, recv_g1)
    recv_e2 = (recv_e20, recv_e21)
    p = lax.axis_index("panel")
    y = lax.axis_index("lat")
    b = lax.axis_index("lon")
    z = b // 4
    w = b % 4
    other = 1 - p
    wx = (w + 2) % 4
    me_k = y * 4 + w
    upper = y >= 2
    half = jnp.where(upper, 1, 0)
    par = jnp.where(upper, 3 - y, y)
    dest_lat = jnp.where(upper, 3, 0)
    is_sum = (z % 2) == par
    is_ns = (y == 0) | (y == 3)
    is_agg = (w == 1) | (w == 2)
    ew_lon = jnp.where(w == 2, 0, N_LON - 1)
    is_ew = (b == 0) | (b == N_LON - 1)
    ew_side = jnp.where(b == 0, 0, 1)
    star = jnp.where(y == 0, z % 2, 3 - z % 2)

    x_copy = pltpu.make_async_copy(x_ref, x_buf, loc_sem.at[0])
    x_copy.start()

    bar = pltpu.get_barrier_semaphore()

    def greet(dev):
        pl.semaphore_signal(bar, inc=1, device_id=dev, device_id_type=MESH)

    @pl.loop(0, 16)
    def _(k):
        @pl.when(k != me_k)
        def _():
            greet((p, k // 4, z * 4 + k % 4))

    @pl.loop(0, 4)
    def _(m):
        greet((other, y, (2 * m + par) * 4 + wx))

    @pl.loop(0, N_Z)
    def _(zz):
        @pl.when(is_sum & (zz != z))
        def _():
            greet((p, y, zz * 4 + w))

        @pl.when(is_ew)
        def _():
            greet((other, y, zz * 4 + wx))

    @pl.when(is_ns)
    def _():
        greet((other, star, z * 4 + wx))

    @pl.when(y > 0)
    def _():
        greet((p, y - 1, b))

    @pl.when(y < N_LAT - 1)
    def _():
        greet((p, y + 1, b))

    @pl.when(b > 0)
    def _():
        greet((p, y, b - 1))

    @pl.when(b < N_LON - 1)
    def _():
        greet((p, y, b + 1))

    one = lambda cond: jnp.where(cond, 1, 0)
    peers = (
        15 + 4 + 8 * one(is_sum) + one(is_agg)
        + one(y > 0) + one(y < N_LAT - 1) + one(b > 0) + one(b < N_LON - 1)
    )

    def rcopy(src, dst, ssem, rsem, dev):
        pltpu.make_async_remote_copy(
            src_ref=src, dst_ref=dst, send_sem=ssem, recv_sem=rsem,
            device_id=dev, device_id_type=MESH,
        ).start()

    def wait_on(ref, sem):
        pltpu.make_async_copy(ref, ref, sem).wait()

    row = lax.broadcasted_iota(jnp.int32, TILE, 0)

    def weights_of(frac):
        a, c = frac[0:1], frac[1:2]
        return jnp.where(row % 2 == 1, a, 1.0 - a) * jnp.where(row % 4 >= 2, c, 1.0 - c)

    def prepare_indices():
        own_i[...] = jnp.zeros(own_i.shape, jnp.int32)
        own_w[...] = jnp.zeros(own_w.shape, jnp.float32)
        adj_ei[...] = jnp.zeros(adj_ei.shape, jnp.int32)
        adj_ew[...] = jnp.zeros(adj_ew.shape, jnp.float32)
        for g in range(2):
            own_i[g, 0:4, 0:LON_DEV] = nsi_ref[half, g]
            own_w[g, 0:2, 0:LON_DEV] = nsf_ref[half, g]
            own_w[g] = weights_of(own_w[g])
            adj_ei[g, 0:4, 0:LAT_DEV] = ewi_ref[ew_side, g]
            adj_ew[g, 0:2, 0:LAT_DEV] = ewf_ref[ew_side, g]
            adj_ew[g] = weights_of(adj_ew[g])
            s = adj_ei[g]
            col = (s >> 2) & (N_LON - 1)
            k = (s >> 7) * 4 + (col & 3)
            adj_ei[g] = (col >> 2) * 64 + k * 4 + (s & 3)
        copies = [pltpu.make_async_copy(adj_ei, smem_ei, loc_sem.at[1]),
                  pltpu.make_async_copy(adj_ew, smem_ew, loc_sem.at[2])]
        for c in copies:
            c.start()
        for c in copies:
            c.wait()

    def send_indices():
        @pl.when(is_sum)
        def _():
            @pl.loop(0, N_Z)
            def _(zz):
                dev = (other, y, zz * 4 + wx)
                rcopy(own_i, got_i.at[z // 2], i_send.at[0, zz], i_recv.at[0, z // 2], dev)
                rcopy(own_w, got_w.at[z // 2], i_send.at[1, zz], i_recv.at[1, z // 2], dev)

    def adjust_indices():
        for m in range(4):
            wait_on(got_i.at[m], i_recv.at[0, m])
            wait_on(got_w.at[m], i_recv.at[1, m])
            s = got_i[m]
            col = (s >> 2) & (N_LON - 1)
            k = (s >> 7) * 4 + (col & 3)
            adj_i[m] = k * 16 + m * 4 + (s & 3)
            adj_w[m] = jnp.where((col >> 2) == z, got_w[m], 0.0)
        copies = [pltpu.make_async_copy(adj_i, smem_i, loc_sem.at[3]),
                  pltpu.make_async_copy(adj_w, smem_w, loc_sem.at[4])]
        for c in copies:
            c.start()
        for c in copies:
            c.wait()

    def load_state():
        zero_rows = jnp.zeros((2, LON_DEV) + TILE, jnp.float32)
        for ref in (q_init, q_mid, p_lat):
            ref[0:2] = zero_rows
            ref[LAT_DEV + 2:LAT_DEV + 4] = zero_rows
        x_copy.wait()

        @pl.loop(0, LAT_DEV // 8)
        def _(ib):
            i0 = pl.multiple_of(ib * 8, 8)
            for j in range(LON_DEV):
                v = x_buf[:, pl.ds(i0, 8), j * NR:(j + 1) * NR]
                q_init[pl.ds(i0 + 2, 8), j] = jnp.swapaxes(v, 0, 1)

    radius = inner_radius + (1.0 - inner_radius) * (
        lax.broadcasted_iota(jnp.int32, TILE, 1).astype(jnp.float32) + 0.5) / NR
    ct = inner_radius / radius
    ct2 = ct * ct * (viscosity / 12.0)

    def build_sines():
        i = y * LAT_DEV + lax.broadcasted_iota(jnp.int32, (LAT_DEV, NR), 0)
        colat = math.pi / 4 + (i.astype(jnp.float32) + 0.5) * (math.pi / 2) / (LAT_DEV * N_LAT)
        isin_ref[...] = 1.0 / jnp.sin(colat)

    def inv_sin(i):
        return isin_ref[pl.ds(i, 1), :]

    def build_lhs():
        r64 = lax.broadcasted_iota(jnp.int32, (64, 8), 0) % 8
        c8 = lax.broadcasted_iota(jnp.int32, (64, 8), 1)
        ex = jnp.where(r64 == c8, 1.0, 0.0).astype(jnp.float32)
        r8 = lax.broadcasted_iota(jnp.int32, (8, 64), 0)
        c64 = lax.broadcasted_iota(jnp.int32, (8, 64), 1) % 8
        ext = jnp.where(r8 == c64, 1.0, 0.0).astype(jnp.float32)
        rr = lax.broadcasted_iota(jnp.int32, (64, 64), 0)
        cc = lax.broadcasted_iota(jnp.int32, (64, 64), 1)
        same = (rr // 8) == (cc // 8)
        eye = jnp.where(rr == cc, 1.0, 0.0).astype(jnp.float32)

        def kron(k):
            tall = jnp.dot(ex, coup_ref[k], precision=lax.Precision.HIGHEST,
                           preferred_element_type=jnp.float32)
            full = jnp.dot(tall, ext, precision=lax.Precision.HIGHEST,
                           preferred_element_type=jnp.float32)
            return jnp.where(same, full, 0.0)

        c0, c1, c2, c3 = kron(0), kron(1), kron(2), kron(3)
        nu = viscosity
        blocks = [
            (8.0 * c0 + 16.0 * nu * eye) / 12.0,
            (-8.0 * c0 + 16.0 * nu * eye) / 12.0,
            (-c0 - nu * eye) / 12.0,
            (c0 - nu * eye) / 12.0,
            c3 - (30.0 * nu / 12.0) * eye,
            c1 / -12.0,
            c2 / -12.0,
        ]
        for n, blk in enumerate(blocks):
            hi = blk.astype(jnp.bfloat16)
            lo = (blk - hi.astype(jnp.float32)).astype(jnp.bfloat16)
            lhs_ref[64 * n:64 * (n + 1), :] = jnp.concatenate([hi, hi, lo], axis=1)

    def split(cols):
        n = cols.shape[0] // 8
        flat = cols.reshape(n * 64, NR)
        wide = jnp.concatenate([flat[64 * t:64 * (t + 1)] for t in range(n)], axis=1)
        hi = wide.astype(jnp.bfloat16)
        lo = (wide - hi.astype(jnp.float32)).astype(jnp.bfloat16)
        return jnp.concatenate([hi, lo, hi], axis=0)

    def mixed(rows, cols):
        return jnp.dot(lhs_ref[rows], split(cols), preferred_element_type=jnp.float32)

    def unsplit(wide, n):
        return jnp.concatenate(
            [wide[:, NR * t:NR * (t + 1)] for t in range(n)], axis=0).reshape((8 * n,) + TILE)

    lane = lax.broadcasted_iota(jnp.int32, (64, NR), 1)

    def column(cur, idx):
        i = (idx * 43691) >> 19
        return cur[i + 2, idx - 12 * i]

    def group_of(k):
        ky = k // 4
        kup = ky >= 2
        kpar = jnp.where(kup, 3 - ky, ky)
        return (jnp.where(kup, 96, 0) + kpar * 4 + (k % 4 + 2) % 4) * 4

    def gather_g(st, cur, k):
        first = group_of(k)
        for m in range(4):
            for s in range(4):
                send_g[st, k, m * 4 + s] = column(cur, exp_ref[first + m * 32 + s])

    def start_g(st, k):
        @pl.when(k != me_k)
        def _():
            rcopy(send_g.at[st, k], recv_g[st].at[me_k], g_send.at[st, k],
                  g_recv.at[st, me_k], (p, k // 4, z * 4 + k % 4))

        @pl.when(k == me_k)
        def _():
            pltpu.make_async_copy(
                send_g.at[st, k], recv_g[st].at[me_k], g_recv.at[st, me_k]).start()

    def gather_e(st, cur, t):
        first = ((t // 2) * N_LON + (t % 2) * (N_LON - 1)) * 4
        for s in range(4):
            send_e[st, t, s] = column(cur, exp_ref[first + s])

    def ew_member(t):
        return (t // 2) * 4 + 2 - t % 2

    def start_e(st, t):
        k = ew_member(t)

        @pl.when(k != me_k)
        def _():
            rcopy(send_e.at[st, t], recv_e1.at[st, me_k], e1_send.at[st, t],
                  e1_recv.at[st, me_k], (p, k // 4, z * 4 + k % 4))

        @pl.when(k == me_k)
        def _():
            pltpu.make_async_copy(
                send_e.at[st, t], recv_e1.at[st, me_k], e1_recv.at[st, me_k]).start()

    def turn(n):
        return lax.rem(me_k + 1 + n, 16)

    def halos(st, cur):
        @pl.when(y < N_LAT - 1)
        def _():
            rcopy(cur.at[LAT_DEV:LAT_DEV + 2], lat_h.at[st, 0], lat_send.at[st, 0],
                  lat_recv.at[st, 0], (p, y + 1, b))

        @pl.when(y > 0)
        def _():
            rcopy(cur.at[2:4], lat_h.at[st, 1], lat_send.at[st, 1],
                  lat_recv.at[st, 1], (p, y - 1, b))

        @pl.when(b < N_LON - 1)
        def _():
            rcopy(cur.at[2:LAT_DEV + 2, 10:12], lon_h.at[st, 0], lon_send.at[st, 0],
                  lon_recv.at[st, 0], (p, y, b + 1))

        @pl.when(b > 0)
        def _():
            rcopy(cur.at[2:LAT_DEV + 2, 0:2], lon_h.at[st, 1], lon_send.at[st, 1],
                  lon_recv.at[st, 1], (p, y, b - 1))

    def products(cur):
        @pl.loop(0, LAT_DEV // 4)
        def _(c):
            i0 = c * 4
            cols = cur[pl.ds(i0 + 2, 4)].reshape((48,) + TILE)
            sums, lats, lons = [], [], []
            for t in range(3):
                wide = mixed(slice(0, 448), cols[16 * t:16 * (t + 1)])
                for h in range(2):
                    part = wide[:, NR * h:NR * (h + 1)]
                    total = part[256:320]
                    total = total + jnp.where(lane >= 1, pltpu.roll(part[0:64], 1, 1), 0.0)
                    total = total + jnp.where(lane < NR - 1, pltpu.roll(part[64:128], NR - 1, 1), 0.0)
                    total = total + jnp.where(lane >= 2, pltpu.roll(part[128:192], 2, 1), 0.0)
                    total = total + jnp.where(lane < NR - 2, pltpu.roll(part[192:256], NR - 2, 1), 0.0)
                    sums.append(total)
                    lats.append(part[320:384])
                    lons.append(part[384:448])
            shape = (4, LON_DEV) + TILE
            s_ref[pl.ds(i0, 4)] = jnp.concatenate(sums, axis=0).reshape(shape)
            p_lat[pl.ds(i0 + 2, 4)] = jnp.concatenate(lats, axis=0).reshape(shape)
            p_lon[pl.ds(i0, 4)] = jnp.concatenate(lons, axis=0).reshape(shape)

    def shifted(v, n):
        pad = jnp.zeros((abs(n),) + TILE, jnp.float32)
        if n > 0:
            return jnp.concatenate([v[n:], pad], axis=0)
        return jnp.concatenate([pad, v[:n]], axis=0)

    def stencil(st, cur):
        @pl.loop(0, LAT_DEV)
        def _(i):
            si = inv_sin(i)
            q0 = cur[i + 2]
            pl0 = p_lon[i]
            d1 = (p_lat[i] - p_lat[i + 4]) + 8.0 * (p_lat[i + 3] - p_lat[i + 1])
            e1 = (shifted(pl0, -2) - shifted(pl0, 2)) + 8.0 * (shifted(pl0, 1) - shifted(pl0, -1))
            d2 = 16.0 * (cur[i + 1] + cur[i + 3]) - (cur[i] + cur[i + 4])
            e2 = 16.0 * (shifted(q0, -1) + shifted(q0, 1)) - (shifted(q0, -2) + shifted(q0, 2))
            rate = s_ref[i] + ct * (d1 + si * e1) + ct2 * (
                d2 + (si * si) * e2 - (30.0 * (1.0 + si * si)) * q0)
            if st == 0:
                q_mid[i + 2] = q0 + time_step * rate
            else:
                res_ref[i] = 0.5 * q_init[i + 2] + 0.5 * (q0 + time_step * rate)

    def aggregate(st):
        @pl.loop(0, 16)
        def _(k):
            wait_on(recv_g[st].at[k], g_recv.at[st, k])

        @pl.loop(0, 4)
        def _(m):
            @pl.loop(0, LON_DEV)
            def _(j):
                for g in range(2):
                    acc = jnp.zeros(TILE, jnp.float32)
                    for t in range(4):
                        idx = smem_i[m, g, t, j]
                        acc = acc + smem_w[m, g, t, j] * recv_g[st][idx >> 4, idx & 15]
                    chunk[st, m, g, j] = acc

            zz = 2 * m + par

            @pl.when(zz != z)
            def _():
                rcopy(chunk.at[st, m], recv_n.at[st, z], n_send.at[st, m], n_recv.at[st, z],
                      (p, y, zz * 4 + w))

            @pl.when(zz == z)
            def _():
                pltpu.make_async_copy(chunk.at[st, m], recv_n.at[st, z], n_recv.at[st, z]).start()

    def sum_over_z(st):
        @pl.when(is_sum)
        def _():
            @pl.loop(0, N_Z)
            def _(zz):
                wait_on(recv_n.at[st, zz], n_recv.at[st, zz])

            for g in range(2):
                acc = recv_n[st, 0, g]
                for zz in range(1, N_Z):
                    acc = acc + recv_n[st, zz, g]
                summed[st, g] = acc
            rcopy(summed.at[st], lat_h.at[st, half], f_send.at[st], lat_recv.at[st, half],
                  (other, dest_lat, z * 4 + wx))

    def forward_ew(st):
        @pl.when(is_agg)
        def _():
            @pl.loop(0, 16)
            def _(k):
                wait_on(recv_e1.at[st, k], e1_recv.at[st, k])

            rcopy(recv_e1.at[st], recv_e2[st].at[z], e2_send.at[st], e2_recv.at[st, z],
                  (other, y, ew_lon))

    def border_ew(st):
        @pl.when(is_ew)
        def _():
            @pl.loop(0, N_Z)
            def _(zz):
                wait_on(recv_e2[st].at[zz], e2_recv.at[st, zz])

            @pl.loop(0, LAT_DEV)
            def _(i):
                for g in range(2):
                    acc = jnp.zeros(TILE, jnp.float32)
                    for t in range(4):
                        idx = smem_ei[g, t, i]
                        acc = acc + smem_ew[g, t, i] * recv_e2[st][idx >> 6, (idx >> 2) & 15, idx & 3]
                    lon_h[st, ew_side, i, g] = acc

    def wait_lon(st):
        @pl.when(b > 0)
        def _():
            wait_on(lon_h.at[st, 0], lon_recv.at[st, 0])

        @pl.when(b < N_LON - 1)
        def _():
            wait_on(lon_h.at[st, 1], lon_recv.at[st, 1])

    def wait_lat(st):
        for side in range(2):
            wait_on(lat_h.at[st, side], lat_recv.at[st, side])

    def target(st):
        if st == 0:
            return q_mid, 2, time_step * ct, time_step * ct2
        return res_ref, 0, 0.5 * time_step * ct, 0.5 * time_step * ct2

    def correct_lat(st):
        dst, off, sc, sc2 = target(st)
        hal = lat_h[st].reshape((48,) + TILE)
        mix_lat = jnp.concatenate(
            [unsplit(mixed(slice(320, 384), hal[16 * t:16 * (t + 1)]), 2) for t in range(3)],
            axis=0).reshape((2, 2, LON_DEV) + TILE)
        hal = hal.reshape((2, 2, LON_DEV) + TILE)
        dst[off] += sc * (mix_lat[0, 0] - 8.0 * mix_lat[0, 1]) + sc2 * (16.0 * hal[0, 1] - hal[0, 0])
        dst[off + 1] += sc * mix_lat[0, 1] - sc2 * hal[0, 1]
        dst[off + 63] += sc * (8.0 * mix_lat[1, 0] - mix_lat[1, 1]) + sc2 * (16.0 * hal[1, 0] - hal[1, 1])
        dst[off + 62] += -sc * mix_lat[1, 0] - sc2 * hal[1, 0]

    def correct_lon(st):
        dst, off, sc, sc2 = target(st)

        @pl.loop(0, LAT_DEV // 4)
        def _(c):
            i0 = c * 4
            west = lon_h[st, 0, pl.ds(i0, 4)].reshape((8,) + TILE)
            east = lon_h[st, 1, pl.ds(i0, 4)].reshape((8,) + TILE)
            both = unsplit(mixed(slice(384, 448), jnp.concatenate([west, east], axis=0)), 2)
            for n in range(4):
                i = i0 + n
                si = inv_sin(i)
                a1 = sc * si
                a2 = sc2 * (si * si)
                w2, w1, pw2, pw1 = west[2 * n], west[2 * n + 1], both[2 * n], both[2 * n + 1]
                e1, e2, pe1, pe2 = east[2 * n], east[2 * n + 1], both[8 + 2 * n], both[9 + 2 * n]
                dst[off + i, 0] += a1 * (pw2 - 8.0 * pw1) + a2 * (16.0 * w1 - w2)
                dst[off + i, 1] += a1 * pw1 - a2 * w1
                dst[off + i, 11] += a1 * (8.0 * pe1 - pe2) + a2 * (16.0 * e1 - e2)
                dst[off + i, 10] += -a1 * pe1 - a2 * e1

    load_state()

    @pl.loop(0, 8)
    def _(t):
        gather_e(0, q_init, t)

    @pl.loop(0, 16)
    def _(n):
        gather_g(0, q_init, n)

    prepare_indices()
    build_lhs()
    build_sines()
    pl.semaphore_wait(bar, peers)

    for st, cur in ((0, q_init), (1, q_mid)):
        @pl.loop(0, 8)
        def _(t):
            if st == 1:
                gather_e(st, cur, t)
            start_e(st, t)

        if st == 0:
            send_indices()

        @pl.loop(0, 16)
        def _(n):
            k = turn(n)
            if st == 1:
                gather_g(st, cur, k)
            start_g(st, k)

        if st == 0:
            adjust_indices()
        forward_ew(st)
        products(cur)
        aggregate(st)
        halos(st, cur)
        stencil(st, cur)
        sum_over_z(st)
        wait_lon(st)
        border_ew(st)
        correct_lon(st)
        wait_lat(st)
        correct_lat(st)

    @pl.loop(0, LAT_DEV // 8)
    def _(ib):
        i0 = pl.multiple_of(ib * 8, 8)
        for j in range(LON_DEV):
            v = res_ref[pl.ds(i0, 8), j]
            out_ref[:, pl.ds(i0, 8), j * NR:(j + 1) * NR] = jnp.swapaxes(v, 0, 1)

    @pl.when(is_sum)
    def _():
        @pl.loop(0, N_Z)
        def _(zz):
            wait_on(own_i, i_send.at[0, zz])
            wait_on(own_w, i_send.at[1, zz])

    for st in range(2):
        @pl.loop(0, 16)
        def _(k):
            @pl.when(k != me_k)
            def _():
                wait_on(send_g.at[st, k], g_send.at[st, k])

        @pl.loop(0, 8)
        def _(t):
            @pl.when(ew_member(t) != me_k)
            def _():
                wait_on(send_e.at[st, t], e1_send.at[st, t])

        @pl.loop(0, 4)
        def _(m):
            @pl.when(2 * m + par != z)
            def _():
                wait_on(chunk.at[st, m], n_send.at[st, m])

        @pl.when(is_sum)
        def _():
            wait_on(summed.at[st], f_send.at[st])

        @pl.when(is_agg)
        def _():
            wait_on(recv_e1.at[st], e2_send.at[st])

        @pl.when(b < N_LON - 1)
        def _():
            wait_on(lon_h.at[st, 0], lon_send.at[st, 0])

        @pl.when(b > 0)
        def _():
            wait_on(lon_h.at[st, 1], lon_send.at[st, 1])

        @pl.when(y < N_LAT - 1)
        def _():
            wait_on(lat_h.at[st, 0], lat_send.at[st, 0])

        @pl.when(y > 0)
        def _():
            wait_on(lat_h.at[st, 1], lat_send.at[st, 1])


def local(
    fields, coupling, export_index, ghost_ns_index, ghost_ns_frac, ghost_ew_index, ghost_ew_frac
):
    x = fields[0]
    exports = export_index.reshape(-1)
    nsi = jnp.swapaxes(ghost_ns_index[0], 2, 3)
    nsf = jnp.swapaxes(ghost_ns_frac[0], 2, 3)
    ewi = jnp.transpose(ghost_ew_index[0], (0, 2, 3, 1))
    ewf = jnp.transpose(ghost_ew_frac[0], (0, 2, 3, 1))

    vm = pl.BlockSpec(memory_space=pltpu.VMEM)
    sm = pl.BlockSpec(memory_space=pltpu.SMEM)
    hbm = pl.BlockSpec(memory_space=pl.ANY)
    V = lambda *shape: pltpu.VMEM(shape + TILE, jnp.float32)
    I = lambda *shape: pltpu.VMEM(shape + TILE, jnp.int32)
    D = lambda *shape: pltpu.SemaphoreType.DMA(shape)
    out = pl.pallas_call(
        kernel,
        out_shape=jax.ShapeDtypeStruct(x.shape, jnp.float32),
        in_specs=[hbm, vm, vm, vm, sm, vm, vm],
        out_specs=vm,
        scratch_shapes=[
            pltpu.VMEM(x.shape, jnp.float32),
            V(LAT_DEV + 4, LON_DEV), V(LAT_DEV + 4, LON_DEV), V(LAT_DEV + 4, LON_DEV),
            V(LAT_DEV, LON_DEV), V(LAT_DEV, LON_DEV), V(LAT_DEV, LON_DEV),
            pltpu.VMEM((448, 192), jnp.bfloat16), pltpu.VMEM((LAT_DEV, NR), jnp.float32),
            V(2, 16, 16), V(16, 16), V(16, 16), V(2, 8, 4), V(2, 16, 4), V(N_Z, 16, 4), V(N_Z, 16, 4),
            V(2, 4, 2, LON_DEV), V(2, N_Z, 2, LON_DEV), V(2, 2, LON_DEV),
            V(2, 2, 2, LON_DEV), V(2, 2, LAT_DEV, 2),
            I(2), V(2), I(4, 2), V(4, 2), I(4, 2), V(4, 2),
            pltpu.SMEM((4, 2) + TILE, jnp.int32), pltpu.SMEM((4, 2) + TILE, jnp.float32),
            I(2), V(2), pltpu.SMEM((2,) + TILE, jnp.int32), pltpu.SMEM((2,) + TILE, jnp.float32),
            D(2, 16), D(2, 16), D(2, 8), D(2, 16), D(2, 8), D(2, 4), D(2, 4), D(2, N_Z), D(2),
            D(2), D(2, N_Z), D(2, 2), D(2, 2), D(2, 2), D(2, 2), D(5),
        ],
        compiler_params=pltpu.CompilerParams(
            collective_id=0, has_side_effects=True, vmem_limit_bytes=60 * 2**20),
        name="two_sections",
    )(x, coupling, nsi, nsf, exports, ewi, ewf)
    return out[None]


def solution(mesh):
    placed = (
        P("panel", None, "lat", "lon"),
        P(),
        P("panel", "lat", "lon", None),
        P("panel", None, None, "lon", None),
        P("panel", None, None, "lon", None),
        P("panel", None, "lat", None, None),
        P("panel", None, "lat", None, None),
    )
    return jax.shard_map(
        local, mesh=mesh, in_specs=placed, out_specs=P("panel", None, "lat", "lon"), check_vma=False
    )
```

```python
import math

import jax
import jax.numpy as jnp
from jax import lax
from jax.experimental import pallas as pl
from jax.experimental.pallas import tpu as pltpu
from jax.sharding import PartitionSpec as P

NR = 128
FIELDS = 8
LAT_DEV = 64
LON_DEV = 12
N_LAT = 4
N_LON = 32
N_Z = 8

time_step = 0.15
viscosity = 0.1
inner_radius = 0.35

MESH = pl.DeviceIdType.MESH
TILE = (FIELDS, NR)


def kernel(
    x_ref, coup_ref, nsi_ref, nsf_ref, exp_ref, ewi_ref, ewf_ref,
    out_ref,
    x_buf, q_init, q_mid, p_lat, p_lon, s_ref, res_ref, lhs_ref, isin_ref,
    send_g, g00, g01, g02, g03, g10, g11, g12, g13, send_e, recv_e1, recv_e20, recv_e21, chunk, recv_n, summed,
    lat_h, lon_h,
    own_i, own_w, got_i, got_w, adj_i, adj_w, smem_i, smem_w,
    adj_ei, adj_ew, smem_ei, smem_ew,
    g_send, g_recv, e1_send, e1_recv, i_send, i_recv, n_send, n_recv, f_send,
    e2_send, e2_recv, lat_send, lat_recv, lon_send, lon_recv, loc_sem,
):
    recv_g = ((g00, g01, g02, g03), (g10, g11, g12, g13))
    recv_e2 = (recv_e20, recv_e21)
    p = lax.axis_index("panel")
    y = lax.axis_index("lat")
    b = lax.axis_index("lon")
    z = b // 4
    w = b % 4
    other = 1 - p
    wx = (w + 2) % 4
    me_k = y * 4 + w
    upper = y >= 2
    half = jnp.where(upper, 1, 0)
    par = jnp.where(upper, 3 - y, y)
    dest_lat = jnp.where(upper, 3, 0)
    is_sum = (z % 2) == par
    is_ns = (y == 0) | (y == 3)
    is_agg = (w == 1) | (w == 2)
    ew_lon = jnp.where(w == 2, 0, N_LON - 1)
    is_ew = (b == 0) | (b == N_LON - 1)
    ew_side = jnp.where(b == 0, 0, 1)
    star = jnp.where(y == 0, z % 2, 3 - z % 2)

    x_copy = pltpu.make_async_copy(x_ref, x_buf, loc_sem.at[0])
    x_copy.start()

    bar = pltpu.get_barrier_semaphore()

    def greet(dev):
        pl.semaphore_signal(bar, inc=1, device_id=dev, device_id_type=MESH)

    @pl.loop(0, 16)
    def _(k):
        @pl.when(k != me_k)
        def _():
            greet((p, k // 4, z * 4 + k % 4))

    @pl.loop(0, 4)
    def _(m):
        greet((other, y, (2 * m + par) * 4 + wx))

    @pl.loop(0, N_Z)
    def _(zz):
        @pl.when(is_sum & (zz != z))
        def _():
            greet((p, y, zz * 4 + w))

        @pl.when(is_ew)
        def _():
            greet((other, y, zz * 4 + wx))

    @pl.when(is_ns)
    def _():
        greet((other, star, z * 4 + wx))

    @pl.when(y > 0)
    def _():
        greet((p, y - 1, b))

    @pl.when(y < N_LAT - 1)
    def _():
        greet((p, y + 1, b))

    @pl.when(b > 0)
    def _():
        greet((p, y, b - 1))

    @pl.when(b < N_LON - 1)
    def _():
        greet((p, y, b + 1))

    one = lambda cond: jnp.where(cond, 1, 0)
    peers = (
        15 + 4 + 8 * one(is_sum) + one(is_agg)
        + one(y > 0) + one(y < N_LAT - 1) + one(b > 0) + one(b < N_LON - 1)
    )

    def rcopy(src, dst, ssem, rsem, dev):
        pltpu.make_async_remote_copy(
            src_ref=src, dst_ref=dst, send_sem=ssem, recv_sem=rsem,
            device_id=dev, device_id_type=MESH,
        ).start()

    def wait_on(ref, sem):
        pltpu.make_async_copy(ref, ref, sem).wait()

    row = lax.broadcasted_iota(jnp.int32, TILE, 0)

    def weights_of(frac):
        a, c = frac[0:1], frac[1:2]
        return jnp.where(row % 2 == 1, a, 1.0 - a) * jnp.where(row % 4 >= 2, c, 1.0 - c)

    def prepare_indices():
        own_i[...] = jnp.zeros(own_i.shape, jnp.int32)
        own_w[...] = jnp.zeros(own_w.shape, jnp.float32)
        adj_ei[...] = jnp.zeros(adj_ei.shape, jnp.int32)
        adj_ew[...] = jnp.zeros(adj_ew.shape, jnp.float32)
        for g in range(2):
            own_i[g, 0:4, 0:LON_DEV] = nsi_ref[half, g]
            own_w[g, 0:2, 0:LON_DEV] = nsf_ref[half, g]
            own_w[g] = weights_of(own_w[g])
            adj_ei[g, 0:4, 0:LAT_DEV] = ewi_ref[ew_side, g]
            adj_ew[g, 0:2, 0:LAT_DEV] = ewf_ref[ew_side, g]
            adj_ew[g] = weights_of(adj_ew[g])
            s = adj_ei[g]
            col = (s >> 2) & (N_LON - 1)
            k = (s >> 7) * 4 + (col & 3)
            adj_ei[g] = (col >> 2) * 64 + k * 4 + (s & 3)
        copies = [pltpu.make_async_copy(adj_ei, smem_ei, loc_sem.at[1]),
                  pltpu.make_async_copy(adj_ew, smem_ew, loc_sem.at[2])]
        for c in copies:
            c.start()
        for c in copies:
            c.wait()

    def send_indices():
        @pl.when(is_sum)
        def _():
            @pl.loop(0, N_Z)
            def _(zz):
                dev = (other, y, zz * 4 + wx)
                rcopy(own_i, got_i.at[z // 2], i_send.at[0, zz], i_recv.at[0, z // 2], dev)
                rcopy(own_w, got_w.at[z // 2], i_send.at[1, zz], i_recv.at[1, z // 2], dev)

    def adjust_indices():
        for m in range(4):
            wait_on(got_i.at[m], i_recv.at[0, m])
            wait_on(got_w.at[m], i_recv.at[1, m])
            s = got_i[m]
            col = (s >> 2) & (N_LON - 1)
            k = (s >> 7) * 4 + (col & 3)
            adj_i[m] = k * 4 + (s & 3)
            adj_w[m] = jnp.where((col >> 2) == z, got_w[m], 0.0)
        copies = [pltpu.make_async_copy(adj_i, smem_i, loc_sem.at[3]),
                  pltpu.make_async_copy(adj_w, smem_w, loc_sem.at[4])]
        for c in copies:
            c.start()
        for c in copies:
            c.wait()

    def load_state():
        zero_rows = jnp.zeros((2, LON_DEV) + TILE, jnp.float32)
        for ref in (q_init, q_mid, p_lat):
            ref[0:2] = zero_rows
            ref[LAT_DEV + 2:LAT_DEV + 4] = zero_rows
        x_copy.wait()

        @pl.loop(0, LAT_DEV // 8)
        def _(ib):
            i0 = pl.multiple_of(ib * 8, 8)
            for j in range(LON_DEV):
                v = x_buf[:, pl.ds(i0, 8), j * NR:(j + 1) * NR]
                q_init[pl.ds(i0 + 2, 8), j] = jnp.swapaxes(v, 0, 1)

    radius = inner_radius + (1.0 - inner_radius) * (
        lax.broadcasted_iota(jnp.int32, TILE, 1).astype(jnp.float32) + 0.5) / NR
    ct = inner_radius / radius
    ct2 = ct * ct * (viscosity / 12.0)

    def build_sines():
        i = y * LAT_DEV + lax.broadcasted_iota(jnp.int32, (LAT_DEV, NR), 0)
        colat = math.pi / 4 + (i.astype(jnp.float32) + 0.5) * (math.pi / 2) / (LAT_DEV * N_LAT)
        isin_ref[...] = 1.0 / jnp.sin(colat)

    def inv_sin(i):
        return isin_ref[pl.ds(i, 1), :]

    def build_lhs():
        r64 = lax.broadcasted_iota(jnp.int32, (64, 8), 0) % 8
        c8 = lax.broadcasted_iota(jnp.int32, (64, 8), 1)
        ex = jnp.where(r64 == c8, 1.0, 0.0).astype(jnp.float32)
        r8 = lax.broadcasted_iota(jnp.int32, (8, 64), 0)
        c64 = lax.broadcasted_iota(jnp.int32, (8, 64), 1) % 8
        ext = jnp.where(r8 == c64, 1.0, 0.0).astype(jnp.float32)
        rr = lax.broadcasted_iota(jnp.int32, (64, 64), 0)
        cc = lax.broadcasted_iota(jnp.int32, (64, 64), 1)
        same = (rr // 8) == (cc // 8)
        eye = jnp.where(rr == cc, 1.0, 0.0).astype(jnp.float32)

        def kron(k):
            tall = jnp.dot(ex, coup_ref[k], precision=lax.Precision.HIGHEST,
                           preferred_element_type=jnp.float32)
            full = jnp.dot(tall, ext, precision=lax.Precision.HIGHEST,
                           preferred_element_type=jnp.float32)
            return jnp.where(same, full, 0.0)

        c0, c1, c2, c3 = kron(0), kron(1), kron(2), kron(3)
        nu = viscosity
        blocks = [
            (8.0 * c0 + 16.0 * nu * eye) / 12.0,
            (-8.0 * c0 + 16.0 * nu * eye) / 12.0,
            (-c0 - nu * eye) / 12.0,
            (c0 - nu * eye) / 12.0,
            c3 - (30.0 * nu / 12.0) * eye,
            c1 / -12.0,
            c2 / -12.0,
        ]
        for n, blk in enumerate(blocks):
            hi = blk.astype(jnp.bfloat16)
            lo = (blk - hi.astype(jnp.float32)).astype(jnp.bfloat16)
            lhs_ref[64 * n:64 * (n + 1), :] = jnp.concatenate([hi, hi, lo], axis=1)

    def split(cols):
        n = cols.shape[0] // 8
        flat = cols.reshape(n * 64, NR)
        wide = jnp.concatenate([flat[64 * t:64 * (t + 1)] for t in range(n)], axis=1)
        hi = wide.astype(jnp.bfloat16)
        lo = (wide - hi.astype(jnp.float32)).astype(jnp.bfloat16)
        return jnp.concatenate([hi, lo, hi], axis=0)

    def mixed(rows, cols):
        return jnp.dot(lhs_ref[rows], split(cols), preferred_element_type=jnp.float32)

    def unsplit(wide, n):
        return jnp.concatenate(
            [wide[:, NR * t:NR * (t + 1)] for t in range(n)], axis=0).reshape((8 * n,) + TILE)

    lane = lax.broadcasted_iota(jnp.int32, (64, NR), 1)

    def column(cur, idx):
        i = (idx * 43691) >> 19
        return cur[i + 2, idx - 12 * i]

    def group_of(k):
        ky = k // 4
        kup = ky >= 2
        kpar = jnp.where(kup, 3 - ky, ky)
        return (jnp.where(kup, 96, 0) + kpar * 4 + (k % 4 + 2) % 4) * 4

    def nth(n):
        return lax.rem(z // 2 + 1 + n, 4)

    def gather_g(st, cur, n, k):
        first = group_of(k) + nth(n) * 32
        for s in range(4):
            send_g[st, n, k, s] = column(cur, exp_ref[first + s])

    def start_g(st, n, k):
        dst = recv_g[st][n].at[pl.ds(me_k * 4, 4)]

        @pl.when(k != me_k)
        def _():
            rcopy(send_g.at[st, n, k], dst, g_send.at[st, n, k],
                  g_recv.at[st, n, me_k], (p, k // 4, z * 4 + k % 4))

        @pl.when(k == me_k)
        def _():
            pltpu.make_async_copy(send_g.at[st, n, k], dst, g_recv.at[st, n, me_k]).start()

    def gather_e(st, cur, t):
        first = ((t // 2) * N_LON + (t % 2) * (N_LON - 1)) * 4
        for s in range(4):
            send_e[st, t, s] = column(cur, exp_ref[first + s])

    def ew_member(t):
        return (t // 2) * 4 + 2 - t % 2

    def start_e(st, t):
        k = ew_member(t)

        @pl.when(k != me_k)
        def _():
            rcopy(send_e.at[st, t], recv_e1.at[st, me_k], e1_send.at[st, t],
                  e1_recv.at[st, me_k], (p, k // 4, z * 4 + k % 4))

        @pl.when(k == me_k)
        def _():
            pltpu.make_async_copy(
                send_e.at[st, t], recv_e1.at[st, me_k], e1_recv.at[st, me_k]).start()

    def turn(n):
        return lax.rem(me_k + 1 + n, 16)

    def halos(st, cur):
        @pl.when(y < N_LAT - 1)
        def _():
            rcopy(cur.at[LAT_DEV:LAT_DEV + 2], lat_h.at[st, 0], lat_send.at[st, 0],
                  lat_recv.at[st, 0], (p, y + 1, b))

        @pl.when(y > 0)
        def _():
            rcopy(cur.at[2:4], lat_h.at[st, 1], lat_send.at[st, 1],
                  lat_recv.at[st, 1], (p, y - 1, b))

        @pl.when(b < N_LON - 1)
        def _():
            rcopy(cur.at[2:LAT_DEV + 2, 10:12], lon_h.at[st, 0], lon_send.at[st, 0],
                  lon_recv.at[st, 0], (p, y, b + 1))

        @pl.when(b > 0)
        def _():
            rcopy(cur.at[2:LAT_DEV + 2, 0:2], lon_h.at[st, 1], lon_send.at[st, 1],
                  lon_recv.at[st, 1], (p, y, b - 1))

    def products(cur, quarter):
        @pl.loop(quarter * (LAT_DEV // 16), (quarter + 1) * (LAT_DEV // 16))
        def _(c):
            i0 = c * 4
            cols = cur[pl.ds(i0 + 2, 4)].reshape((48,) + TILE)
            sums, lats, lons = [], [], []
            for t in range(3):
                wide = mixed(slice(0, 448), cols[16 * t:16 * (t + 1)])
                for h in range(2):
                    part = wide[:, NR * h:NR * (h + 1)]
                    total = part[256:320]
                    total = total + jnp.where(lane >= 1, pltpu.roll(part[0:64], 1, 1), 0.0)
                    total = total + jnp.where(lane < NR - 1, pltpu.roll(part[64:128], NR - 1, 1), 0.0)
                    total = total + jnp.where(lane >= 2, pltpu.roll(part[128:192], 2, 1), 0.0)
                    total = total + jnp.where(lane < NR - 2, pltpu.roll(part[192:256], NR - 2, 1), 0.0)
                    sums.append(total)
                    lats.append(part[320:384])
                    lons.append(part[384:448])
            shape = (4, LON_DEV) + TILE
            s_ref[pl.ds(i0, 4)] = jnp.concatenate(sums, axis=0).reshape(shape)
            p_lat[pl.ds(i0 + 2, 4)] = jnp.concatenate(lats, axis=0).reshape(shape)
            p_lon[pl.ds(i0, 4)] = jnp.concatenate(lons, axis=0).reshape(shape)

    def shifted(v, n):
        pad = jnp.zeros((abs(n),) + TILE, jnp.float32)
        if n > 0:
            return jnp.concatenate([v[n:], pad], axis=0)
        return jnp.concatenate([pad, v[:n]], axis=0)

    def stencil(st, cur):
        @pl.loop(0, LAT_DEV)
        def _(i):
            si = inv_sin(i)
            q0 = cur[i + 2]
            pl0 = p_lon[i]
            d1 = (p_lat[i] - p_lat[i + 4]) + 8.0 * (p_lat[i + 3] - p_lat[i + 1])
            e1 = (shifted(pl0, -2) - shifted(pl0, 2)) + 8.0 * (shifted(pl0, 1) - shifted(pl0, -1))
            d2 = 16.0 * (cur[i + 1] + cur[i + 3]) - (cur[i] + cur[i + 4])
            e2 = 16.0 * (shifted(q0, -1) + shifted(q0, 1)) - (shifted(q0, -2) + shifted(q0, 2))
            rate = s_ref[i] + ct * (d1 + si * e1) + ct2 * (
                d2 + (si * si) * e2 - (30.0 * (1.0 + si * si)) * q0)
            if st == 0:
                q_mid[i + 2] = q0 + time_step * rate
            else:
                res_ref[i] = 0.5 * q_init[i + 2] + 0.5 * (q0 + time_step * rate)

    def aggregate(st, n):
        got = recv_g[st][n]

        @pl.loop(0, 16)
        def _(k):
            wait_on(got.at[pl.ds(k * 4, 4)], g_recv.at[st, n, k])

        m = nth(n)

        @pl.loop(0, LON_DEV)
        def _(j):
            for g in range(2):
                acc = jnp.zeros(TILE, jnp.float32)
                for t in range(4):
                    acc = acc + smem_w[m, g, t, j] * got[smem_i[m, g, t, j]]
                chunk[st, n, g, j] = acc

        zz = 2 * m + par

        @pl.when(zz != z)
        def _():
            rcopy(chunk.at[st, n], recv_n.at[st, z], n_send.at[st, n], n_recv.at[st, z],
                  (p, y, zz * 4 + w))

        @pl.when(zz == z)
        def _():
            pltpu.make_async_copy(chunk.at[st, n], recv_n.at[st, z], n_recv.at[st, z]).start()

    def sum_over_z(st):
        @pl.when(is_sum)
        def _():
            @pl.loop(0, N_Z)
            def _(zz):
                wait_on(recv_n.at[st, zz], n_recv.at[st, zz])

            for g in range(2):
                acc = recv_n[st, 0, g]
                for zz in range(1, N_Z):
                    acc = acc + recv_n[st, zz, g]
                summed[st, g] = acc
            rcopy(summed.at[st], lat_h.at[st, half], f_send.at[st], lat_recv.at[st, half],
                  (other, dest_lat, z * 4 + wx))

    def forward_ew(st):
        @pl.when(is_agg)
        def _():
            @pl.loop(0, 16)
            def _(k):
                wait_on(recv_e1.at[st, k], e1_recv.at[st, k])

            rcopy(recv_e1.at[st], recv_e2[st].at[z], e2_send.at[st], e2_recv.at[st, z],
                  (other, y, ew_lon))

    def border_ew(st):
        @pl.when(is_ew)
        def _():
            @pl.loop(0, N_Z)
            def _(zz):
                wait_on(recv_e2[st].at[zz], e2_recv.at[st, zz])

            @pl.loop(0, LAT_DEV)
            def _(i):
                for g in range(2):
                    acc = jnp.zeros(TILE, jnp.float32)
                    for t in range(4):
                        idx = smem_ei[g, t, i]
                        acc = acc + smem_ew[g, t, i] * recv_e2[st][idx >> 6, (idx >> 2) & 15, idx & 3]
                    lon_h[st, ew_side, i, g] = acc

    def wait_lon(st):
        @pl.when(b > 0)
        def _():
            wait_on(lon_h.at[st, 0], lon_recv.at[st, 0])

        @pl.when(b < N_LON - 1)
        def _():
            wait_on(lon_h.at[st, 1], lon_recv.at[st, 1])

    def wait_lat(st):
        for side in range(2):
            wait_on(lat_h.at[st, side], lat_recv.at[st, side])

    def target(st):
        if st == 0:
            return q_mid, 2, time_step * ct, time_step * ct2
        return res_ref, 0, 0.5 * time_step * ct, 0.5 * time_step * ct2

    def correct_lat(st):
        dst, off, sc, sc2 = target(st)
        hal = lat_h[st].reshape((48,) + TILE)
        mix_lat = jnp.concatenate(
            [unsplit(mixed(slice(320, 384), hal[16 * t:16 * (t + 1)]), 2) for t in range(3)],
            axis=0).reshape((2, 2, LON_DEV) + TILE)
        hal = hal.reshape((2, 2, LON_DEV) + TILE)
        dst[off] += sc * (mix_lat[0, 0] - 8.0 * mix_lat[0, 1]) + sc2 * (16.0 * hal[0, 1] - hal[0, 0])
        dst[off + 1] += sc * mix_lat[0, 1] - sc2 * hal[0, 1]
        dst[off + 63] += sc * (8.0 * mix_lat[1, 0] - mix_lat[1, 1]) + sc2 * (16.0 * hal[1, 0] - hal[1, 1])
        dst[off + 62] += -sc * mix_lat[1, 0] - sc2 * hal[1, 0]

    def correct_lon(st):
        dst, off, sc, sc2 = target(st)

        @pl.loop(0, LAT_DEV // 4)
        def _(c):
            i0 = c * 4
            west = lon_h[st, 0, pl.ds(i0, 4)].reshape((8,) + TILE)
            east = lon_h[st, 1, pl.ds(i0, 4)].reshape((8,) + TILE)
            both = unsplit(mixed(slice(384, 448), jnp.concatenate([west, east], axis=0)), 2)
            for n in range(4):
                i = i0 + n
                si = inv_sin(i)
                a1 = sc * si
                a2 = sc2 * (si * si)
                w2, w1, pw2, pw1 = west[2 * n], west[2 * n + 1], both[2 * n], both[2 * n + 1]
                e1, e2, pe1, pe2 = east[2 * n], east[2 * n + 1], both[8 + 2 * n], both[9 + 2 * n]
                dst[off + i, 0] += a1 * (pw2 - 8.0 * pw1) + a2 * (16.0 * w1 - w2)
                dst[off + i, 1] += a1 * pw1 - a2 * w1
                dst[off + i, 11] += a1 * (8.0 * pe1 - pe2) + a2 * (16.0 * e1 - e2)
                dst[off + i, 10] += -a1 * pe1 - a2 * e1

    load_state()

    @pl.loop(0, 8)
    def _(t):
        gather_e(0, q_init, t)

    for n in range(4):
        @pl.loop(0, 16)
        def _(k):
            gather_g(0, q_init, n, k)

    prepare_indices()
    build_lhs()
    build_sines()
    pl.semaphore_wait(bar, peers)

    for st, cur in ((0, q_init), (1, q_mid)):
        @pl.loop(0, 8)
        def _(t):
            if st == 1:
                gather_e(st, cur, t)
            start_e(st, t)

        if st == 0:
            send_indices()

        for n in range(4):
            @pl.loop(0, 16)
            def _(r):
                k = turn(r)
                if st == 1:
                    gather_g(st, cur, n, k)
                start_g(st, n, k)

        if st == 0:
            adjust_indices()
        products(cur, 0)
        forward_ew(st)
        products(cur, 1)
        aggregate(st, 0)
        products(cur, 2)
        aggregate(st, 1)
        products(cur, 3)
        aggregate(st, 2)
        aggregate(st, 3)
        halos(st, cur)
        stencil(st, cur)
        sum_over_z(st)
        wait_lon(st)
        border_ew(st)
        correct_lon(st)
        wait_lat(st)
        correct_lat(st)

    @pl.loop(0, LAT_DEV // 8)
    def _(ib):
        i0 = pl.multiple_of(ib * 8, 8)
        for j in range(LON_DEV):
            v = res_ref[pl.ds(i0, 8), j]
            out_ref[:, pl.ds(i0, 8), j * NR:(j + 1) * NR] = jnp.swapaxes(v, 0, 1)

    @pl.when(is_sum)
    def _():
        @pl.loop(0, N_Z)
        def _(zz):
            wait_on(own_i, i_send.at[0, zz])
            wait_on(own_w, i_send.at[1, zz])

    for st in range(2):
        for n in range(4):
            @pl.loop(0, 16)
            def _(k):
                @pl.when(k != me_k)
                def _():
                    wait_on(send_g.at[st, n, k], g_send.at[st, n, k])

        @pl.loop(0, 8)
        def _(t):
            @pl.when(ew_member(t) != me_k)
            def _():
                wait_on(send_e.at[st, t], e1_send.at[st, t])

        for n in range(4):
            @pl.when(2 * nth(n) + par != z)
            def _():
                wait_on(chunk.at[st, n], n_send.at[st, n])

        @pl.when(is_sum)
        def _():
            wait_on(summed.at[st], f_send.at[st])

        @pl.when(is_agg)
        def _():
            wait_on(recv_e1.at[st], e2_send.at[st])

        @pl.when(b < N_LON - 1)
        def _():
            wait_on(lon_h.at[st, 0], lon_send.at[st, 0])

        @pl.when(b > 0)
        def _():
            wait_on(lon_h.at[st, 1], lon_send.at[st, 1])

        @pl.when(y < N_LAT - 1)
        def _():
            wait_on(lat_h.at[st, 0], lat_send.at[st, 0])

        @pl.when(y > 0)
        def _():
            wait_on(lat_h.at[st, 1], lat_send.at[st, 1])


def local(
    fields, coupling, export_index, ghost_ns_index, ghost_ns_frac, ghost_ew_index, ghost_ew_frac
):
    x = fields[0]
    exports = export_index.reshape(-1)
    nsi = jnp.swapaxes(ghost_ns_index[0], 2, 3)
    nsf = jnp.swapaxes(ghost_ns_frac[0], 2, 3)
    ewi = jnp.transpose(ghost_ew_index[0], (0, 2, 3, 1))
    ewf = jnp.transpose(ghost_ew_frac[0], (0, 2, 3, 1))

    vm = pl.BlockSpec(memory_space=pltpu.VMEM)
    sm = pl.BlockSpec(memory_space=pltpu.SMEM)
    hbm = pl.BlockSpec(memory_space=pl.ANY)
    V = lambda *shape: pltpu.VMEM(shape + TILE, jnp.float32)
    I = lambda *shape: pltpu.VMEM(shape + TILE, jnp.int32)
    D = lambda *shape: pltpu.SemaphoreType.DMA(shape)
    out = pl.pallas_call(
        kernel,
        out_shape=jax.ShapeDtypeStruct(x.shape, jnp.float32),
        in_specs=[hbm, vm, vm, vm, sm, vm, vm],
        out_specs=vm,
        scratch_shapes=[
            pltpu.VMEM(x.shape, jnp.float32),
            V(LAT_DEV + 4, LON_DEV), V(LAT_DEV + 4, LON_DEV), V(LAT_DEV + 4, LON_DEV),
            V(LAT_DEV, LON_DEV), V(LAT_DEV, LON_DEV), V(LAT_DEV, LON_DEV),
            pltpu.VMEM((448, 192), jnp.bfloat16), pltpu.VMEM((LAT_DEV, NR), jnp.float32),
            V(2, 4, 16, 4)] + [V(64)] * 8 + [V(2, 8, 4), V(2, 16, 4), V(N_Z, 16, 4), V(N_Z, 16, 4),
            V(2, 4, 2, LON_DEV), V(2, N_Z, 2, LON_DEV), V(2, 2, LON_DEV),
            V(2, 2, 2, LON_DEV), V(2, 2, LAT_DEV, 2),
            I(2), V(2), I(4, 2), V(4, 2), I(4, 2), V(4, 2),
            pltpu.SMEM((4, 2) + TILE, jnp.int32), pltpu.SMEM((4, 2) + TILE, jnp.float32),
            I(2), V(2), pltpu.SMEM((2,) + TILE, jnp.int32), pltpu.SMEM((2,) + TILE, jnp.float32),
            D(2, 4, 16), D(2, 4, 16), D(2, 8), D(2, 16), D(2, 8), D(2, 4), D(2, 4), D(2, N_Z), D(2),
            D(2), D(2, N_Z), D(2, 2), D(2, 2), D(2, 2), D(2, 2), D(5),
        ],
        compiler_params=pltpu.CompilerParams(
            collective_id=0, has_side_effects=True, vmem_limit_bytes=60 * 2**20),
        name="two_sections",
    )(x, coupling, nsi, nsf, exports, ewi, ewf)
    return out[None]


def solution(mesh):
    placed = (
        P("panel", None, "lat", "lon"),
        P(),
        P("panel", "lat", "lon", None),
        P("panel", None, None, "lon", None),
        P("panel", None, None, "lon", None),
        P("panel", None, "lat", None, None),
        P("panel", None, "lat", None, None),
    )
    return jax.shard_map(
        local, mesh=mesh, in_specs=placed, out_specs=P("panel", None, "lat", "lon"), check_vma=False
    )
```

```python
import math

import jax
import jax.numpy as jnp
from jax import lax
from jax.experimental import pallas as pl
from jax.experimental.pallas import tpu as pltpu
from jax.sharding import PartitionSpec as P

NR = 128
FIELDS = 8
LAT_DEV = 64
LON_DEV = 12
N_LAT = 4
N_LON = 32
N_Z = 8

time_step = 0.15
viscosity = 0.1
inner_radius = 0.35

MESH = pl.DeviceIdType.MESH
TILE = (FIELDS, NR)


def kernel(
    x_ref, coup_ref, nsi_ref, nsf_ref, exp_ref, ewi_ref, ewf_ref,
    out_ref,
    q_init, q_mid, p_lat, p_lon, s_ref, res_ref, lhs_ref, isin_ref,
    send_g, g00, g01, g02, g03, g10, g11, g12, g13, send_e, recv_e1, recv_e20, recv_e21, chunk, recv_n, summed,
    lat_h, lon_h,
    own_i, own_w, got_i, got_w, adj_i, adj_w, smem_i, smem_w,
    adj_ei, adj_ew, smem_ei, smem_ew,
    g_send, g_recv, e1_send, e1_recv, i_send, i_recv, n_send, n_recv, f_send,
    e2_send, e2_recv, lat_send, lat_recv, lon_send, lon_recv, loc_sem,
):
    recv_g = ((g00, g01, g02, g03), (g10, g11, g12, g13))
    recv_e2 = (recv_e20, recv_e21)
    p = lax.axis_index("panel")
    y = lax.axis_index("lat")
    b = lax.axis_index("lon")
    z = b // 4
    w = b % 4
    other = 1 - p
    wx = (w + 2) % 4
    me_k = y * 4 + w
    upper = y >= 2
    half = jnp.where(upper, 1, 0)
    par = jnp.where(upper, 3 - y, y)
    dest_lat = jnp.where(upper, 3, 0)
    is_sum = (z % 2) == par
    is_ns = (y == 0) | (y == 3)
    is_agg = (w == 1) | (w == 2)
    ew_lon = jnp.where(w == 2, 0, N_LON - 1)
    is_ew = (b == 0) | (b == N_LON - 1)
    ew_side = jnp.where(b == 0, 0, 1)
    star = jnp.where(y == 0, z % 2, 3 - z % 2)

    x_copy = pltpu.make_async_copy(x_ref, out_ref, loc_sem.at[0])
    x_copy.start()

    bar = pltpu.get_barrier_semaphore()

    def greet(dev):
        pl.semaphore_signal(bar, inc=1, device_id=dev, device_id_type=MESH)

    @pl.loop(0, 16)
    def _(k):
        @pl.when(k != me_k)
        def _():
            greet((p, k // 4, z * 4 + k % 4))

    @pl.loop(0, 4)
    def _(m):
        greet((other, y, (2 * m + par) * 4 + wx))

    @pl.loop(0, N_Z)
    def _(zz):
        @pl.when(is_sum & (zz != z))
        def _():
            greet((p, y, zz * 4 + w))

        @pl.when(is_ew)
        def _():
            greet((other, y, zz * 4 + wx))

    @pl.when(is_ns)
    def _():
        greet((other, star, z * 4 + wx))

    @pl.when(y > 0)
    def _():
        greet((p, y - 1, b))

    @pl.when(y < N_LAT - 1)
    def _():
        greet((p, y + 1, b))

    @pl.when(b > 0)
    def _():
        greet((p, y, b - 1))

    @pl.when(b < N_LON - 1)
    def _():
        greet((p, y, b + 1))

    one = lambda cond: jnp.where(cond, 1, 0)
    peers = (
        15 + 4 + 8 * one(is_sum) + one(is_agg)
        + one(y > 0) + one(y < N_LAT - 1) + one(b > 0) + one(b < N_LON - 1)
    )

    def rcopy(src, dst, ssem, rsem, dev):
        pltpu.make_async_remote_copy(
            src_ref=src, dst_ref=dst, send_sem=ssem, recv_sem=rsem,
            device_id=dev, device_id_type=MESH,
        ).start()

    def wait_on(ref, sem):
        pltpu.make_async_copy(ref, ref, sem).wait()

    row = lax.broadcasted_iota(jnp.int32, TILE, 0)

    def weights_of(frac):
        a, c = frac[0:1], frac[1:2]
        return jnp.where(row % 2 == 1, a, 1.0 - a) * jnp.where(row % 4 >= 2, c, 1.0 - c)

    def prepare_indices():
        own_i[...] = jnp.zeros(own_i.shape, jnp.int32)
        own_w[...] = jnp.zeros(own_w.shape, jnp.float32)
        adj_ei[...] = jnp.zeros(adj_ei.shape, jnp.int32)
        adj_ew[...] = jnp.zeros(adj_ew.shape, jnp.float32)
        for g in range(2):
            own_i[g, 0:4, 0:LON_DEV] = nsi_ref[half, g]
            own_w[g, 0:2, 0:LON_DEV] = nsf_ref[half, g]
            own_w[g] = weights_of(own_w[g])
            adj_ei[g, 0:4, 0:LAT_DEV] = ewi_ref[ew_side, g]
            adj_ew[g, 0:2, 0:LAT_DEV] = ewf_ref[ew_side, g]
            adj_ew[g] = weights_of(adj_ew[g])
            s = adj_ei[g]
            col = (s >> 2) & (N_LON - 1)
            k = (s >> 7) * 4 + (col & 3)
            adj_ei[g] = (col >> 2) * 64 + k * 4 + (s & 3)
        copies = [pltpu.make_async_copy(adj_ei, smem_ei, loc_sem.at[1]),
                  pltpu.make_async_copy(adj_ew, smem_ew, loc_sem.at[2])]
        for c in copies:
            c.start()
        for c in copies:
            c.wait()

    def send_indices():
        @pl.when(is_sum)
        def _():
            @pl.loop(0, N_Z)
            def _(zz):
                dev = (other, y, zz * 4 + wx)
                rcopy(own_i, got_i.at[z // 2], i_send.at[0, zz], i_recv.at[0, z // 2], dev)
                rcopy(own_w, got_w.at[z // 2], i_send.at[1, zz], i_recv.at[1, z // 2], dev)

    def adjust_indices():
        for m in range(4):
            wait_on(got_i.at[m], i_recv.at[0, m])
            wait_on(got_w.at[m], i_recv.at[1, m])
            s = got_i[m]
            col = (s >> 2) & (N_LON - 1)
            k = (s >> 7) * 4 + (col & 3)
            adj_i[m] = k * 4 + (s & 3)
            adj_w[m] = jnp.where((col >> 2) == z, got_w[m], 0.0)
        copies = [pltpu.make_async_copy(adj_i, smem_i, loc_sem.at[3]),
                  pltpu.make_async_copy(adj_w, smem_w, loc_sem.at[4])]
        for c in copies:
            c.start()
        for c in copies:
            c.wait()

    def load_state():
        zero_rows = jnp.zeros((2, LON_DEV) + TILE, jnp.float32)
        for ref in (q_init, q_mid, p_lat):
            ref[0:2] = zero_rows
            ref[LAT_DEV + 2:LAT_DEV + 4] = zero_rows
        x_copy.wait()

        @pl.loop(0, LAT_DEV // 8)
        def _(ib):
            i0 = pl.multiple_of(ib * 8, 8)
            for j in range(LON_DEV):
                v = out_ref[:, pl.ds(i0, 8), j * NR:(j + 1) * NR]
                q_init[pl.ds(i0 + 2, 8), j] = jnp.swapaxes(v, 0, 1)

    radius = inner_radius + (1.0 - inner_radius) * (
        lax.broadcasted_iota(jnp.int32, TILE, 1).astype(jnp.float32) + 0.5) / NR
    ct = inner_radius / radius
    ct2 = ct * ct * (viscosity / 12.0)

    def build_sines():
        i = y * LAT_DEV + lax.broadcasted_iota(jnp.int32, (LAT_DEV, NR), 0)
        colat = math.pi / 4 + (i.astype(jnp.float32) + 0.5) * (math.pi / 2) / (LAT_DEV * N_LAT)
        isin_ref[...] = 1.0 / jnp.sin(colat)

    def inv_sin(i):
        return isin_ref[pl.ds(i, 1), :]

    def build_lhs():
        r64 = lax.broadcasted_iota(jnp.int32, (64, 8), 0) % 8
        c8 = lax.broadcasted_iota(jnp.int32, (64, 8), 1)
        ex = jnp.where(r64 == c8, 1.0, 0.0).astype(jnp.float32)
        r8 = lax.broadcasted_iota(jnp.int32, (8, 64), 0)
        c64 = lax.broadcasted_iota(jnp.int32, (8, 64), 1) % 8
        ext = jnp.where(r8 == c64, 1.0, 0.0).astype(jnp.float32)
        rr = lax.broadcasted_iota(jnp.int32, (64, 64), 0)
        cc = lax.broadcasted_iota(jnp.int32, (64, 64), 1)
        same = (rr // 8) == (cc // 8)
        eye = jnp.where(rr == cc, 1.0, 0.0).astype(jnp.float32)

        def kron(k):
            tall = jnp.dot(ex, coup_ref[k], precision=lax.Precision.HIGHEST,
                           preferred_element_type=jnp.float32)
            full = jnp.dot(tall, ext, precision=lax.Precision.HIGHEST,
                           preferred_element_type=jnp.float32)
            return jnp.where(same, full, 0.0)

        c0, c1, c2, c3 = kron(0), kron(1), kron(2), kron(3)
        nu = viscosity
        blocks = [
            (8.0 * c0 + 16.0 * nu * eye) / 12.0,
            (-8.0 * c0 + 16.0 * nu * eye) / 12.0,
            (-c0 - nu * eye) / 12.0,
            (c0 - nu * eye) / 12.0,
            c3 - (30.0 * nu / 12.0) * eye,
            c1 / -12.0,
            c2 / -12.0,
        ]
        for n, blk in enumerate(blocks):
            hi = blk.astype(jnp.bfloat16)
            lo = (blk - hi.astype(jnp.float32)).astype(jnp.bfloat16)
            lhs_ref[64 * n:64 * (n + 1), :] = jnp.concatenate([hi, hi, lo], axis=1)

    def split(cols):
        n = cols.shape[0] // 8
        flat = cols.reshape(n * 64, NR)
        wide = jnp.concatenate([flat[64 * t:64 * (t + 1)] for t in range(n)], axis=1)
        hi = wide.astype(jnp.bfloat16)
        lo = (wide - hi.astype(jnp.float32)).astype(jnp.bfloat16)
        return jnp.concatenate([hi, lo, hi], axis=0)

    def mixed(rows, cols):
        return jnp.dot(lhs_ref[rows], split(cols), preferred_element_type=jnp.float32)

    def unsplit(wide, n):
        return jnp.concatenate(
            [wide[:, NR * t:NR * (t + 1)] for t in range(n)], axis=0).reshape((8 * n,) + TILE)

    lane = lax.broadcasted_iota(jnp.int32, (64, NR), 1)

    def column(cur, idx):
        i = (idx * 43691) >> 19
        return cur[i + 2, idx - 12 * i]

    def group_of(k):
        ky = k // 4
        kup = ky >= 2
        kpar = jnp.where(kup, 3 - ky, ky)
        return (jnp.where(kup, 96, 0) + kpar * 4 + (k % 4 + 2) % 4) * 4

    def nth(n):
        return lax.rem(z // 2 + 1 + n, 4)

    def gather_g(st, cur, n, k):
        first = group_of(k) + nth(n) * 32
        for s in range(4):
            send_g[st, n, k, s] = column(cur, exp_ref[first + s])

    def start_g(st, n, k):
        dst = recv_g[st][n].at[pl.ds(me_k * 4, 4)]

        @pl.when(k != me_k)
        def _():
            rcopy(send_g.at[st, n, k], dst, g_send.at[st, n, k],
                  g_recv.at[st, n, me_k], (p, k // 4, z * 4 + k % 4))

        @pl.when(k == me_k)
        def _():
            pltpu.make_async_copy(send_g.at[st, n, k], dst, g_recv.at[st, n, me_k]).start()

    def gather_e(st, cur, t):
        first = ((t // 2) * N_LON + (t % 2) * (N_LON - 1)) * 4
        for s in range(4):
            send_e[st, t, s] = column(cur, exp_ref[first + s])

    def ew_member(t):
        return (t // 2) * 4 + 2 - t % 2

    def start_e(st, t):
        k = ew_member(t)

        @pl.when(k != me_k)
        def _():
            rcopy(send_e.at[st, t], recv_e1.at[st, me_k], e1_send.at[st, t],
                  e1_recv.at[st, me_k], (p, k // 4, z * 4 + k % 4))

        @pl.when(k == me_k)
        def _():
            pltpu.make_async_copy(
                send_e.at[st, t], recv_e1.at[st, me_k], e1_recv.at[st, me_k]).start()

    def turn(n):
        return lax.rem(me_k + 1 + n, 16)

    def halos(st, cur):
        @pl.when(y < N_LAT - 1)
        def _():
            rcopy(cur.at[LAT_DEV:LAT_DEV + 2], lat_h.at[st, 0], lat_send.at[st, 0],
                  lat_recv.at[st, 0], (p, y + 1, b))

        @pl.when(y > 0)
        def _():
            rcopy(cur.at[2:4], lat_h.at[st, 1], lat_send.at[st, 1],
                  lat_recv.at[st, 1], (p, y - 1, b))

        @pl.when(b < N_LON - 1)
        def _():
            rcopy(cur.at[2:LAT_DEV + 2, 10:12], lon_h.at[st, 0], lon_send.at[st, 0],
                  lon_recv.at[st, 0], (p, y, b + 1))

        @pl.when(b > 0)
        def _():
            rcopy(cur.at[2:LAT_DEV + 2, 0:2], lon_h.at[st, 1], lon_send.at[st, 1],
                  lon_recv.at[st, 1], (p, y, b - 1))

    def products(cur, quarter):
        @pl.loop(quarter * (LAT_DEV // 16), (quarter + 1) * (LAT_DEV // 16))
        def _(c):
            i0 = c * 4
            cols = cur[pl.ds(i0 + 2, 4)].reshape((48,) + TILE)
            sums, lats, lons = [], [], []
            for t in range(3):
                wide = mixed(slice(0, 448), cols[16 * t:16 * (t + 1)])
                for h in range(2):
                    part = wide[:, NR * h:NR * (h + 1)]
                    total = part[256:320]
                    total = total + jnp.where(lane >= 1, pltpu.roll(part[0:64], 1, 1), 0.0)
                    total = total + jnp.where(lane < NR - 1, pltpu.roll(part[64:128], NR - 1, 1), 0.0)
                    total = total + jnp.where(lane >= 2, pltpu.roll(part[128:192], 2, 1), 0.0)
                    total = total + jnp.where(lane < NR - 2, pltpu.roll(part[192:256], NR - 2, 1), 0.0)
                    sums.append(total)
                    lats.append(part[320:384])
                    lons.append(part[384:448])
            shape = (4, LON_DEV) + TILE
            s_ref[pl.ds(i0, 4)] = jnp.concatenate(sums, axis=0).reshape(shape)
            p_lat[pl.ds(i0 + 2, 4)] = jnp.concatenate(lats, axis=0).reshape(shape)
            p_lon[pl.ds(i0, 4)] = jnp.concatenate(lons, axis=0).reshape(shape)

    def shifted(v, n):
        pad = jnp.zeros((abs(n),) + TILE, jnp.float32)
        if n > 0:
            return jnp.concatenate([v[n:], pad], axis=0)
        return jnp.concatenate([pad, v[:n]], axis=0)

    def stencil(st, cur):
        @pl.loop(0, LAT_DEV)
        def _(i):
            si = inv_sin(i)
            q0 = cur[i + 2]
            pl0 = p_lon[i]
            d1 = (p_lat[i] - p_lat[i + 4]) + 8.0 * (p_lat[i + 3] - p_lat[i + 1])
            e1 = (shifted(pl0, -2) - shifted(pl0, 2)) + 8.0 * (shifted(pl0, 1) - shifted(pl0, -1))
            d2 = 16.0 * (cur[i + 1] + cur[i + 3]) - (cur[i] + cur[i + 4])
            e2 = 16.0 * (shifted(q0, -1) + shifted(q0, 1)) - (shifted(q0, -2) + shifted(q0, 2))
            rate = s_ref[i] + ct * (d1 + si * e1) + ct2 * (
                d2 + (si * si) * e2 - (30.0 * (1.0 + si * si)) * q0)
            if st == 0:
                q_mid[i + 2] = q0 + time_step * rate
            else:
                res_ref[i] = 0.5 * q_init[i + 2] + 0.5 * (q0 + time_step * rate)

    def aggregate(st, n):
        got = recv_g[st][n]

        @pl.loop(0, 16)
        def _(k):
            wait_on(got.at[pl.ds(k * 4, 4)], g_recv.at[st, n, k])

        m = nth(n)

        @pl.loop(0, LON_DEV)
        def _(j):
            for g in range(2):
                acc = jnp.zeros(TILE, jnp.float32)
                for t in range(4):
                    acc = acc + smem_w[m, g, t, j] * got[smem_i[m, g, t, j]]
                chunk[st, n, g, j] = acc

        zz = 2 * m + par

        @pl.when(zz != z)
        def _():
            rcopy(chunk.at[st, n], recv_n.at[st, z], n_send.at[st, n], n_recv.at[st, z],
                  (p, y, zz * 4 + w))

        @pl.when(zz == z)
        def _():
            pltpu.make_async_copy(chunk.at[st, n], recv_n.at[st, z], n_recv.at[st, z]).start()

    def sum_over_z(st):
        @pl.when(is_sum)
        def _():
            @pl.loop(0, N_Z)
            def _(zz):
                wait_on(recv_n.at[st, zz], n_recv.at[st, zz])

            for g in range(2):
                acc = recv_n[st, 0, g]
                for zz in range(1, N_Z):
                    acc = acc + recv_n[st, zz, g]
                summed[st, g] = acc
            rcopy(summed.at[st], lat_h.at[st, half], f_send.at[st], lat_recv.at[st, half],
                  (other, dest_lat, z * 4 + wx))

    def forward_ew(st):
        @pl.when(is_agg)
        def _():
            @pl.loop(0, 16)
            def _(k):
                wait_on(recv_e1.at[st, k], e1_recv.at[st, k])

            rcopy(recv_e1.at[st], recv_e2[st].at[z], e2_send.at[st], e2_recv.at[st, z],
                  (other, y, ew_lon))

    def border_ew(st):
        @pl.when(is_ew)
        def _():
            @pl.loop(0, N_Z)
            def _(zz):
                wait_on(recv_e2[st].at[zz], e2_recv.at[st, zz])

            @pl.loop(0, LAT_DEV)
            def _(i):
                for g in range(2):
                    acc = jnp.zeros(TILE, jnp.float32)
                    for t in range(4):
                        idx = smem_ei[g, t, i]
                        acc = acc + smem_ew[g, t, i] * recv_e2[st][idx >> 6, (idx >> 2) & 15, idx & 3]
                    lon_h[st, ew_side, i, g] = acc

    def wait_lon(st):
        @pl.when(b > 0)
        def _():
            wait_on(lon_h.at[st, 0], lon_recv.at[st, 0])

        @pl.when(b < N_LON - 1)
        def _():
            wait_on(lon_h.at[st, 1], lon_recv.at[st, 1])

    def wait_lat(st):
        for side in range(2):
            wait_on(lat_h.at[st, side], lat_recv.at[st, side])

    def target(st):
        if st == 0:
            return q_mid, 2, time_step * ct, time_step * ct2
        return res_ref, 0, 0.5 * time_step * ct, 0.5 * time_step * ct2

    def correct_lat(st):
        dst, off, sc, sc2 = target(st)
        hal = lat_h[st].reshape((48,) + TILE)
        mix_lat = jnp.concatenate(
            [unsplit(mixed(slice(320, 384), hal[16 * t:16 * (t + 1)]), 2) for t in range(3)],
            axis=0).reshape((2, 2, LON_DEV) + TILE)
        hal = hal.reshape((2, 2, LON_DEV) + TILE)
        dst[off] += sc * (mix_lat[0, 0] - 8.0 * mix_lat[0, 1]) + sc2 * (16.0 * hal[0, 1] - hal[0, 0])
        dst[off + 1] += sc * mix_lat[0, 1] - sc2 * hal[0, 1]
        dst[off + 63] += sc * (8.0 * mix_lat[1, 0] - mix_lat[1, 1]) + sc2 * (16.0 * hal[1, 0] - hal[1, 1])
        dst[off + 62] += -sc * mix_lat[1, 0] - sc2 * hal[1, 0]

    def correct_lon(st):
        dst, off, sc, sc2 = target(st)

        @pl.loop(0, LAT_DEV // 4)
        def _(c):
            i0 = c * 4
            west = lon_h[st, 0, pl.ds(i0, 4)].reshape((8,) + TILE)
            east = lon_h[st, 1, pl.ds(i0, 4)].reshape((8,) + TILE)
            both = unsplit(mixed(slice(384, 448), jnp.concatenate([west, east], axis=0)), 2)
            for n in range(4):
                i = i0 + n
                si = inv_sin(i)
                a1 = sc * si
                a2 = sc2 * (si * si)
                w2, w1, pw2, pw1 = west[2 * n], west[2 * n + 1], both[2 * n], both[2 * n + 1]
                e1, e2, pe1, pe2 = east[2 * n], east[2 * n + 1], both[8 + 2 * n], both[9 + 2 * n]
                dst[off + i, 0] += a1 * (pw2 - 8.0 * pw1) + a2 * (16.0 * w1 - w2)
                dst[off + i, 1] += a1 * pw1 - a2 * w1
                dst[off + i, 11] += a1 * (8.0 * pe1 - pe2) + a2 * (16.0 * e1 - e2)
                dst[off + i, 10] += -a1 * pe1 - a2 * e1

    load_state()

    @pl.loop(0, 8)
    def _(t):
        gather_e(0, q_init, t)

    for n in range(4):
        @pl.loop(0, 16)
        def _(k):
            gather_g(0, q_init, n, k)

    prepare_indices()
    build_lhs()
    build_sines()
    pl.semaphore_wait(bar, peers)

    for st, cur in ((0, q_init), (1, q_mid)):
        @pl.loop(0, 8)
        def _(t):
            if st == 1:
                gather_e(st, cur, t)
            start_e(st, t)

        if st == 0:
            send_indices()

        for n in range(4):
            @pl.loop(0, 16)
            def _(r):
                k = turn(r)
                if st == 1:
                    gather_g(st, cur, n, k)
                start_g(st, n, k)

        if st == 0:
            adjust_indices()
        products(cur, 0)
        forward_ew(st)
        products(cur, 1)
        aggregate(st, 0)
        products(cur, 2)
        aggregate(st, 1)
        products(cur, 3)
        aggregate(st, 2)
        aggregate(st, 3)
        halos(st, cur)
        stencil(st, cur)
        sum_over_z(st)
        wait_lon(st)
        border_ew(st)
        correct_lon(st)
        wait_lat(st)
        correct_lat(st)

    @pl.loop(0, LAT_DEV // 8)
    def _(ib):
        i0 = pl.multiple_of(ib * 8, 8)
        for j in range(LON_DEV):
            v = res_ref[pl.ds(i0, 8), j]
            out_ref[:, pl.ds(i0, 8), j * NR:(j + 1) * NR] = jnp.swapaxes(v, 0, 1)

    @pl.when(is_sum)
    def _():
        @pl.loop(0, N_Z)
        def _(zz):
            wait_on(own_i, i_send.at[0, zz])
            wait_on(own_w, i_send.at[1, zz])

    for st in range(2):
        for n in range(4):
            @pl.loop(0, 16)
            def _(k):
                @pl.when(k != me_k)
                def _():
                    wait_on(send_g.at[st, n, k], g_send.at[st, n, k])

        @pl.loop(0, 8)
        def _(t):
            @pl.when(ew_member(t) != me_k)
            def _():
                wait_on(send_e.at[st, t], e1_send.at[st, t])

        for n in range(4):
            @pl.when(2 * nth(n) + par != z)
            def _():
                wait_on(chunk.at[st, n], n_send.at[st, n])

        @pl.when(is_sum)
        def _():
            wait_on(summed.at[st], f_send.at[st])

        @pl.when(is_agg)
        def _():
            wait_on(recv_e1.at[st], e2_send.at[st])

        @pl.when(b < N_LON - 1)
        def _():
            wait_on(lon_h.at[st, 0], lon_send.at[st, 0])

        @pl.when(b > 0)
        def _():
            wait_on(lon_h.at[st, 1], lon_send.at[st, 1])

        @pl.when(y < N_LAT - 1)
        def _():
            wait_on(lat_h.at[st, 0], lat_send.at[st, 0])

        @pl.when(y > 0)
        def _():
            wait_on(lat_h.at[st, 1], lat_send.at[st, 1])


def local(
    fields, coupling, export_index, ghost_ns_index, ghost_ns_frac, ghost_ew_index, ghost_ew_frac
):
    x = fields[0]
    exports = export_index.reshape(-1)
    nsi = jnp.swapaxes(ghost_ns_index[0], 2, 3)
    nsf = jnp.swapaxes(ghost_ns_frac[0], 2, 3)
    ewi = jnp.transpose(ghost_ew_index[0], (0, 2, 3, 1))
    ewf = jnp.transpose(ghost_ew_frac[0], (0, 2, 3, 1))

    vm = pl.BlockSpec(memory_space=pltpu.VMEM)
    sm = pl.BlockSpec(memory_space=pltpu.SMEM)
    hbm = pl.BlockSpec(memory_space=pltpu.HBM)
    V = lambda *shape: pltpu.VMEM(shape + TILE, jnp.float32)
    I = lambda *shape: pltpu.VMEM(shape + TILE, jnp.int32)
    D = lambda *shape: pltpu.SemaphoreType.DMA(shape)
    out = pl.pallas_call(
        kernel,
        out_shape=jax.ShapeDtypeStruct(x.shape, jnp.float32),
        in_specs=[hbm, vm, vm, vm, sm, vm, vm],
        out_specs=vm,
        scratch_shapes=[
            V(LAT_DEV + 4, LON_DEV), V(LAT_DEV + 4, LON_DEV), V(LAT_DEV + 4, LON_DEV),
            V(LAT_DEV, LON_DEV), V(LAT_DEV, LON_DEV), V(LAT_DEV, LON_DEV),
            pltpu.VMEM((448, 192), jnp.bfloat16), pltpu.VMEM((LAT_DEV, NR), jnp.float32),
            V(2, 4, 16, 4)] + [V(64)] * 8 + [V(2, 8, 4), V(2, 16, 4), V(N_Z, 16, 4), V(N_Z, 16, 4),
            V(2, 4, 2, LON_DEV), V(2, N_Z, 2, LON_DEV), V(2, 2, LON_DEV),
            V(2, 2, 2, LON_DEV), V(2, 2, LAT_DEV, 2),
            I(2), V(2), I(4, 2), V(4, 2), I(4, 2), V(4, 2),
            pltpu.SMEM((4, 2) + TILE, jnp.int32), pltpu.SMEM((4, 2) + TILE, jnp.float32),
            I(2), V(2), pltpu.SMEM((2,) + TILE, jnp.int32), pltpu.SMEM((2,) + TILE, jnp.float32),
            D(2, 4, 16), D(2, 4, 16), D(2, 8), D(2, 16), D(2, 8), D(2, 4), D(2, 4), D(2, N_Z), D(2),
            D(2), D(2, N_Z), D(2, 2), D(2, 2), D(2, 2), D(2, 2), D(5),
        ],
        compiler_params=pltpu.CompilerParams(
            collective_id=0, has_side_effects=True, vmem_limit_bytes=49 * 2**20),
        name="two_sections",
    )(x, coupling, nsi, nsf, exports, ewi, ewf)
    return out[None]


def solution(mesh):
    placed = (
        P("panel", None, "lat", "lon"),
        P(),
        P("panel", "lat", "lon", None),
        P("panel", None, None, "lon", None),
        P("panel", None, None, "lon", None),
        P("panel", None, "lat", None, None),
        P("panel", None, "lat", None, None),
    )
    return jax.shard_map(
        local, mesh=mesh, in_specs=placed, out_specs=P("panel", None, "lat", "lon"), check_vma=False
    )
```

```python
import math

import jax
import jax.numpy as jnp
from jax import lax
from jax.experimental import pallas as pl
from jax.experimental.pallas import tpu as pltpu
from jax.sharding import PartitionSpec as P

NR = 128
FIELDS = 8
LAT_DEV = 64
LON_DEV = 12
N_LAT = 4
N_LON = 32
N_Z = 8

time_step = 0.15
viscosity = 0.1
inner_radius = 0.35

MESH = pl.DeviceIdType.MESH
TILE = (FIELDS, NR)


def kernel(
    x_ref, coup_ref, nsi_ref, nsf_ref, exp_ref, ewi_ref, ewf_ref,
    out_ref,
    x_buf, q_init, q_mid, p_lat, p_lon, s_ref, res_ref, lhs_ref, isin_ref,
    send_g, g00, g01, g02, g03, g10, g11, g12, g13, send_e, recv_e1, recv_e20, recv_e21, chunk, recv_n, summed,
    lat_h, lon_h,
    own_i, own_w, got_i, got_w, adj_i, adj_w, smem_i, smem_w,
    adj_ei, adj_ew, smem_ei, smem_ew,
    g_send, g_recv, e1_send, e1_recv, i_send, i_recv, n_send, n_recv, f_send,
    e2_send, e2_recv, lat_send, lat_recv, lon_send, lon_recv, loc_sem,
):
    recv_g = ((g00, g01, g02, g03), (g10, g11, g12, g13))
    recv_e2 = (recv_e20, recv_e21)
    p = lax.axis_index("panel")
    y = lax.axis_index("lat")
    b = lax.axis_index("lon")
    z = b // 4
    w = b % 4
    other = 1 - p
    wx = (w + 2) % 4
    me_k = y * 4 + w
    upper = y >= 2
    half = jnp.where(upper, 1, 0)
    par = jnp.where(upper, 3 - y, y)
    dest_lat = jnp.where(upper, 3, 0)
    is_sum = (z % 2) == par
    is_ns = (y == 0) | (y == 3)
    is_agg = (w == 1) | (w == 2)
    ew_lon = jnp.where(w == 2, 0, N_LON - 1)
    is_ew = (b == 0) | (b == N_LON - 1)
    ew_side = jnp.where(b == 0, 0, 1)
    star = jnp.where(y == 0, z % 2, 3 - z % 2)

    x_copy = pltpu.make_async_copy(x_ref, x_buf, loc_sem.at[0])
    x_copy.start()

    bar = pltpu.get_barrier_semaphore()

    def greet(dev):
        pl.semaphore_signal(bar, inc=1, device_id=dev, device_id_type=MESH)

    @pl.loop(0, 16)
    def _(k):
        @pl.when(k != me_k)
        def _():
            greet((p, k // 4, z * 4 + k % 4))

    @pl.loop(0, 4)
    def _(m):
        greet((other, y, (2 * m + par) * 4 + wx))

    @pl.loop(0, N_Z)
    def _(zz):
        @pl.when(is_sum & (zz != z))
        def _():
            greet((p, y, zz * 4 + w))

        @pl.when(is_ew)
        def _():
            greet((other, y, zz * 4 + wx))

    @pl.when(is_ns)
    def _():
        greet((other, star, z * 4 + wx))

    @pl.when(y > 0)
    def _():
        greet((p, y - 1, b))

    @pl.when(y < N_LAT - 1)
    def _():
        greet((p, y + 1, b))

    @pl.when(b > 0)
    def _():
        greet((p, y, b - 1))

    @pl.when(b < N_LON - 1)
    def _():
        greet((p, y, b + 1))

    one = lambda cond: jnp.where(cond, 1, 0)
    peers = (
        15 + 4 + 8 * one(is_sum) + one(is_agg)
        + one(y > 0) + one(y < N_LAT - 1) + one(b > 0) + one(b < N_LON - 1)
    )

    def rcopy(src, dst, ssem, rsem, dev):
        pltpu.make_async_remote_copy(
            src_ref=src, dst_ref=dst, send_sem=ssem, recv_sem=rsem,
            device_id=dev, device_id_type=MESH,
        ).start()

    def wait_on(ref, sem):
        pltpu.make_async_copy(ref, ref, sem).wait()

    row = lax.broadcasted_iota(jnp.int32, TILE, 0)

    def weights_of(frac):
        a, c = frac[0:1], frac[1:2]
        return jnp.where(row % 2 == 1, a, 1.0 - a) * jnp.where(row % 4 >= 2, c, 1.0 - c)

    def prepare_indices():
        own_i[...] = jnp.zeros(own_i.shape, jnp.int32)
        own_w[...] = jnp.zeros(own_w.shape, jnp.float32)
        adj_ei[...] = jnp.zeros(adj_ei.shape, jnp.int32)
        adj_ew[...] = jnp.zeros(adj_ew.shape, jnp.float32)
        for g in range(2):
            own_i[g, 0:4, 0:LON_DEV] = nsi_ref[half, g]
            own_w[g, 0:2, 0:LON_DEV] = nsf_ref[half, g]
            own_w[g] = weights_of(own_w[g])
            adj_ei[g, 0:4, 0:LAT_DEV] = ewi_ref[ew_side, g]
            adj_ew[g, 0:2, 0:LAT_DEV] = ewf_ref[ew_side, g]
            adj_ew[g] = weights_of(adj_ew[g])
            s = adj_ei[g]
            col = (s >> 2) & (N_LON - 1)
            k = (s >> 7) * 4 + (col & 3)
            adj_ei[g] = (col >> 2) * 64 + k * 4 + (s & 3)
        copies = [pltpu.make_async_copy(adj_ei, smem_ei, loc_sem.at[1]),
                  pltpu.make_async_copy(adj_ew, smem_ew, loc_sem.at[2])]
        for c in copies:
            c.start()
        for c in copies:
            c.wait()

    def send_indices():
        @pl.when(is_sum)
        def _():
            @pl.loop(0, N_Z)
            def _(zz):
                dev = (other, y, zz * 4 + wx)
                rcopy(own_i, got_i.at[z // 2], i_send.at[0, zz], i_recv.at[0, z // 2], dev)
                rcopy(own_w, got_w.at[z // 2], i_send.at[1, zz], i_recv.at[1, z // 2], dev)

    def adjust_indices():
        for m in range(4):
            wait_on(got_i.at[m], i_recv.at[0, m])
            wait_on(got_w.at[m], i_recv.at[1, m])
            s = got_i[m]
            col = (s >> 2) & (N_LON - 1)
            k = (s >> 7) * 4 + (col & 3)
            adj_i[m] = k * 4 + (s & 3)
            adj_w[m] = jnp.where((col >> 2) == z, got_w[m], 0.0)
        copies = [pltpu.make_async_copy(adj_i, smem_i, loc_sem.at[3]),
                  pltpu.make_async_copy(adj_w, smem_w, loc_sem.at[4])]
        for c in copies:
            c.start()
        for c in copies:
            c.wait()

    def load_state():
        zero_rows = jnp.zeros((2, LON_DEV) + TILE, jnp.float32)
        for ref in (q_init, q_mid, p_lat):
            ref[0:2] = zero_rows
            ref[LAT_DEV + 2:LAT_DEV + 4] = zero_rows
        x_copy.wait()

        @pl.loop(0, LAT_DEV // 8)
        def _(ib):
            i0 = pl.multiple_of(ib * 8, 8)
            for j in range(LON_DEV):
                v = x_buf[:, pl.ds(i0, 8), j * NR:(j + 1) * NR]
                q_init[pl.ds(i0 + 2, 8), j] = jnp.swapaxes(v, 0, 1)

    radius = inner_radius + (1.0 - inner_radius) * (
        lax.broadcasted_iota(jnp.int32, TILE, 1).astype(jnp.float32) + 0.5) / NR
    ct = inner_radius / radius
    ct2 = ct * ct * (viscosity / 12.0)

    def build_sines():
        i = y * LAT_DEV + lax.broadcasted_iota(jnp.int32, (LAT_DEV, NR), 0)
        colat = math.pi / 4 + (i.astype(jnp.float32) + 0.5) * (math.pi / 2) / (LAT_DEV * N_LAT)
        isin_ref[...] = 1.0 / jnp.sin(colat)

    def inv_sin(i):
        return isin_ref[pl.ds(i, 1), :]

    def build_lhs():
        r64 = lax.broadcasted_iota(jnp.int32, (64, 8), 0) % 8
        c8 = lax.broadcasted_iota(jnp.int32, (64, 8), 1)
        ex = jnp.where(r64 == c8, 1.0, 0.0).astype(jnp.float32)
        r8 = lax.broadcasted_iota(jnp.int32, (8, 64), 0)
        c64 = lax.broadcasted_iota(jnp.int32, (8, 64), 1) % 8
        ext = jnp.where(r8 == c64, 1.0, 0.0).astype(jnp.float32)
        rr = lax.broadcasted_iota(jnp.int32, (64, 64), 0)
        cc = lax.broadcasted_iota(jnp.int32, (64, 64), 1)
        same = (rr // 8) == (cc // 8)
        eye = jnp.where(rr == cc, 1.0, 0.0).astype(jnp.float32)

        def kron(k):
            tall = jnp.dot(ex, coup_ref[k], precision=lax.Precision.HIGHEST,
                           preferred_element_type=jnp.float32)
            full = jnp.dot(tall, ext, precision=lax.Precision.HIGHEST,
                           preferred_element_type=jnp.float32)
            return jnp.where(same, full, 0.0)

        c0, c1, c2, c3 = kron(0), kron(1), kron(2), kron(3)
        nu = viscosity
        blocks = [
            (8.0 * c0 + 16.0 * nu * eye) / 12.0,
            (-8.0 * c0 + 16.0 * nu * eye) / 12.0,
            (-c0 - nu * eye) / 12.0,
            (c0 - nu * eye) / 12.0,
            c3 - (30.0 * nu / 12.0) * eye,
            c1 / -12.0,
            c2 / -12.0,
        ]
        for n, blk in enumerate(blocks):
            hi = blk.astype(jnp.bfloat16)
            lo = (blk - hi.astype(jnp.float32)).astype(jnp.bfloat16)
            lhs_ref[64 * n:64 * (n + 1), :] = jnp.concatenate([hi, hi, lo], axis=1)

    def split(cols):
        n = cols.shape[0] // 8
        flat = cols.reshape(n * 64, NR)
        wide = jnp.concatenate([flat[64 * t:64 * (t + 1)] for t in range(n)], axis=1)
        hi = wide.astype(jnp.bfloat16)
        lo = (wide - hi.astype(jnp.float32)).astype(jnp.bfloat16)
        return jnp.concatenate([hi, lo, hi], axis=0)

    def mixed(rows, cols):
        return jnp.dot(lhs_ref[rows], split(cols), preferred_element_type=jnp.float32)

    def unsplit(wide, n):
        return jnp.concatenate(
            [wide[:, NR * t:NR * (t + 1)] for t in range(n)], axis=0).reshape((8 * n,) + TILE)

    lane = lax.broadcasted_iota(jnp.int32, (64, NR), 1)

    def column(cur, idx):
        i = (idx * 43691) >> 19
        return cur[i + 2, idx - 12 * i]

    def group_of(k):
        ky = k // 4
        kup = ky >= 2
        kpar = jnp.where(kup, 3 - ky, ky)
        return (jnp.where(kup, 96, 0) + kpar * 4 + (k % 4 + 2) % 4) * 4

    def nth(n):
        return lax.rem(z // 2 + 1 + n, 4)

    def gather_g(st, cur, n, k):
        first = group_of(k) + nth(n) * 32
        for s in range(4):
            send_g[st, n, k, s] = column(cur, exp_ref[first + s])

    def start_g(st, n, k):
        dst = recv_g[st][n].at[pl.ds(me_k * 4, 4)]

        @pl.when(k != me_k)
        def _():
            rcopy(send_g.at[st, n, k], dst, g_send.at[st, n, k],
                  g_recv.at[st, n, me_k], (p, k // 4, z * 4 + k % 4))

        @pl.when(k == me_k)
        def _():
            pltpu.make_async_copy(send_g.at[st, n, k], dst, g_recv.at[st, n, me_k]).start()

    def gather_e(st, cur, t):
        first = ((t // 2) * N_LON + (t % 2) * (N_LON - 1)) * 4
        for s in range(4):
            send_e[st, t, s] = column(cur, exp_ref[first + s])

    def ew_member(t):
        return (t // 2) * 4 + 2 - t % 2

    def start_e(st, t):
        k = ew_member(t)

        @pl.when(k != me_k)
        def _():
            rcopy(send_e.at[st, t], recv_e1.at[st, me_k], e1_send.at[st, t],
                  e1_recv.at[st, me_k], (p, k // 4, z * 4 + k % 4))

        @pl.when(k == me_k)
        def _():
            pltpu.make_async_copy(
                send_e.at[st, t], recv_e1.at[st, me_k], e1_recv.at[st, me_k]).start()

    def turn(n):
        return lax.rem(me_k + 1 + n, 16)

    def halos(st, cur):
        @pl.when(y < N_LAT - 1)
        def _():
            rcopy(cur.at[LAT_DEV:LAT_DEV + 2], lat_h.at[st, 0], lat_send.at[st, 0],
                  lat_recv.at[st, 0], (p, y + 1, b))

        @pl.when(y > 0)
        def _():
            rcopy(cur.at[2:4], lat_h.at[st, 1], lat_send.at[st, 1],
                  lat_recv.at[st, 1], (p, y - 1, b))

        @pl.when(b < N_LON - 1)
        def _():
            rcopy(cur.at[2:LAT_DEV + 2, 10:12], lon_h.at[st, 0], lon_send.at[st, 0],
                  lon_recv.at[st, 0], (p, y, b + 1))

        @pl.when(b > 0)
        def _():
            rcopy(cur.at[2:LAT_DEV + 2, 0:2], lon_h.at[st, 1], lon_send.at[st, 1],
                  lon_recv.at[st, 1], (p, y, b - 1))

    def products(cur, quarter):
        @pl.loop(quarter * (LAT_DEV // 16), (quarter + 1) * (LAT_DEV // 16))
        def _(c):
            i0 = c * 4
            cols = cur[pl.ds(i0 + 2, 4)].reshape((48,) + TILE)
            sums, lats, lons = [], [], []
            for t in range(3):
                wide = mixed(slice(0, 448), cols[16 * t:16 * (t + 1)])
                for h in range(2):
                    part = wide[:, NR * h:NR * (h + 1)]
                    total = part[256:320]
                    total = total + jnp.where(lane >= 1, pltpu.roll(part[0:64], 1, 1), 0.0)
                    total = total + jnp.where(lane < NR - 1, pltpu.roll(part[64:128], NR - 1, 1), 0.0)
                    total = total + jnp.where(lane >= 2, pltpu.roll(part[128:192], 2, 1), 0.0)
                    total = total + jnp.where(lane < NR - 2, pltpu.roll(part[192:256], NR - 2, 1), 0.0)
                    sums.append(total)
                    lats.append(part[320:384])
                    lons.append(part[384:448])
            shape = (4, LON_DEV) + TILE
            s_ref[pl.ds(i0, 4)] = jnp.concatenate(sums, axis=0).reshape(shape)
            p_lat[pl.ds(i0 + 2, 4)] = jnp.concatenate(lats, axis=0).reshape(shape)
            p_lon[pl.ds(i0, 4)] = jnp.concatenate(lons, axis=0).reshape(shape)

    def shifted(v, n):
        pad = jnp.zeros((abs(n),) + TILE, jnp.float32)
        if n > 0:
            return jnp.concatenate([v[n:], pad], axis=0)
        return jnp.concatenate([pad, v[:n]], axis=0)

    def stencil(st, cur):
        @pl.loop(0, LAT_DEV)
        def _(i):
            si = inv_sin(i)
            q0 = cur[i + 2]
            pl0 = p_lon[i]
            d1 = (p_lat[i] - p_lat[i + 4]) + 8.0 * (p_lat[i + 3] - p_lat[i + 1])
            e1 = (shifted(pl0, -2) - shifted(pl0, 2)) + 8.0 * (shifted(pl0, 1) - shifted(pl0, -1))
            d2 = 16.0 * (cur[i + 1] + cur[i + 3]) - (cur[i] + cur[i + 4])
            e2 = 16.0 * (shifted(q0, -1) + shifted(q0, 1)) - (shifted(q0, -2) + shifted(q0, 2))
            rate = s_ref[i] + ct * (d1 + si * e1) + ct2 * (
                d2 + (si * si) * e2 - (30.0 * (1.0 + si * si)) * q0)
            if st == 0:
                q_mid[i + 2] = q0 + time_step * rate
            else:
                res_ref[i] = 0.5 * q_init[i + 2] + 0.5 * (q0 + time_step * rate)

    def aggregate(st, n):
        got = recv_g[st][n]

        @pl.loop(0, 16)
        def _(k):
            wait_on(got.at[pl.ds(k * 4, 4)], g_recv.at[st, n, k])

        m = nth(n)

        @pl.loop(0, LON_DEV)
        def _(j):
            for g in range(2):
                acc = jnp.zeros(TILE, jnp.float32)
                for t in range(4):
                    acc = acc + smem_w[m, g, t, j] * got[smem_i[m, g, t, j]]
                chunk[st, n, g, j] = acc

        zz = 2 * m + par

        @pl.when(zz != z)
        def _():
            rcopy(chunk.at[st, n], recv_n.at[st, z], n_send.at[st, n], n_recv.at[st, z],
                  (p, y, zz * 4 + w))

        @pl.when(zz == z)
        def _():
            pltpu.make_async_copy(chunk.at[st, n], recv_n.at[st, z], n_recv.at[st, z]).start()

    def sum_over_z(st):
        @pl.when(is_sum)
        def _():
            @pl.loop(0, N_Z)
            def _(zz):
                wait_on(recv_n.at[st, zz], n_recv.at[st, zz])

            for g in range(2):
                acc = recv_n[st, 0, g]
                for zz in range(1, N_Z):
                    acc = acc + recv_n[st, zz, g]
                summed[st, g] = acc
            rcopy(summed.at[st], lat_h.at[st, half], f_send.at[st], lat_recv.at[st, half],
                  (other, dest_lat, z * 4 + wx))

    def forward_ew(st):
        @pl.when(is_agg)
        def _():
            @pl.loop(0, 16)
            def _(k):
                wait_on(recv_e1.at[st, k], e1_recv.at[st, k])

            rcopy(recv_e1.at[st], recv_e2[st].at[z], e2_send.at[st], e2_recv.at[st, z],
                  (other, y, ew_lon))

    def border_ew(st):
        @pl.when(is_ew)
        def _():
            @pl.loop(0, N_Z)
            def _(zz):
                wait_on(recv_e2[st].at[zz], e2_recv.at[st, zz])

            @pl.loop(0, LAT_DEV)
            def _(i):
                for g in range(2):
                    acc = jnp.zeros(TILE, jnp.float32)
                    for t in range(4):
                        idx = smem_ei[g, t, i]
                        acc = acc + smem_ew[g, t, i] * recv_e2[st][idx >> 6, (idx >> 2) & 15, idx & 3]
                    lon_h[st, ew_side, i, g] = acc

    def wait_lon(st):
        @pl.when(b > 0)
        def _():
            wait_on(lon_h.at[st, 0], lon_recv.at[st, 0])

        @pl.when(b < N_LON - 1)
        def _():
            wait_on(lon_h.at[st, 1], lon_recv.at[st, 1])

    def wait_lat(st):
        for side in range(2):
            wait_on(lat_h.at[st, side], lat_recv.at[st, side])

    def target(st):
        if st == 0:
            return q_mid, 2, time_step * ct, time_step * ct2
        return res_ref, 0, 0.5 * time_step * ct, 0.5 * time_step * ct2

    def correct_lat(st):
        dst, off, sc, sc2 = target(st)
        hal = lat_h[st].reshape((48,) + TILE)
        mix_lat = jnp.concatenate(
            [unsplit(mixed(slice(320, 384), hal[16 * t:16 * (t + 1)]), 2) for t in range(3)],
            axis=0).reshape((2, 2, LON_DEV) + TILE)
        hal = hal.reshape((2, 2, LON_DEV) + TILE)
        dst[off] += sc * (mix_lat[0, 0] - 8.0 * mix_lat[0, 1]) + sc2 * (16.0 * hal[0, 1] - hal[0, 0])
        dst[off + 1] += sc * mix_lat[0, 1] - sc2 * hal[0, 1]
        dst[off + 63] += sc * (8.0 * mix_lat[1, 0] - mix_lat[1, 1]) + sc2 * (16.0 * hal[1, 0] - hal[1, 1])
        dst[off + 62] += -sc * mix_lat[1, 0] - sc2 * hal[1, 0]

    def correct_lon(st):
        dst, off, sc, sc2 = target(st)

        @pl.loop(0, LAT_DEV // 4)
        def _(c):
            i0 = c * 4
            west = lon_h[st, 0, pl.ds(i0, 4)].reshape((8,) + TILE)
            east = lon_h[st, 1, pl.ds(i0, 4)].reshape((8,) + TILE)
            both = unsplit(mixed(slice(384, 448), jnp.concatenate([west, east], axis=0)), 2)
            for n in range(4):
                i = i0 + n
                si = inv_sin(i)
                a1 = sc * si
                a2 = sc2 * (si * si)
                w2, w1, pw2, pw1 = west[2 * n], west[2 * n + 1], both[2 * n], both[2 * n + 1]
                e1, e2, pe1, pe2 = east[2 * n], east[2 * n + 1], both[8 + 2 * n], both[9 + 2 * n]
                dst[off + i, 0] += a1 * (pw2 - 8.0 * pw1) + a2 * (16.0 * w1 - w2)
                dst[off + i, 1] += a1 * pw1 - a2 * w1
                dst[off + i, 11] += a1 * (8.0 * pe1 - pe2) + a2 * (16.0 * e1 - e2)
                dst[off + i, 10] += -a1 * pe1 - a2 * e1

    load_state()

    @pl.loop(0, 8)
    def _(t):
        gather_e(0, q_init, t)

    for n in range(4):
        @pl.loop(0, 16)
        def _(k):
            gather_g(0, q_init, n, k)

    prepare_indices()
    build_lhs()
    build_sines()
    pl.semaphore_wait(bar, peers)

    for st, cur in ((0, q_init), (1, q_mid)):
        @pl.loop(0, 8)
        def _(t):
            if st == 1:
                gather_e(st, cur, t)
            start_e(st, t)

        if st == 0:
            send_indices()

        for n in range(4):
            @pl.loop(0, 16)
            def _(r):
                k = turn(r)
                if st == 1:
                    gather_g(st, cur, n, k)
                start_g(st, n, k)

        forward_ew(st)
        if st == 0:
            adjust_indices()
        products(cur, 0)
        products(cur, 1)
        aggregate(st, 0)
        products(cur, 2)
        aggregate(st, 1)
        products(cur, 3)
        aggregate(st, 2)
        aggregate(st, 3)
        halos(st, cur)
        stencil(st, cur)
        sum_over_z(st)
        wait_lon(st)
        border_ew(st)
        correct_lon(st)
        wait_lat(st)
        correct_lat(st)

    @pl.loop(0, LAT_DEV // 8)
    def _(ib):
        i0 = pl.multiple_of(ib * 8, 8)
        for j in range(LON_DEV):
            v = res_ref[pl.ds(i0, 8), j]
            out_ref[:, pl.ds(i0, 8), j * NR:(j + 1) * NR] = jnp.swapaxes(v, 0, 1)

    @pl.when(is_sum)
    def _():
        @pl.loop(0, N_Z)
        def _(zz):
            wait_on(own_i, i_send.at[0, zz])
            wait_on(own_w, i_send.at[1, zz])

    for st in range(2):
        for n in range(4):
            @pl.loop(0, 16)
            def _(k):
                @pl.when(k != me_k)
                def _():
                    wait_on(send_g.at[st, n, k], g_send.at[st, n, k])

        @pl.loop(0, 8)
        def _(t):
            @pl.when(ew_member(t) != me_k)
            def _():
                wait_on(send_e.at[st, t], e1_send.at[st, t])

        for n in range(4):
            @pl.when(2 * nth(n) + par != z)
            def _():
                wait_on(chunk.at[st, n], n_send.at[st, n])

        @pl.when(is_sum)
        def _():
            wait_on(summed.at[st], f_send.at[st])

        @pl.when(is_agg)
        def _():
            wait_on(recv_e1.at[st], e2_send.at[st])

        @pl.when(b < N_LON - 1)
        def _():
            wait_on(lon_h.at[st, 0], lon_send.at[st, 0])

        @pl.when(b > 0)
        def _():
            wait_on(lon_h.at[st, 1], lon_send.at[st, 1])

        @pl.when(y < N_LAT - 1)
        def _():
            wait_on(lat_h.at[st, 0], lat_send.at[st, 0])

        @pl.when(y > 0)
        def _():
            wait_on(lat_h.at[st, 1], lat_send.at[st, 1])


def local(
    fields, coupling, export_index, ghost_ns_index, ghost_ns_frac, ghost_ew_index, ghost_ew_frac
):
    x = fields[0]
    exports = export_index.reshape(-1)
    nsi = jnp.swapaxes(ghost_ns_index[0], 2, 3)
    nsf = jnp.swapaxes(ghost_ns_frac[0], 2, 3)
    ewi = jnp.transpose(ghost_ew_index[0], (0, 2, 3, 1))
    ewf = jnp.transpose(ghost_ew_frac[0], (0, 2, 3, 1))

    vm = pl.BlockSpec(memory_space=pltpu.VMEM)
    sm = pl.BlockSpec(memory_space=pltpu.SMEM)
    hbm = pl.BlockSpec(memory_space=pl.ANY)
    V = lambda *shape: pltpu.VMEM(shape + TILE, jnp.float32)
    I = lambda *shape: pltpu.VMEM(shape + TILE, jnp.int32)
    D = lambda *shape: pltpu.SemaphoreType.DMA(shape)
    out = pl.pallas_call(
        kernel,
        out_shape=jax.ShapeDtypeStruct(x.shape, jnp.float32),
        in_specs=[hbm, vm, vm, vm, sm, vm, vm],
        out_specs=vm,
        scratch_shapes=[
            pltpu.VMEM(x.shape, jnp.float32),
            V(LAT_DEV + 4, LON_DEV), V(LAT_DEV + 4, LON_DEV), V(LAT_DEV + 4, LON_DEV),
            V(LAT_DEV, LON_DEV), V(LAT_DEV, LON_DEV), V(LAT_DEV, LON_DEV),
            pltpu.VMEM((448, 192), jnp.bfloat16), pltpu.VMEM((LAT_DEV, NR), jnp.float32),
            V(2, 4, 16, 4)] + [V(64)] * 8 + [V(2, 8, 4), V(2, 16, 4), V(N_Z, 16, 4), V(N_Z, 16, 4),
            V(2, 4, 2, LON_DEV), V(2, N_Z, 2, LON_DEV), V(2, 2, LON_DEV),
            V(2, 2, 2, LON_DEV), V(2, 2, LAT_DEV, 2),
            I(2), V(2), I(4, 2), V(4, 2), I(4, 2), V(4, 2),
            pltpu.SMEM((4, 2) + TILE, jnp.int32), pltpu.SMEM((4, 2) + TILE, jnp.float32),
            I(2), V(2), pltpu.SMEM((2,) + TILE, jnp.int32), pltpu.SMEM((2,) + TILE, jnp.float32),
            D(2, 4, 16), D(2, 4, 16), D(2, 8), D(2, 16), D(2, 8), D(2, 4), D(2, 4), D(2, N_Z), D(2),
            D(2), D(2, N_Z), D(2, 2), D(2, 2), D(2, 2), D(2, 2), D(5),
        ],
        compiler_params=pltpu.CompilerParams(
            collective_id=0, has_side_effects=True, vmem_limit_bytes=60 * 2**20),
        name="two_sections",
    )(x, coupling, nsi, nsf, exports, ewi, ewf)
    return out[None]


def solution(mesh):
    placed = (
        P("panel", None, "lat", "lon"),
        P(),
        P("panel", "lat", "lon", None),
        P("panel", None, None, "lon", None),
        P("panel", None, None, "lon", None),
        P("panel", None, "lat", None, None),
        P("panel", None, "lat", None, None),
    )
    return jax.shard_map(
        local, mesh=mesh, in_specs=placed, out_specs=P("panel", None, "lat", "lon"), check_vma=False
    )
```

```python
import math

import jax
import jax.numpy as jnp
from jax import lax
from jax.experimental import pallas as pl
from jax.experimental.pallas import tpu as pltpu
from jax.sharding import PartitionSpec as P

NR = 128
FIELDS = 8
LAT_DEV = 64
LON_DEV = 12
N_LAT = 4
N_LON = 32
N_Z = 8

time_step = 0.15
viscosity = 0.1
inner_radius = 0.35

MESH = pl.DeviceIdType.MESH
TILE = (FIELDS, NR)


def kernel(
    x_ref, coup_ref, nsi_ref, nsf_ref, exp_ref, ewi_ref, ewf_ref,
    out_ref,
    x_buf, q_init, q_mid, p_lat, p_lon, s_ref, res_ref, lhs_ref, isin_ref,
    send_g, g00, g01, g02, g03, g10, g11, g12, g13, send_e, recv_e1, recv_e20, recv_e21, chunk, recv_n, summed,
    lat_h, lon_h,
    own_i, own_w, got_i, got_w, adj_i, adj_w, smem_i, smem_w,
    adj_ei, adj_ew, smem_ei, smem_ew,
    g_send, g_recv, e1_send, e1_recv, i_send, i_recv, n_send, n_recv, f_send,
    e2_send, e2_recv, lat_send, lat_recv, lon_send, lon_recv, loc_sem,
):
    recv_g = ((g00, g01, g02, g03), (g10, g11, g12, g13))
    recv_e2 = (recv_e20, recv_e21)
    p = lax.axis_index("panel")
    y = lax.axis_index("lat")
    b = lax.axis_index("lon")
    z = b // 4
    w = b % 4
    other = 1 - p
    wx = (w + 2) % 4
    me_k = y * 4 + w
    upper = y >= 2
    half = jnp.where(upper, 1, 0)
    par = jnp.where(upper, 3 - y, y)
    dest_lat = jnp.where(upper, 3, 0)
    is_sum = (z % 2) == par
    is_ns = (y == 0) | (y == 3)
    is_agg = (w == 1) | (w == 2)
    ew_lon = jnp.where(w == 2, 0, N_LON - 1)
    is_ew = (b == 0) | (b == N_LON - 1)
    ew_side = jnp.where(b == 0, 0, 1)
    star = jnp.where(y == 0, z % 2, 3 - z % 2)

    x_copy = pltpu.make_async_copy(x_ref, x_buf, loc_sem.at[0])
    x_copy.start()

    bar = pltpu.get_barrier_semaphore()

    def greet(dev):
        pl.semaphore_signal(bar, inc=1, device_id=dev, device_id_type=MESH)

    @pl.loop(0, 16)
    def _(k):
        @pl.when(k != me_k)
        def _():
            greet((p, k // 4, z * 4 + k % 4))

    @pl.loop(0, 4)
    def _(m):
        greet((other, y, (2 * m + par) * 4 + wx))

    @pl.loop(0, N_Z)
    def _(zz):
        @pl.when(is_sum & (zz != z))
        def _():
            greet((p, y, zz * 4 + w))

        @pl.when(is_ew)
        def _():
            greet((other, y, zz * 4 + wx))

    @pl.when(is_ns)
    def _():
        greet((other, star, z * 4 + wx))

    @pl.when(y > 0)
    def _():
        greet((p, y - 1, b))

    @pl.when(y < N_LAT - 1)
    def _():
        greet((p, y + 1, b))

    @pl.when(b > 0)
    def _():
        greet((p, y, b - 1))

    @pl.when(b < N_LON - 1)
    def _():
        greet((p, y, b + 1))

    one = lambda cond: jnp.where(cond, 1, 0)
    peers = (
        15 + 4 + 8 * one(is_sum) + one(is_agg)
        + one(y > 0) + one(y < N_LAT - 1) + one(b > 0) + one(b < N_LON - 1)
    )

    def rcopy(src, dst, ssem, rsem, dev):
        pltpu.make_async_remote_copy(
            src_ref=src, dst_ref=dst, send_sem=ssem, recv_sem=rsem,
            device_id=dev, device_id_type=MESH,
        ).start()

    def wait_on(ref, sem):
        pltpu.make_async_copy(ref, ref, sem).wait()

    row = lax.broadcasted_iota(jnp.int32, TILE, 0)

    def weights_of(frac):
        a, c = frac[0:1], frac[1:2]
        return jnp.where(row % 2 == 1, a, 1.0 - a) * jnp.where(row % 4 >= 2, c, 1.0 - c)

    def prepare_indices():
        own_i[...] = jnp.zeros(own_i.shape, jnp.int32)
        own_w[...] = jnp.zeros(own_w.shape, jnp.float32)
        adj_ei[...] = jnp.zeros(adj_ei.shape, jnp.int32)
        adj_ew[...] = jnp.zeros(adj_ew.shape, jnp.float32)
        for g in range(2):
            own_i[g, 0:4, 0:LON_DEV] = nsi_ref[half, g]
            own_w[g, 0:2, 0:LON_DEV] = nsf_ref[half, g]
            own_w[g] = weights_of(own_w[g])
            adj_ei[g, 0:4, 0:LAT_DEV] = ewi_ref[ew_side, g]
            adj_ew[g, 0:2, 0:LAT_DEV] = ewf_ref[ew_side, g]
            adj_ew[g] = weights_of(adj_ew[g])
            s = adj_ei[g]
            col = (s >> 2) & (N_LON - 1)
            k = (s >> 7) * 4 + (col & 3)
            adj_ei[g] = (col >> 2) * 64 + k * 4 + (s & 3)
        copies = [pltpu.make_async_copy(adj_ei, smem_ei, loc_sem.at[1]),
                  pltpu.make_async_copy(adj_ew, smem_ew, loc_sem.at[2])]
        for c in copies:
            c.start()
        for c in copies:
            c.wait()

    def send_indices():
        @pl.when(is_sum)
        def _():
            @pl.loop(0, N_Z)
            def _(zz):
                dev = (other, y, zz * 4 + wx)
                rcopy(own_i, got_i.at[z // 2], i_send.at[0, zz], i_recv.at[0, z // 2], dev)
                rcopy(own_w, got_w.at[z // 2], i_send.at[1, zz], i_recv.at[1, z // 2], dev)

    def adjust_indices():
        for m in range(4):
            wait_on(got_i.at[m], i_recv.at[0, m])
            wait_on(got_w.at[m], i_recv.at[1, m])
            s = got_i[m]
            col = (s >> 2) & (N_LON - 1)
            k = (s >> 7) * 4 + (col & 3)
            adj_i[m] = k * 4 + (s & 3)
            adj_w[m] = jnp.where((col >> 2) == z, got_w[m], 0.0)
        copies = [pltpu.make_async_copy(adj_i, smem_i, loc_sem.at[3]),
                  pltpu.make_async_copy(adj_w, smem_w, loc_sem.at[4])]
        for c in copies:
            c.start()
        for c in copies:
            c.wait()

    def load_state():
        zero_rows = jnp.zeros((2, LON_DEV) + TILE, jnp.float32)
        for ref in (q_init, q_mid, p_lat):
            ref[0:2] = zero_rows
            ref[LAT_DEV + 2:LAT_DEV + 4] = zero_rows
        x_copy.wait()

        @pl.loop(0, LAT_DEV // 8)
        def _(ib):
            i0 = pl.multiple_of(ib * 8, 8)
            for j in range(LON_DEV):
                v = x_buf[:, pl.ds(i0, 8), j * NR:(j + 1) * NR]
                q_init[pl.ds(i0 + 2, 8), j] = jnp.swapaxes(v, 0, 1)

    radius = inner_radius + (1.0 - inner_radius) * (
        lax.broadcasted_iota(jnp.int32, TILE, 1).astype(jnp.float32) + 0.5) / NR
    ct = inner_radius / radius
    ct2 = ct * ct * (viscosity / 12.0)

    def build_sines():
        i = y * LAT_DEV + lax.broadcasted_iota(jnp.int32, (LAT_DEV, NR), 0)
        colat = math.pi / 4 + (i.astype(jnp.float32) + 0.5) * (math.pi / 2) / (LAT_DEV * N_LAT)
        isin_ref[...] = 1.0 / jnp.sin(colat)

    def inv_sin(i):
        return isin_ref[pl.ds(i, 1), :]

    def build_lhs():
        r64 = lax.broadcasted_iota(jnp.int32, (64, 8), 0) % 8
        c8 = lax.broadcasted_iota(jnp.int32, (64, 8), 1)
        ex = jnp.where(r64 == c8, 1.0, 0.0).astype(jnp.float32)
        r8 = lax.broadcasted_iota(jnp.int32, (8, 64), 0)
        c64 = lax.broadcasted_iota(jnp.int32, (8, 64), 1) % 8
        ext = jnp.where(r8 == c64, 1.0, 0.0).astype(jnp.float32)
        rr = lax.broadcasted_iota(jnp.int32, (64, 64), 0)
        cc = lax.broadcasted_iota(jnp.int32, (64, 64), 1)
        same = (rr // 8) == (cc // 8)
        eye = jnp.where(rr == cc, 1.0, 0.0).astype(jnp.float32)

        def kron(k):
            tall = jnp.dot(ex, coup_ref[k], precision=lax.Precision.HIGHEST,
                           preferred_element_type=jnp.float32)
            full = jnp.dot(tall, ext, precision=lax.Precision.HIGHEST,
                           preferred_element_type=jnp.float32)
            return jnp.where(same, full, 0.0)

        c0, c1, c2, c3 = kron(0), kron(1), kron(2), kron(3)
        nu = viscosity
        blocks = [
            (8.0 * c0 + 16.0 * nu * eye) / 12.0,
            (-8.0 * c0 + 16.0 * nu * eye) / 12.0,
            (-c0 - nu * eye) / 12.0,
            (c0 - nu * eye) / 12.0,
            c3 - (30.0 * nu / 12.0) * eye,
            c1 / -12.0,
            c2 / -12.0,
        ]
        for n, blk in enumerate(blocks):
            hi = blk.astype(jnp.bfloat16)
            lo = (blk - hi.astype(jnp.float32)).astype(jnp.bfloat16)
            lhs_ref[64 * n:64 * (n + 1), :] = jnp.concatenate([hi, hi, lo], axis=1)

    def split(cols):
        n = cols.shape[0] // 8
        flat = cols.reshape(n * 64, NR)
        wide = jnp.concatenate([flat[64 * t:64 * (t + 1)] for t in range(n)], axis=1)
        hi = wide.astype(jnp.bfloat16)
        lo = (wide - hi.astype(jnp.float32)).astype(jnp.bfloat16)
        return jnp.concatenate([hi, lo, hi], axis=0)

    def mixed(rows, cols):
        return jnp.dot(lhs_ref[rows], split(cols), preferred_element_type=jnp.float32)

    def unsplit(wide, n):
        return jnp.concatenate(
            [wide[:, NR * t:NR * (t + 1)] for t in range(n)], axis=0).reshape((8 * n,) + TILE)

    lane = lax.broadcasted_iota(jnp.int32, (64, NR), 1)

    def column(cur, idx):
        i = (idx * 43691) >> 19
        return cur[i + 2, idx - 12 * i]

    def group_of(k):
        ky = k // 4
        kup = ky >= 2
        kpar = jnp.where(kup, 3 - ky, ky)
        return (jnp.where(kup, 96, 0) + kpar * 4 + (k % 4 + 2) % 4) * 4

    def nth(n):
        return lax.rem(z // 2 + 1 + n, 4)

    def gather_g(st, cur, n, k):
        first = group_of(k) + nth(n) * 32
        for s in range(4):
            send_g[st, n, k, s] = column(cur, exp_ref[first + s])

    def start_g(st, n, k):
        dst = recv_g[st][n].at[pl.ds(me_k * 4, 4)]

        @pl.when(k != me_k)
        def _():
            rcopy(send_g.at[st, n, k], dst, g_send.at[st, n, k],
                  g_recv.at[st, n, me_k], (p, k // 4, z * 4 + k % 4))

        @pl.when(k == me_k)
        def _():
            pltpu.make_async_copy(send_g.at[st, n, k], dst, g_recv.at[st, n, me_k]).start()

    def gather_e(st, cur, t):
        first = ((t // 2) * N_LON + (t % 2) * (N_LON - 1)) * 4
        for s in range(4):
            send_e[st, t, s] = column(cur, exp_ref[first + s])

    def ew_member(t):
        return (t // 2) * 4 + 2 - t % 2

    def start_e(st, t):
        k = ew_member(t)

        @pl.when(k != me_k)
        def _():
            rcopy(send_e.at[st, t], recv_e1.at[st, me_k], e1_send.at[st, t],
                  e1_recv.at[st, me_k], (p, k // 4, z * 4 + k % 4))

        @pl.when(k == me_k)
        def _():
            pltpu.make_async_copy(
                send_e.at[st, t], recv_e1.at[st, me_k], e1_recv.at[st, me_k]).start()

    def turn(n):
        return lax.rem(me_k + 1 + n, 16)

    def halos(st, cur):
        @pl.when(y < N_LAT - 1)
        def _():
            rcopy(cur.at[LAT_DEV:LAT_DEV + 2], lat_h.at[st, 0], lat_send.at[st, 0],
                  lat_recv.at[st, 0], (p, y + 1, b))

        @pl.when(y > 0)
        def _():
            rcopy(cur.at[2:4], lat_h.at[st, 1], lat_send.at[st, 1],
                  lat_recv.at[st, 1], (p, y - 1, b))

        @pl.when(b < N_LON - 1)
        def _():
            rcopy(cur.at[2:LAT_DEV + 2, 10:12], lon_h.at[st, 0], lon_send.at[st, 0],
                  lon_recv.at[st, 0], (p, y, b + 1))

        @pl.when(b > 0)
        def _():
            rcopy(cur.at[2:LAT_DEV + 2, 0:2], lon_h.at[st, 1], lon_send.at[st, 1],
                  lon_recv.at[st, 1], (p, y, b - 1))

    def products(cur, quarter):
        @pl.loop(quarter * (LAT_DEV // 16), (quarter + 1) * (LAT_DEV // 16))
        def _(c):
            i0 = c * 4
            cols = cur[pl.ds(i0 + 2, 4)].reshape((48,) + TILE)
            sums, lats, lons = [], [], []
            for t in range(3):
                wide = mixed(slice(0, 448), cols[16 * t:16 * (t + 1)])
                for h in range(2):
                    part = wide[:, NR * h:NR * (h + 1)]
                    total = part[256:320]
                    total = total + jnp.where(lane >= 1, pltpu.roll(part[0:64], 1, 1), 0.0)
                    total = total + jnp.where(lane < NR - 1, pltpu.roll(part[64:128], NR - 1, 1), 0.0)
                    total = total + jnp.where(lane >= 2, pltpu.roll(part[128:192], 2, 1), 0.0)
                    total = total + jnp.where(lane < NR - 2, pltpu.roll(part[192:256], NR - 2, 1), 0.0)
                    sums.append(total)
                    lats.append(part[320:384])
                    lons.append(part[384:448])
            shape = (4, LON_DEV) + TILE
            s_ref[pl.ds(i0, 4)] = jnp.concatenate(sums, axis=0).reshape(shape)
            p_lat[pl.ds(i0 + 2, 4)] = jnp.concatenate(lats, axis=0).reshape(shape)
            p_lon[pl.ds(i0, 4)] = jnp.concatenate(lons, axis=0).reshape(shape)

    def shifted(v, n):
        pad = jnp.zeros((abs(n),) + TILE, jnp.float32)
        if n > 0:
            return jnp.concatenate([v[n:], pad], axis=0)
        return jnp.concatenate([pad, v[:n]], axis=0)

    def stencil(st, cur):
        @pl.loop(0, LAT_DEV)
        def _(i):
            si = inv_sin(i)
            q0 = cur[i + 2]
            pl0 = p_lon[i]
            d1 = (p_lat[i] - p_lat[i + 4]) + 8.0 * (p_lat[i + 3] - p_lat[i + 1])
            e1 = (shifted(pl0, -2) - shifted(pl0, 2)) + 8.0 * (shifted(pl0, 1) - shifted(pl0, -1))
            d2 = 16.0 * (cur[i + 1] + cur[i + 3]) - (cur[i] + cur[i + 4])
            e2 = 16.0 * (shifted(q0, -1) + shifted(q0, 1)) - (shifted(q0, -2) + shifted(q0, 2))
            rate = s_ref[i] + ct * (d1 + si * e1) + ct2 * (
                d2 + (si * si) * e2 - (30.0 * (1.0 + si * si)) * q0)
            if st == 0:
                q_mid[i + 2] = q0 + time_step * rate
            else:
                res_ref[i] = 0.5 * q_init[i + 2] + 0.5 * (q0 + time_step * rate)

    def aggregate(st, n):
        got = recv_g[st][n]

        @pl.loop(0, 16)
        def _(k):
            wait_on(got.at[pl.ds(k * 4, 4)], g_recv.at[st, n, k])

        m = nth(n)

        @pl.loop(0, LON_DEV, unroll=4)
        def _(j):
            for g in range(2):
                acc = jnp.zeros(TILE, jnp.float32)
                for t in range(4):
                    acc = acc + smem_w[m, g, t, j] * got[smem_i[m, g, t, j]]
                chunk[st, n, g, j] = acc

        zz = 2 * m + par

        @pl.when(zz != z)
        def _():
            rcopy(chunk.at[st, n], recv_n.at[st, z], n_send.at[st, n], n_recv.at[st, z],
                  (p, y, zz * 4 + w))

        @pl.when(zz == z)
        def _():
            pltpu.make_async_copy(chunk.at[st, n], recv_n.at[st, z], n_recv.at[st, z]).start()

    def sum_over_z(st):
        @pl.when(is_sum)
        def _():
            @pl.loop(0, N_Z)
            def _(zz):
                wait_on(recv_n.at[st, zz], n_recv.at[st, zz])

            for g in range(2):
                acc = recv_n[st, 0, g]
                for zz in range(1, N_Z):
                    acc = acc + recv_n[st, zz, g]
                summed[st, g] = acc
            rcopy(summed.at[st], lat_h.at[st, half], f_send.at[st], lat_recv.at[st, half],
                  (other, dest_lat, z * 4 + wx))

    def forward_ew(st):
        @pl.when(is_agg)
        def _():
            @pl.loop(0, 16)
            def _(k):
                wait_on(recv_e1.at[st, k], e1_recv.at[st, k])

            rcopy(recv_e1.at[st], recv_e2[st].at[z], e2_send.at[st], e2_recv.at[st, z],
                  (other, y, ew_lon))

    def border_ew(st):
        @pl.when(is_ew)
        def _():
            @pl.loop(0, N_Z)
            def _(zz):
                wait_on(recv_e2[st].at[zz], e2_recv.at[st, zz])

            @pl.loop(0, LAT_DEV, unroll=4)
            def _(i):
                for g in range(2):
                    acc = jnp.zeros(TILE, jnp.float32)
                    for t in range(4):
                        idx = smem_ei[g, t, i]
                        acc = acc + smem_ew[g, t, i] * recv_e2[st][idx >> 6, (idx >> 2) & 15, idx & 3]
                    lon_h[st, ew_side, i, g] = acc

    def wait_lon(st):
        @pl.when(b > 0)
        def _():
            wait_on(lon_h.at[st, 0], lon_recv.at[st, 0])

        @pl.when(b < N_LON - 1)
        def _():
            wait_on(lon_h.at[st, 1], lon_recv.at[st, 1])

    def wait_lat(st):
        for side in range(2):
            wait_on(lat_h.at[st, side], lat_recv.at[st, side])

    def target(st):
        if st == 0:
            return q_mid, 2, time_step * ct, time_step * ct2
        return res_ref, 0, 0.5 * time_step * ct, 0.5 * time_step * ct2

    def correct_lat(st):
        dst, off, sc, sc2 = target(st)
        hal = lat_h[st].reshape((48,) + TILE)
        mix_lat = jnp.concatenate(
            [unsplit(mixed(slice(320, 384), hal[16 * t:16 * (t + 1)]), 2) for t in range(3)],
            axis=0).reshape((2, 2, LON_DEV) + TILE)
        hal = hal.reshape((2, 2, LON_DEV) + TILE)
        dst[off] += sc * (mix_lat[0, 0] - 8.0 * mix_lat[0, 1]) + sc2 * (16.0 * hal[0, 1] - hal[0, 0])
        dst[off + 1] += sc * mix_lat[0, 1] - sc2 * hal[0, 1]
        dst[off + 63] += sc * (8.0 * mix_lat[1, 0] - mix_lat[1, 1]) + sc2 * (16.0 * hal[1, 0] - hal[1, 1])
        dst[off + 62] += -sc * mix_lat[1, 0] - sc2 * hal[1, 0]

    def correct_lon(st):
        dst, off, sc, sc2 = target(st)

        @pl.loop(0, LAT_DEV // 16)
        def _(c):
            i0 = c * 16
            west = lon_h[st, 0, pl.ds(i0, 16)].reshape((32,) + TILE)
            east = lon_h[st, 1, pl.ds(i0, 16)].reshape((32,) + TILE)
            both = unsplit(mixed(slice(384, 448), jnp.concatenate([west, east], axis=0)), 8)
            for n in range(16):
                i = i0 + n
                si = inv_sin(i)
                a1 = sc * si
                a2 = sc2 * (si * si)
                w2, w1, pw2, pw1 = west[2 * n], west[2 * n + 1], both[2 * n], both[2 * n + 1]
                e1, e2, pe1, pe2 = east[2 * n], east[2 * n + 1], both[32 + 2 * n], both[33 + 2 * n]
                dst[off + i, 0] += a1 * (pw2 - 8.0 * pw1) + a2 * (16.0 * w1 - w2)
                dst[off + i, 1] += a1 * pw1 - a2 * w1
                dst[off + i, 11] += a1 * (8.0 * pe1 - pe2) + a2 * (16.0 * e1 - e2)
                dst[off + i, 10] += -a1 * pe1 - a2 * e1

    load_state()

    @pl.loop(0, 8)
    def _(t):
        gather_e(0, q_init, t)

    for n in range(4):
        @pl.loop(0, 16)
        def _(k):
            gather_g(0, q_init, n, k)

    prepare_indices()
    build_lhs()
    build_sines()
    pl.semaphore_wait(bar, peers)

    for st, cur in ((0, q_init), (1, q_mid)):
        @pl.loop(0, 8)
        def _(t):
            if st == 1:
                gather_e(st, cur, t)
            start_e(st, t)

        if st == 0:
            send_indices()

        for n in range(4):
            @pl.loop(0, 16)
            def _(r):
                k = turn(r)
                if st == 1:
                    gather_g(st, cur, n, k)
                start_g(st, n, k)

        if st == 0:
            adjust_indices()
        products(cur, 0)
        forward_ew(st)
        products(cur, 1)
        aggregate(st, 0)
        products(cur, 2)
        aggregate(st, 1)
        products(cur, 3)
        aggregate(st, 2)
        aggregate(st, 3)
        halos(st, cur)
        stencil(st, cur)
        sum_over_z(st)
        wait_lon(st)
        border_ew(st)
        correct_lon(st)
        wait_lat(st)
        correct_lat(st)

    @pl.loop(0, LAT_DEV // 8)
    def _(ib):
        i0 = pl.multiple_of(ib * 8, 8)
        for j in range(LON_DEV):
            v = res_ref[pl.ds(i0, 8), j]
            out_ref[:, pl.ds(i0, 8), j * NR:(j + 1) * NR] = jnp.swapaxes(v, 0, 1)

    @pl.when(is_sum)
    def _():
        @pl.loop(0, N_Z)
        def _(zz):
            wait_on(own_i, i_send.at[0, zz])
            wait_on(own_w, i_send.at[1, zz])

    for st in range(2):
        for n in range(4):
            @pl.loop(0, 16)
            def _(k):
                @pl.when(k != me_k)
                def _():
                    wait_on(send_g.at[st, n, k], g_send.at[st, n, k])

        @pl.loop(0, 8)
        def _(t):
            @pl.when(ew_member(t) != me_k)
            def _():
                wait_on(send_e.at[st, t], e1_send.at[st, t])

        for n in range(4):
            @pl.when(2 * nth(n) + par != z)
            def _():
                wait_on(chunk.at[st, n], n_send.at[st, n])

        @pl.when(is_sum)
        def _():
            wait_on(summed.at[st], f_send.at[st])

        @pl.when(is_agg)
        def _():
            wait_on(recv_e1.at[st], e2_send.at[st])

        @pl.when(b < N_LON - 1)
        def _():
            wait_on(lon_h.at[st, 0], lon_send.at[st, 0])

        @pl.when(b > 0)
        def _():
            wait_on(lon_h.at[st, 1], lon_send.at[st, 1])

        @pl.when(y < N_LAT - 1)
        def _():
            wait_on(lat_h.at[st, 0], lat_send.at[st, 0])

        @pl.when(y > 0)
        def _():
            wait_on(lat_h.at[st, 1], lat_send.at[st, 1])


def local(
    fields, coupling, export_index, ghost_ns_index, ghost_ns_frac, ghost_ew_index, ghost_ew_frac
):
    x = fields[0]
    exports = export_index.reshape(-1)
    nsi = jnp.swapaxes(ghost_ns_index[0], 2, 3)
    nsf = jnp.swapaxes(ghost_ns_frac[0], 2, 3)
    ewi = jnp.transpose(ghost_ew_index[0], (0, 2, 3, 1))
    ewf = jnp.transpose(ghost_ew_frac[0], (0, 2, 3, 1))

    vm = pl.BlockSpec(memory_space=pltpu.VMEM)
    sm = pl.BlockSpec(memory_space=pltpu.SMEM)
    hbm = pl.BlockSpec(memory_space=pl.ANY)
    V = lambda *shape: pltpu.VMEM(shape + TILE, jnp.float32)
    I = lambda *shape: pltpu.VMEM(shape + TILE, jnp.int32)
    D = lambda *shape: pltpu.SemaphoreType.DMA(shape)
    out = pl.pallas_call(
        kernel,
        out_shape=jax.ShapeDtypeStruct(x.shape, jnp.float32),
        in_specs=[hbm, vm, vm, vm, sm, vm, vm],
        out_specs=vm,
        scratch_shapes=[
            pltpu.VMEM(x.shape, jnp.float32),
            V(LAT_DEV + 4, LON_DEV), V(LAT_DEV + 4, LON_DEV), V(LAT_DEV + 4, LON_DEV),
            V(LAT_DEV, LON_DEV), V(LAT_DEV, LON_DEV), V(LAT_DEV, LON_DEV),
            pltpu.VMEM((448, 192), jnp.bfloat16), pltpu.VMEM((LAT_DEV, NR), jnp.float32),
            V(2, 4, 16, 4)] + [V(64)] * 8 + [V(2, 8, 4), V(2, 16, 4), V(N_Z, 16, 4), V(N_Z, 16, 4),
            V(2, 4, 2, LON_DEV), V(2, N_Z, 2, LON_DEV), V(2, 2, LON_DEV),
            V(2, 2, 2, LON_DEV), V(2, 2, LAT_DEV, 2),
            I(2), V(2), I(4, 2), V(4, 2), I(4, 2), V(4, 2),
            pltpu.SMEM((4, 2) + TILE, jnp.int32), pltpu.SMEM((4, 2) + TILE, jnp.float32),
            I(2), V(2), pltpu.SMEM((2,) + TILE, jnp.int32), pltpu.SMEM((2,) + TILE, jnp.float32),
            D(2, 4, 16), D(2, 4, 16), D(2, 8), D(2, 16), D(2, 8), D(2, 4), D(2, 4), D(2, N_Z), D(2),
            D(2), D(2, N_Z), D(2, 2), D(2, 2), D(2, 2), D(2, 2), D(5),
        ],
        compiler_params=pltpu.CompilerParams(
            collective_id=0, has_side_effects=True, vmem_limit_bytes=60 * 2**20),
        name="two_sections",
    )(x, coupling, nsi, nsf, exports, ewi, ewf)
    return out[None]


def solution(mesh):
    placed = (
        P("panel", None, "lat", "lon"),
        P(),
        P("panel", "lat", "lon", None),
        P("panel", None, None, "lon", None),
        P("panel", None, None, "lon", None),
        P("panel", None, "lat", None, None),
        P("panel", None, "lat", None, None),
    )
    return jax.shard_map(
        local, mesh=mesh, in_specs=placed, out_specs=P("panel", None, "lat", "lon"), check_vma=False
    )
```

```python
import math

import jax
import jax.numpy as jnp
from jax import lax
from jax.experimental import pallas as pl
from jax.experimental.pallas import tpu as pltpu
from jax.sharding import PartitionSpec as P

NR = 128
FIELDS = 8
LAT_DEV = 64
LON_DEV = 12
N_LAT = 4
N_LON = 32
N_Z = 8

time_step = 0.15
viscosity = 0.1
inner_radius = 0.35

MESH = pl.DeviceIdType.MESH
TILE = (FIELDS, NR)


def kernel(
    x_ref, coup_ref, nsi_ref, nsf_ref, exp_ref, ewi_ref, ewf_ref,
    out_ref,
    x_buf, q_init, q_mid, p_lat, p_lon, s_ref, lhs_ref, isin_ref,
    send_g, g00, g01, g02, g03, g10, g11, g12, g13, send_e, recv_e1, recv_e20, recv_e21, chunk, recv_n, summed,
    lat_h, lon_h,
    own_i, own_w, got_i, got_w, adj_i, adj_w, smem_i, smem_w,
    adj_ei, adj_ew, smem_ei, smem_ew,
    g_send, g_recv, e1_send, e1_recv, i_send, i_recv, n_send, n_recv, f_send,
    e2_send, e2_recv, lat_send, lat_recv, lon_send, lon_recv, loc_sem,
):
    recv_g = ((g00, g01, g02, g03), (g10, g11, g12, g13))
    recv_e2 = (recv_e20, recv_e21)
    p = lax.axis_index("panel")
    y = lax.axis_index("lat")
    b = lax.axis_index("lon")
    z = b // 4
    w = b % 4
    other = 1 - p
    wx = (w + 2) % 4
    me_k = y * 4 + w
    upper = y >= 2
    half = jnp.where(upper, 1, 0)
    par = jnp.where(upper, 3 - y, y)
    dest_lat = jnp.where(upper, 3, 0)
    is_sum = (z % 2) == par
    is_ns = (y == 0) | (y == 3)
    is_agg = (w == 1) | (w == 2)
    ew_lon = jnp.where(w == 2, 0, N_LON - 1)
    is_ew = (b == 0) | (b == N_LON - 1)
    ew_side = jnp.where(b == 0, 0, 1)
    star = jnp.where(y == 0, z % 2, 3 - z % 2)

    x_copy = pltpu.make_async_copy(x_ref, x_buf, loc_sem.at[0])
    x_copy.start()

    bar = pltpu.get_barrier_semaphore()

    def greet(dev):
        pl.semaphore_signal(bar, inc=1, device_id=dev, device_id_type=MESH)

    @pl.loop(0, 16)
    def _(k):
        @pl.when(k != me_k)
        def _():
            greet((p, k // 4, z * 4 + k % 4))

    @pl.loop(0, 4)
    def _(m):
        greet((other, y, (2 * m + par) * 4 + wx))

    @pl.loop(0, N_Z)
    def _(zz):
        @pl.when(is_sum & (zz != z))
        def _():
            greet((p, y, zz * 4 + w))

        @pl.when(is_ew)
        def _():
            greet((other, y, zz * 4 + wx))

    @pl.when(is_ns)
    def _():
        greet((other, star, z * 4 + wx))

    @pl.when(y > 0)
    def _():
        greet((p, y - 1, b))

    @pl.when(y < N_LAT - 1)
    def _():
        greet((p, y + 1, b))

    @pl.when(b > 0)
    def _():
        greet((p, y, b - 1))

    @pl.when(b < N_LON - 1)
    def _():
        greet((p, y, b + 1))

    one = lambda cond: jnp.where(cond, 1, 0)
    peers = (
        15 + 4 + 8 * one(is_sum) + one(is_agg)
        + one(y > 0) + one(y < N_LAT - 1) + one(b > 0) + one(b < N_LON - 1)
    )

    def rcopy(src, dst, ssem, rsem, dev):
        pltpu.make_async_remote_copy(
            src_ref=src, dst_ref=dst, send_sem=ssem, recv_sem=rsem,
            device_id=dev, device_id_type=MESH,
        ).start()

    def wait_on(ref, sem):
        pltpu.make_async_copy(ref, ref, sem).wait()

    row = lax.broadcasted_iota(jnp.int32, TILE, 0)

    def weights_of(frac):
        a, c = frac[0:1], frac[1:2]
        return jnp.where(row % 2 == 1, a, 1.0 - a) * jnp.where(row % 4 >= 2, c, 1.0 - c)

    def prepare_indices():
        own_i[...] = jnp.zeros(own_i.shape, jnp.int32)
        own_w[...] = jnp.zeros(own_w.shape, jnp.float32)
        adj_ei[...] = jnp.zeros(adj_ei.shape, jnp.int32)
        adj_ew[...] = jnp.zeros(adj_ew.shape, jnp.float32)
        for g in range(2):
            own_i[g, 0:4, 0:LON_DEV] = nsi_ref[half, g]
            own_w[g, 0:2, 0:LON_DEV] = nsf_ref[half, g]
            own_w[g] = weights_of(own_w[g])
            adj_ei[g, 0:4, 0:LAT_DEV] = ewi_ref[ew_side, g]
            adj_ew[g, 0:2, 0:LAT_DEV] = ewf_ref[ew_side, g]
            adj_ew[g] = weights_of(adj_ew[g])
            s = adj_ei[g]
            col = (s >> 2) & (N_LON - 1)
            k = (s >> 7) * 4 + (col & 3)
            adj_ei[g] = (col >> 2) * 64 + k * 4 + (s & 3)
        copies = [pltpu.make_async_copy(adj_ei, smem_ei, loc_sem.at[1]),
                  pltpu.make_async_copy(adj_ew, smem_ew, loc_sem.at[2])]
        for c in copies:
            c.start()
        for c in copies:
            c.wait()

    def send_indices():
        @pl.when(is_sum)
        def _():
            @pl.loop(0, N_Z)
            def _(zz):
                dev = (other, y, zz * 4 + wx)
                rcopy(own_i, got_i.at[z // 2], i_send.at[0, zz], i_recv.at[0, z // 2], dev)
                rcopy(own_w, got_w.at[z // 2], i_send.at[1, zz], i_recv.at[1, z // 2], dev)

    def adjust_indices():
        for m in range(4):
            wait_on(got_i.at[m], i_recv.at[0, m])
            wait_on(got_w.at[m], i_recv.at[1, m])
            s = got_i[m]
            col = (s >> 2) & (N_LON - 1)
            k = (s >> 7) * 4 + (col & 3)
            adj_i[m] = k * 4 + (s & 3)
            adj_w[m] = jnp.where((col >> 2) == z, got_w[m], 0.0)
        copies = [pltpu.make_async_copy(adj_i, smem_i, loc_sem.at[3]),
                  pltpu.make_async_copy(adj_w, smem_w, loc_sem.at[4])]
        for c in copies:
            c.start()
        for c in copies:
            c.wait()

    def load_state():
        zero_rows = jnp.zeros((2, LON_DEV) + TILE, jnp.float32)
        for ref in (q_init, q_mid, p_lat):
            ref[0:2] = zero_rows
            ref[LAT_DEV + 2:LAT_DEV + 4] = zero_rows
        x_copy.wait()

        @pl.loop(0, LAT_DEV // 8)
        def _(ib):
            i0 = pl.multiple_of(ib * 8, 8)
            for j in range(LON_DEV):
                v = x_buf[:, pl.ds(i0, 8), j * NR:(j + 1) * NR]
                q_init[pl.ds(i0 + 2, 8), j] = jnp.swapaxes(v, 0, 1)

    radius = inner_radius + (1.0 - inner_radius) * (
        lax.broadcasted_iota(jnp.int32, TILE, 1).astype(jnp.float32) + 0.5) / NR
    ct = inner_radius / radius
    ct2 = ct * ct * (viscosity / 12.0)

    def build_sines():
        i = y * LAT_DEV + lax.broadcasted_iota(jnp.int32, (LAT_DEV, NR), 0)
        colat = math.pi / 4 + (i.astype(jnp.float32) + 0.5) * (math.pi / 2) / (LAT_DEV * N_LAT)
        isin_ref[...] = 1.0 / jnp.sin(colat)

    def inv_sin(i):
        return isin_ref[pl.ds(i, 1), :]

    def build_lhs():
        r64 = lax.broadcasted_iota(jnp.int32, (64, 8), 0) % 8
        c8 = lax.broadcasted_iota(jnp.int32, (64, 8), 1)
        ex = jnp.where(r64 == c8, 1.0, 0.0).astype(jnp.float32)
        r8 = lax.broadcasted_iota(jnp.int32, (8, 64), 0)
        c64 = lax.broadcasted_iota(jnp.int32, (8, 64), 1) % 8
        ext = jnp.where(r8 == c64, 1.0, 0.0).astype(jnp.float32)
        rr = lax.broadcasted_iota(jnp.int32, (64, 64), 0)
        cc = lax.broadcasted_iota(jnp.int32, (64, 64), 1)
        same = (rr // 8) == (cc // 8)
        eye = jnp.where(rr == cc, 1.0, 0.0).astype(jnp.float32)

        def kron(k):
            tall = jnp.dot(ex, coup_ref[k], precision=lax.Precision.HIGHEST,
                           preferred_element_type=jnp.float32)
            full = jnp.dot(tall, ext, precision=lax.Precision.HIGHEST,
                           preferred_element_type=jnp.float32)
            return jnp.where(same, full, 0.0)

        c0, c1, c2, c3 = kron(0), kron(1), kron(2), kron(3)
        nu = viscosity
        blocks = [
            (8.0 * c0 + 16.0 * nu * eye) / 12.0,
            (-8.0 * c0 + 16.0 * nu * eye) / 12.0,
            (-c0 - nu * eye) / 12.0,
            (c0 - nu * eye) / 12.0,
            c3 - (30.0 * nu / 12.0) * eye,
            c1 / -12.0,
            c2 / -12.0,
        ]
        for n, blk in enumerate(blocks):
            hi = blk.astype(jnp.bfloat16)
            lo = (blk - hi.astype(jnp.float32)).astype(jnp.bfloat16)
            lhs_ref[64 * n:64 * (n + 1), :] = jnp.concatenate([hi, hi, lo], axis=1)

    def split(cols):
        n = cols.shape[0] // 8
        flat = cols.reshape(n * 64, NR)
        wide = jnp.concatenate([flat[64 * t:64 * (t + 1)] for t in range(n)], axis=1)
        hi = wide.astype(jnp.bfloat16)
        lo = (wide - hi.astype(jnp.float32)).astype(jnp.bfloat16)
        return jnp.concatenate([hi, lo, hi], axis=0)

    def mixed(rows, cols):
        return jnp.dot(lhs_ref[rows], split(cols), preferred_element_type=jnp.float32)

    def unsplit(wide, n):
        return jnp.concatenate(
            [wide[:, NR * t:NR * (t + 1)] for t in range(n)], axis=0).reshape((8 * n,) + TILE)

    lane = lax.broadcasted_iota(jnp.int32, (64, NR), 1)

    def column(cur, idx):
        i = (idx * 43691) >> 19
        return cur[i + 2, idx - 12 * i]

    def group_of(k):
        ky = k // 4
        kup = ky >= 2
        kpar = jnp.where(kup, 3 - ky, ky)
        return (jnp.where(kup, 96, 0) + kpar * 4 + (k % 4 + 2) % 4) * 4

    def nth(n):
        return lax.rem(z // 2 + 1 + n, 4)

    def gather_g(st, cur, n, k):
        first = group_of(k) + nth(n) * 32
        for s in range(4):
            send_g[st, n, k, s] = column(cur, exp_ref[first + s])

    def start_g(st, n, k):
        dst = recv_g[st][n].at[pl.ds(me_k * 4, 4)]

        @pl.when(k != me_k)
        def _():
            rcopy(send_g.at[st, n, k], dst, g_send.at[st, n, k],
                  g_recv.at[st, n, me_k], (p, k // 4, z * 4 + k % 4))

        @pl.when(k == me_k)
        def _():
            pltpu.make_async_copy(send_g.at[st, n, k], dst, g_recv.at[st, n, me_k]).start()

    def gather_e(st, cur, t):
        first = ((t // 2) * N_LON + (t % 2) * (N_LON - 1)) * 4
        for s in range(4):
            send_e[st, t, s] = column(cur, exp_ref[first + s])

    def ew_member(t):
        return (t // 2) * 4 + 2 - t % 2

    def start_e(st, t):
        k = ew_member(t)

        @pl.when(k != me_k)
        def _():
            rcopy(send_e.at[st, t], recv_e1.at[st, me_k], e1_send.at[st, t],
                  e1_recv.at[st, me_k], (p, k // 4, z * 4 + k % 4))

        @pl.when(k == me_k)
        def _():
            pltpu.make_async_copy(
                send_e.at[st, t], recv_e1.at[st, me_k], e1_recv.at[st, me_k]).start()

    def turn(n):
        return lax.rem(me_k + 1 + n, 16)

    def halos(st, cur):
        @pl.when(y < N_LAT - 1)
        def _():
            rcopy(cur.at[LAT_DEV:LAT_DEV + 2], lat_h.at[st, 0], lat_send.at[st, 0],
                  lat_recv.at[st, 0], (p, y + 1, b))

        @pl.when(y > 0)
        def _():
            rcopy(cur.at[2:4], lat_h.at[st, 1], lat_send.at[st, 1],
                  lat_recv.at[st, 1], (p, y - 1, b))

        @pl.when(b < N_LON - 1)
        def _():
            rcopy(cur.at[2:LAT_DEV + 2, 10:12], lon_h.at[st, 0], lon_send.at[st, 0],
                  lon_recv.at[st, 0], (p, y, b + 1))

        @pl.when(b > 0)
        def _():
            rcopy(cur.at[2:LAT_DEV + 2, 0:2], lon_h.at[st, 1], lon_send.at[st, 1],
                  lon_recv.at[st, 1], (p, y, b - 1))

    def products(cur, quarter):
        @pl.loop(quarter * (LAT_DEV // 16), (quarter + 1) * (LAT_DEV // 16))
        def _(c):
            i0 = c * 4
            cols = cur[pl.ds(i0 + 2, 4)].reshape((48,) + TILE)
            sums, lats, lons = [], [], []
            for t in range(3):
                wide = mixed(slice(0, 448), cols[16 * t:16 * (t + 1)])
                for h in range(2):
                    part = wide[:, NR * h:NR * (h + 1)]
                    total = part[256:320]
                    total = total + jnp.where(lane >= 1, pltpu.roll(part[0:64], 1, 1), 0.0)
                    total = total + jnp.where(lane < NR - 1, pltpu.roll(part[64:128], NR - 1, 1), 0.0)
                    total = total + jnp.where(lane >= 2, pltpu.roll(part[128:192], 2, 1), 0.0)
                    total = total + jnp.where(lane < NR - 2, pltpu.roll(part[192:256], NR - 2, 1), 0.0)
                    sums.append(total)
                    lats.append(part[320:384])
                    lons.append(part[384:448])
            shape = (4, LON_DEV) + TILE
            s_ref[pl.ds(i0, 4)] = jnp.concatenate(sums, axis=0).reshape(shape)
            p_lat[pl.ds(i0 + 2, 4)] = jnp.concatenate(lats, axis=0).reshape(shape)
            p_lon[pl.ds(i0, 4)] = jnp.concatenate(lons, axis=0).reshape(shape)

    def shifted(v, n):
        pad = jnp.zeros((abs(n),) + TILE, jnp.float32)
        if n > 0:
            return jnp.concatenate([v[n:], pad], axis=0)
        return jnp.concatenate([pad, v[:n]], axis=0)

    def stencil(st, cur):
        @pl.loop(0, LAT_DEV)
        def _(i):
            si = inv_sin(i)
            q0 = cur[i + 2]
            pl0 = p_lon[i]
            d1 = (p_lat[i] - p_lat[i + 4]) + 8.0 * (p_lat[i + 3] - p_lat[i + 1])
            e1 = (shifted(pl0, -2) - shifted(pl0, 2)) + 8.0 * (shifted(pl0, 1) - shifted(pl0, -1))
            d2 = 16.0 * (cur[i + 1] + cur[i + 3]) - (cur[i] + cur[i + 4])
            e2 = 16.0 * (shifted(q0, -1) + shifted(q0, 1)) - (shifted(q0, -2) + shifted(q0, 2))
            rate = s_ref[i] + ct * (d1 + si * e1) + ct2 * (
                d2 + (si * si) * e2 - (30.0 * (1.0 + si * si)) * q0)
            if st == 0:
                q_mid[i + 2] = q0 + time_step * rate
            else:
                out_ref[i] = 0.5 * q_init[i + 2] + 0.5 * (q0 + time_step * rate)

    def aggregate(st, n):
        got = recv_g[st][n]

        @pl.loop(0, 16)
        def _(k):
            wait_on(got.at[pl.ds(k * 4, 4)], g_recv.at[st, n, k])

        m = nth(n)

        @pl.loop(0, LON_DEV)
        def _(j):
            for g in range(2):
                acc = jnp.zeros(TILE, jnp.float32)
                for t in range(4):
                    acc = acc + smem_w[m, g, t, j] * got[smem_i[m, g, t, j]]
                chunk[st, n, g, j] = acc

        zz = 2 * m + par

        @pl.when(zz != z)
        def _():
            rcopy(chunk.at[st, n], recv_n.at[st, z], n_send.at[st, n], n_recv.at[st, z],
                  (p, y, zz * 4 + w))

        @pl.when(zz == z)
        def _():
            pltpu.make_async_copy(chunk.at[st, n], recv_n.at[st, z], n_recv.at[st, z]).start()

    def sum_over_z(st):
        @pl.when(is_sum)
        def _():
            @pl.loop(0, N_Z)
            def _(zz):
                wait_on(recv_n.at[st, zz], n_recv.at[st, zz])

            for g in range(2):
                acc = recv_n[st, 0, g]
                for zz in range(1, N_Z):
                    acc = acc + recv_n[st, zz, g]
                summed[st, g] = acc
            rcopy(summed.at[st], lat_h.at[st, half], f_send.at[st], lat_recv.at[st, half],
                  (other, dest_lat, z * 4 + wx))

    def forward_ew(st):
        @pl.when(is_agg)
        def _():
            @pl.loop(0, 16)
            def _(k):
                wait_on(recv_e1.at[st, k], e1_recv.at[st, k])

            rcopy(recv_e1.at[st], recv_e2[st].at[z], e2_send.at[st], e2_recv.at[st, z],
                  (other, y, ew_lon))

    def border_ew(st):
        @pl.when(is_ew)
        def _():
            @pl.loop(0, N_Z)
            def _(zz):
                wait_on(recv_e2[st].at[zz], e2_recv.at[st, zz])

            @pl.loop(0, LAT_DEV)
            def _(i):
                for g in range(2):
                    acc = jnp.zeros(TILE, jnp.float32)
                    for t in range(4):
                        idx = smem_ei[g, t, i]
                        acc = acc + smem_ew[g, t, i] * recv_e2[st][idx >> 6, (idx >> 2) & 15, idx & 3]
                    lon_h[st, ew_side, i, g] = acc

    def wait_lon(st):
        @pl.when(b > 0)
        def _():
            wait_on(lon_h.at[st, 0], lon_recv.at[st, 0])

        @pl.when(b < N_LON - 1)
        def _():
            wait_on(lon_h.at[st, 1], lon_recv.at[st, 1])

    def wait_lat(st):
        for side in range(2):
            wait_on(lat_h.at[st, side], lat_recv.at[st, side])

    def target(st):
        if st == 0:
            return q_mid, 2, time_step * ct, time_step * ct2
        return out_ref, 0, 0.5 * time_step * ct, 0.5 * time_step * ct2

    def correct_lat(st):
        dst, off, sc, sc2 = target(st)
        hal = lat_h[st].reshape((48,) + TILE)
        mix_lat = jnp.concatenate(
            [unsplit(mixed(slice(320, 384), hal[16 * t:16 * (t + 1)]), 2) for t in range(3)],
            axis=0).reshape((2, 2, LON_DEV) + TILE)
        hal = hal.reshape((2, 2, LON_DEV) + TILE)
        dst[off] += sc * (mix_lat[0, 0] - 8.0 * mix_lat[0, 1]) + sc2 * (16.0 * hal[0, 1] - hal[0, 0])
        dst[off + 1] += sc * mix_lat[0, 1] - sc2 * hal[0, 1]
        dst[off + 63] += sc * (8.0 * mix_lat[1, 0] - mix_lat[1, 1]) + sc2 * (16.0 * hal[1, 0] - hal[1, 1])
        dst[off + 62] += -sc * mix_lat[1, 0] - sc2 * hal[1, 0]

    def correct_lon(st):
        dst, off, sc, sc2 = target(st)

        @pl.loop(0, LAT_DEV // 4)
        def _(c):
            i0 = c * 4
            west = lon_h[st, 0, pl.ds(i0, 4)].reshape((8,) + TILE)
            east = lon_h[st, 1, pl.ds(i0, 4)].reshape((8,) + TILE)
            both = unsplit(mixed(slice(384, 448), jnp.concatenate([west, east], axis=0)), 2)
            for n in range(4):
                i = i0 + n
                si = inv_sin(i)
                a1 = sc * si
                a2 = sc2 * (si * si)
                w2, w1, pw2, pw1 = west[2 * n], west[2 * n + 1], both[2 * n], both[2 * n + 1]
                e1, e2, pe1, pe2 = east[2 * n], east[2 * n + 1], both[8 + 2 * n], both[9 + 2 * n]
                dst[off + i, 0] += a1 * (pw2 - 8.0 * pw1) + a2 * (16.0 * w1 - w2)
                dst[off + i, 1] += a1 * pw1 - a2 * w1
                dst[off + i, 11] += a1 * (8.0 * pe1 - pe2) + a2 * (16.0 * e1 - e2)
                dst[off + i, 10] += -a1 * pe1 - a2 * e1

    load_state()

    @pl.loop(0, 8)
    def _(t):
        gather_e(0, q_init, t)

    for n in range(4):
        @pl.loop(0, 16)
        def _(k):
            gather_g(0, q_init, n, k)

    prepare_indices()
    build_lhs()
    build_sines()
    pl.semaphore_wait(bar, peers)

    for st, cur in ((0, q_init), (1, q_mid)):
        @pl.loop(0, 8)
        def _(t):
            if st == 1:
                gather_e(st, cur, t)
            start_e(st, t)

        if st == 0:
            send_indices()

        for n in range(4):
            @pl.loop(0, 16)
            def _(r):
                k = turn(r)
                if st == 1:
                    gather_g(st, cur, n, k)
                start_g(st, n, k)

        if st == 0:
            adjust_indices()
        products(cur, 0)
        forward_ew(st)
        products(cur, 1)
        aggregate(st, 0)
        products(cur, 2)
        aggregate(st, 1)
        products(cur, 3)
        aggregate(st, 2)
        aggregate(st, 3)
        halos(st, cur)
        stencil(st, cur)
        sum_over_z(st)
        wait_lon(st)
        border_ew(st)
        correct_lon(st)
        wait_lat(st)
        correct_lat(st)

    @pl.when(is_sum)
    def _():
        @pl.loop(0, N_Z)
        def _(zz):
            wait_on(own_i, i_send.at[0, zz])
            wait_on(own_w, i_send.at[1, zz])

    for st in range(2):
        for n in range(4):
            @pl.loop(0, 16)
            def _(k):
                @pl.when(k != me_k)
                def _():
                    wait_on(send_g.at[st, n, k], g_send.at[st, n, k])

        @pl.loop(0, 8)
        def _(t):
            @pl.when(ew_member(t) != me_k)
            def _():
                wait_on(send_e.at[st, t], e1_send.at[st, t])

        for n in range(4):
            @pl.when(2 * nth(n) + par != z)
            def _():
                wait_on(chunk.at[st, n], n_send.at[st, n])

        @pl.when(is_sum)
        def _():
            wait_on(summed.at[st], f_send.at[st])

        @pl.when(is_agg)
        def _():
            wait_on(recv_e1.at[st], e2_send.at[st])

        @pl.when(b < N_LON - 1)
        def _():
            wait_on(lon_h.at[st, 0], lon_send.at[st, 0])

        @pl.when(b > 0)
        def _():
            wait_on(lon_h.at[st, 1], lon_send.at[st, 1])

        @pl.when(y < N_LAT - 1)
        def _():
            wait_on(lat_h.at[st, 0], lat_send.at[st, 0])

        @pl.when(y > 0)
        def _():
            wait_on(lat_h.at[st, 1], lat_send.at[st, 1])


def fields_first(cells_ref, out_ref):
    for ib in range(cells_ref.shape[0] // 8):
        part = slice(8 * ib, 8 * ib + 8)
        for j in range(LON_DEV):
            out_ref[:, part, j * NR:(j + 1) * NR] = jnp.swapaxes(cells_ref[part, j], 0, 1)


def local(
    fields, coupling, export_index, ghost_ns_index, ghost_ns_frac, ghost_ew_index, ghost_ew_frac
):
    x = fields[0]
    exports = export_index.reshape(-1)
    nsi = jnp.swapaxes(ghost_ns_index[0], 2, 3)
    nsf = jnp.swapaxes(ghost_ns_frac[0], 2, 3)
    ewi = jnp.transpose(ghost_ew_index[0], (0, 2, 3, 1))
    ewf = jnp.transpose(ghost_ew_frac[0], (0, 2, 3, 1))

    vm = pl.BlockSpec(memory_space=pltpu.VMEM)
    sm = pl.BlockSpec(memory_space=pltpu.SMEM)
    hbm = pl.BlockSpec(memory_space=pl.ANY)
    V = lambda *shape: pltpu.VMEM(shape + TILE, jnp.float32)
    I = lambda *shape: pltpu.VMEM(shape + TILE, jnp.int32)
    D = lambda *shape: pltpu.SemaphoreType.DMA(shape)
    out = pl.pallas_call(
        kernel,
        out_shape=jax.ShapeDtypeStruct((LAT_DEV, LON_DEV) + TILE, jnp.float32),
        in_specs=[hbm, vm, vm, vm, sm, vm, vm],
        out_specs=vm,
        scratch_shapes=[
            pltpu.VMEM(x.shape, jnp.float32),
            V(LAT_DEV + 4, LON_DEV), V(LAT_DEV + 4, LON_DEV), V(LAT_DEV + 4, LON_DEV),
            V(LAT_DEV, LON_DEV), V(LAT_DEV, LON_DEV),
            pltpu.VMEM((448, 192), jnp.bfloat16), pltpu.VMEM((LAT_DEV, NR), jnp.float32),
            V(2, 4, 16, 4)] + [V(64)] * 8 + [V(2, 8, 4), V(2, 16, 4), V(N_Z, 16, 4), V(N_Z, 16, 4),
            V(2, 4, 2, LON_DEV), V(2, N_Z, 2, LON_DEV), V(2, 2, LON_DEV),
            V(2, 2, 2, LON_DEV), V(2, 2, LAT_DEV, 2),
            I(2), V(2), I(4, 2), V(4, 2), I(4, 2), V(4, 2),
            pltpu.SMEM((4, 2) + TILE, jnp.int32), pltpu.SMEM((4, 2) + TILE, jnp.float32),
            I(2), V(2), pltpu.SMEM((2,) + TILE, jnp.int32), pltpu.SMEM((2,) + TILE, jnp.float32),
            D(2, 4, 16), D(2, 4, 16), D(2, 8), D(2, 16), D(2, 8), D(2, 4), D(2, 4), D(2, N_Z), D(2),
            D(2), D(2, N_Z), D(2, 2), D(2, 2), D(2, 2), D(2, 2), D(5),
        ],
        compiler_params=pltpu.CompilerParams(
            collective_id=0, has_side_effects=True, vmem_limit_bytes=60 * 2**20),
        name="two_sections",
    )(x, coupling, nsi, nsf, exports, ewi, ewf)
    rows = 16
    return pl.pallas_call(
        fields_first,
        grid=(LAT_DEV // rows,),
        out_shape=jax.ShapeDtypeStruct(x.shape, jnp.float32),
        in_specs=[pl.BlockSpec((rows, LON_DEV) + TILE, lambda i: (i, 0, 0, 0))],
        out_specs=pl.BlockSpec((FIELDS, rows, LON_DEV * NR), lambda i: (0, i, 0)),
        name="fields_first",
    )(out)[None]


def solution(mesh):
    placed = (
        P("panel", None, "lat", "lon"),
        P(),
        P("panel", "lat", "lon", None),
        P("panel", None, None, "lon", None),
        P("panel", None, None, "lon", None),
        P("panel", None, "lat", None, None),
        P("panel", None, "lat", None, None),
    )
    return jax.shard_map(
        local, mesh=mesh, in_specs=placed, out_specs=P("panel", None, "lat", "lon"), check_vma=False
    )
```
